32 devices in a mesh: replica: 4 (over x, core), fsdp: 4 (over z), tensor: 2 (over y).
Axes of the slice: x: 2, y: 2, z: 4, core: 2. Of those that a mesh axis runs over, the one named last changes fastest.
Arguments:
- tokens: bfloat16 [2, 8192, 2048], P(None, ('replica', 'fsdp')), may hold values from -6 to 6
- cotangent: bfloat16 [2, 8192, 2048], P(None, ('replica', 'fsdp')), may hold values from -6 to 6
- lengths: int32 [2, 4, 9], P(None, 'replica'), may hold values from 1 to 1024, as said below
- parents: int32 [2, 4, 9], P(None, 'replica'), may hold values from 0 to 4, as said below
- attn_gain: float32 [1, 2048], replicated, may hold values from 0.5 to 1.5
- qk_gain: float32 [1, 2, 128], replicated, may hold values from 0.5 to 1.5
- w_query: bfloat16 [1, 2048, 2048], P(None, 'fsdp', 'tensor'), may hold values from -0.125 to 0.125
- key_weight_matrix: bfloat16 [1, 2048, 1024], P(None, 'fsdp', 'tensor'), may hold values from -0.125 to 0.125
- value_weight_matrix: bfloat16 [1, 2048, 1024], P(None, 'fsdp', 'tensor'), may hold values from -0.125 to 0.125
- w_headgate: bfloat16 [1, 2048, 16], P(None, 'fsdp', 'tensor'), may hold values from -0.125 to 0.125
- w_out: bfloat16 [1, 2048, 2048], P(None, 'tensor', 'fsdp'), may hold values from -1.5 to 1.5
- mlp_gain: float32 [1, 2048], replicated, may hold values from 0.5 to 1.5
- w_gate: bfloat16 [1, 2048, 6144], P(None, 'fsdp', 'tensor'), may hold values from -0.125 to 0.125
- w_up: bfloat16 [1, 2048, 6144], P(None, 'fsdp', 'tensor'), may hold values from -0.125 to 0.125
- w_down: bfloat16 [1, 6144, 2048], P(None, 'tensor', 'fsdp'), may hold values from -0.078125 to 0.078125
Outputs:
- output: bfloat16 [2, 8192, 2048], P(None, ('replica', 'fsdp'))
- input_grad: bfloat16 [2, 8192, 2048], P(None, ('replica', 'fsdp'))
- grad_attn_gain: float32 [1, 2048], P(None, 'fsdp')
- grad_qk_gain: float32 [1, 2, 128], P(None, None, 'fsdp')
- query_weight_gradient: float32 [1, 2048, 2048], P(None, 'fsdp', 'tensor')
- grad_w_key: float32 [1, 2048, 1024], P(None, 'fsdp', 'tensor')
- grad_w_value: float32 [1, 2048, 1024], P(None, 'fsdp', 'tensor')
- grad_w_headgate: float32 [1, 2048, 16], P(None, 'fsdp', 'tensor')
- grad_w_out: float32 [1, 2048, 2048], P(None, 'tensor', 'fsdp')
- grad_mlp_gain: float32 [1, 2048], P(None, 'fsdp')
- grad_w_gate: float32 [1, 2048, 6144], P(None, 'fsdp', 'tensor')
- grad_w_up: float32 [1, 2048, 6144], P(None, 'fsdp', 'tensor')
- grad_w_down: float32 [1, 6144, 2048], P(None, 'tensor', 'fsdp')
The draws below stay inside these ranges and needn't reach their ends.
Inputs may be any that keep to these rules, and one draw needn't show every extreme that they name: In each tree segment 0 is the trunk with exactly 1024 tokens; all 9 lengths sum to 2048. `parents`: segment 0 is the root (its entry is 0); segments 1 to 4 are branches with parent 0; each later segment is a leaf whose parent is a branch, each branch parent of exactly one leaf.
All inputs are finite; a program needn't handle non-finite values.
Results may differ from the reference program's by a relative error of at most 0.02.
Values may be sent and summed in bfloat16 or wider, within the bound.
No kernel may reach another device: no remote copies, remote signals or barrier semaphores. Data moves between devices by JAX's collectives and lax.ppermute only.
A program may use at most 448 MiB of HBM per device.

```python
import math
import jax
import jax.numpy as jnp
from jax import lax

MODEL_WIDTH = 2048
HQ = 16
KEY_VALUE_HEADS = 8
HEAD_SIZE = 128
FF = 6144
LAYER_TOTAL = 1
MB = 2
NSEG = 9
TREE = 2048
ROWS = 8192
N_REPLICA = 4


def draw_lengths(key, part):
    key = jax.random.fold_in(key, 11)
    half_tree = TREE // 2
    base_len = half_tree // (NSEG - 1)
    reach_len = half_tree // 32
    shifts = jax.random.randint(key, (MB, N_REPLICA, NSEG - 1), -reach_len, reach_len + 1)
    others = base_len + shifts - jnp.roll(shifts, 1, axis=-1)
    trunk = jnp.full((MB, N_REPLICA, 1), half_tree, jnp.int32)
    return jnp.concatenate([trunk, others.astype(jnp.int32)], axis=-1)


def draw_parents(key, part):
    key = jax.random.fold_in(key, 23)
    branch_count = (NSEG - 1) // 2
    keys_all = jax.random.split(key, MB * N_REPLICA)
    orders = jax.vmap(lambda single: jax.random.permutation(single, branch_count))(keys_all)
    orders = orders.reshape(MB, N_REPLICA, branch_count).astype(jnp.int32)
    heads_part = jnp.zeros((MB, N_REPLICA, 1 + branch_count), jnp.int32)
    return jnp.concatenate([heads_part, orders + 1], axis=-1)


def block_scale(key, shape, cuts, smallest, high):
    loudness, own = 1.0, jax.random.fold_in(key, 6)
    for axis_at, blocks in cuts:
        steps = jnp.exp(jax.random.uniform(jax.random.fold_in(own, axis_at), (blocks,), jnp.float32, smallest / len(cuts), high / len(cuts)))
        loudness = loudness * jnp.repeat(steps, shape[axis_at] // blocks).reshape([-1 if axis == axis_at else 1 for axis in range(len(shape))])
    return loudness


def centred(own_key, shape, scale, most, cuts=(), kind=jnp.bfloat16):
    loudness = block_scale(own_key, shape, cuts, -0.22, 0.18) if cuts else 1.0
    array = jax.random.normal(own_key, shape, jnp.float32) * scale * loudness
    return jnp.minimum(jnp.maximum(array, -most), most).astype(kind)


def setup_inputs(seed: int = 0) -> dict:
    keys = jax.random.split(jax.random.key(seed), 16)
    tokens = centred(keys[0], (MB, ROWS, MODEL_WIDTH), 1.0, 6.0, ((1, 16),))
    cotangent = centred(keys[1], (MB, ROWS, MODEL_WIDTH), 1.0, 6.0, ((1, 16),))
    lengths = draw_lengths(jax.random.fold_in(keys[15], 71), 0)
    parents = draw_parents(jax.random.fold_in(keys[15], 71), 0)
    attn_gain = jnp.clip(1.0 + 0.1 * jax.random.normal(keys[4], (LAYER_TOTAL, MODEL_WIDTH), jnp.float32), 0.5, 1.5)
    qk_gain = jnp.clip(1.0 + 0.1 * jax.random.normal(keys[5], (LAYER_TOTAL, 2, HEAD_SIZE), jnp.float32), 0.5, 1.5)
    w_query = centred(keys[6], (LAYER_TOTAL, MODEL_WIDTH, HQ * HEAD_SIZE), MODEL_WIDTH ** -0.5, 0.125, ((1, 4), (2, 2)))
    key_weight_matrix = centred(keys[7], (LAYER_TOTAL, MODEL_WIDTH, KEY_VALUE_HEADS * HEAD_SIZE), MODEL_WIDTH ** -0.5, 0.125, ((1, 4), (2, 2)))
    value_weight_matrix = centred(keys[8], (LAYER_TOTAL, MODEL_WIDTH, KEY_VALUE_HEADS * HEAD_SIZE), MODEL_WIDTH ** -0.5, 0.125, ((1, 4), (2, 2)))
    w_headgate = centred(keys[9], (LAYER_TOTAL, MODEL_WIDTH, HQ), MODEL_WIDTH ** -0.5, 0.125, ((1, 4), (2, 2)))
    w_out = centred(keys[10], (LAYER_TOTAL, HQ * HEAD_SIZE, MODEL_WIDTH), (max(1, HQ * HEAD_SIZE // 128)) ** -0.5, 1.5, ((1, 2), (2, 4)))
    mlp_gain = jnp.clip(1.0 + 0.1 * jax.random.normal(keys[11], (LAYER_TOTAL, MODEL_WIDTH), jnp.float32), 0.5, 1.5)
    w_gate = centred(keys[12], (LAYER_TOTAL, MODEL_WIDTH, FF), MODEL_WIDTH ** -0.5, 0.125, ((1, 4), (2, 2)))
    w_up = centred(keys[13], (LAYER_TOTAL, MODEL_WIDTH, FF), MODEL_WIDTH ** -0.5, 0.125, ((1, 4), (2, 2)))
    w_down = centred(keys[14], (LAYER_TOTAL, FF, MODEL_WIDTH), FF ** -0.5, 0.078125, ((1, 2), (2, 4)))
    return dict(tokens=tokens, cotangent=cotangent, lengths=lengths, parents=parents, attn_gain=attn_gain, qk_gain=qk_gain, w_query=w_query, key_weight_matrix=key_weight_matrix, value_weight_matrix=value_weight_matrix, w_headgate=w_headgate, w_out=w_out, mlp_gain=mlp_gain, w_gate=w_gate, w_up=w_up, w_down=w_down)


EPSILON = 1e-06
THETA = 1000000.0
HIGHEST = lax.Precision.HIGHEST

@jax.custom_vjp
def low(v):
    return lax.optimization_barrier(v.astype(jnp.bfloat16)).astype(jnp.float32)

@jax.custom_vjp
def low_back(v):
    return v

def low_keep(v):
    return (low(v), None)

def low_pass(kept, grad):
    return (grad,)

def back_keep(v):
    return (v, None)

def back_low(kept, grad):
    return (low(grad),)
low.defvjp(low_keep, low_pass)
low_back.defvjp(back_keep, back_low)

def segment_table(lengths, parents):
    count = lengths.shape[0]
    starts = (jnp.cumsum(lengths) - lengths).astype(jnp.int32)
    labels = jnp.arange(count, dtype=jnp.int32)
    parent_hot = (parents[:, None] == labels[None, :]).astype(jnp.int32)
    grand_hot = lax.optimization_barrier(jnp.sum(parent_hot[:, :, None] * parent_hot[None, :, :], axis=1)).astype(jnp.int32)
    eye_hot = (labels[:, None] == labels[None, :]).astype(jnp.int32)
    ancestor = (eye_hot + parent_hot + grand_hot > 0).astype(jnp.int32)
    before = lax.optimization_barrier(jnp.sum(ancestor * (1 - eye_hot) * lengths[None, :], axis=1)).astype(jnp.int32)
    return (starts, (before - starts).astype(jnp.int32), ancestor)

def row_segments(indices, starts, count):
    labels = jnp.arange(count, dtype=jnp.int32)
    member = lax.optimization_barrier(jnp.sum((indices[:, None] >= starts[None, :]).astype(jnp.int32), axis=1)).astype(jnp.int32) - 1
    return (member[:, None] == labels[None, :]).astype(jnp.int32)

def tree_tables(lengths, parents, first_row, query_count, tree_len, head_dim):
    count = lengths.shape[0]
    starts, offsets, ancestor = segment_table(lengths, parents)
    query_index = (first_row + jnp.arange(query_count, dtype=jnp.int32)).astype(jnp.int32)
    key_index = jnp.arange(tree_len, dtype=jnp.int32)
    query_hot = row_segments(query_index, starts, count)
    key_hot = row_segments(key_index, starts, count)
    reach_rows = lax.optimization_barrier(jnp.sum(query_hot[:, :, None] * ancestor[None, :, :], axis=1)).astype(jnp.int32)
    reach = lax.optimization_barrier(jnp.sum(reach_rows[:, None, :] * key_hot[None, :, :], axis=-1)).astype(jnp.int32)
    allowed = (reach > 0) & (key_index[None, :] <= query_index[:, None])
    position = query_index + lax.optimization_barrier(jnp.sum(query_hot * offsets[None, :], axis=1)).astype(jnp.int32)
    half_dim = head_dim // 2
    inverse = THETA ** (-(jnp.arange(half_dim, dtype=jnp.float32) * 2.0 / head_dim))
    angle = position.astype(jnp.float32)[:, None] * inverse[None, :]
    return (allowed, jnp.cos(angle), jnp.sin(angle))

def rotate(values, cosine, sine):
    half_dim = values.shape[-1] // 2
    first_half = values[..., :half_dim]
    second_half = values[..., half_dim:]
    cos_rows = cosine[:, None, :]
    sin_rows = sine[:, None, :]
    return jnp.concatenate([first_half * cos_rows - second_half * sin_rows, second_half * cos_rows + first_half * sin_rows], axis=-1)

def rms_norm(values, gain):
    return values * lax.rsqrt(lax.optimization_barrier(jnp.mean(values * values, axis=-1, keepdims=True)) + EPSILON) * gain

def product(left, right):
    return jnp.dot(left, right, precision=HIGHEST)

def layer_forward(stream, weights, tables):
    attn_gain, qk_gain, w_query, key_weight_matrix, value_weight_matrix, w_headgate, w_out, mlp_gain, w_gate, w_up, w_down = weights
    allowed, cosine, sine = tables
    row_count = stream.shape[0]
    head_dim = qk_gain.shape[-1]
    head_count = w_query.shape[1] // head_dim
    kv_count = key_weight_matrix.shape[1] // head_dim
    group_size = head_count // kv_count
    normed = low(rms_norm(stream, attn_gain))
    query_raw = low_back(product(normed, w_query)).reshape(row_count, head_count, head_dim)
    key_raw = low_back(product(normed, key_weight_matrix)).reshape(row_count, kv_count, head_dim)
    value_all = low(low_back(product(normed, value_weight_matrix))).reshape(row_count, kv_count, head_dim)
    gate_value = jax.nn.sigmoid(low_back(product(normed, w_headgate)))
    query_rot = low(rotate(rms_norm(query_raw, qk_gain[0]), cosine, sine))
    key_rot = low(rotate(rms_norm(key_raw, qk_gain[1]), cosine, sine))
    block_rows = math.gcd(row_count, 512)
    score_scale = head_dim ** (-0.5)
    grouped = query_rot.reshape(row_count // block_rows, block_rows, kv_count, group_size, head_dim)
    mask_blocks = allowed.reshape(row_count // block_rows, block_rows, row_count)

    def attend(item_pair):
        query_block, mask_block = item_pair
        scores = jnp.einsum('qhgd,khd->qhgk', query_block, key_rot, precision=HIGHEST) * score_scale
        scores = low_back(scores)
        scores = jnp.where(mask_block[:, None, None, :], scores, -1e+30)
        soft_weights = jnp.exp(scores - jax.nn.logsumexp(scores, axis=-1, keepdims=True))
        return jnp.einsum('qhgk,khd->qhgd', low(soft_weights), value_all, precision=HIGHEST)
    attended = lax.map(jax.checkpoint(attend), (grouped, mask_blocks)).reshape(row_count, head_count, head_dim)
    attended = low_back(attended)
    mixed = low(gate_value[:, :, None] * attended).reshape(row_count, head_count * head_dim)
    middle = stream + low_back(product(mixed, w_out))
    normed_mlp = low(rms_norm(middle, mlp_gain))
    gate_pre = low_back(product(normed_mlp, w_gate))
    up_pre = low_back(product(normed_mlp, w_up))
    hidden = low(jax.nn.silu(gate_pre) * up_pre)
    return middle + low_back(product(hidden, w_down))

def stack_forward(stream, params, tables):
    for layer_index in range(params[0].shape[0]):
        stream = layer_forward(stream, tuple((stacked[layer_index] for stacked in params)), tables)
    return stream

def reference(tokens, cotangent, lengths, parents, attn_gain, qk_gain, w_query, key_weight_matrix, value_weight_matrix, w_headgate, w_out, mlp_gain, w_gate, w_up, w_down):
    params = tuple((stacked.astype(jnp.float32) for stacked in (attn_gain, qk_gain, w_query, key_weight_matrix, value_weight_matrix, w_headgate, w_out, mlp_gain, w_gate, w_up, w_down)))
    batch_count, total_rows, width = tokens.shape
    tree_count = lengths.shape[1]
    tree_len = total_rows // tree_count
    head_dim = qk_gain.shape[-1]
    inputs = tokens.reshape(batch_count * tree_count, tree_len, width)
    seeds = cotangent.reshape(batch_count * tree_count, tree_len, width)
    length_rows = lengths.reshape(batch_count * tree_count, -1)
    parent_rows = parents.reshape(batch_count * tree_count, -1)

    def one_tree(totals, packed):
        tree_in, tree_seed, tree_lengths, tree_parents = packed
        tables = tree_tables(tree_lengths, tree_parents, jnp.int32(0), tree_len, tree_len, head_dim)
        result, pullback = jax.vjp(lambda flow, weights: stack_forward(flow, weights, tables), tree_in.astype(jnp.float32), params)
        grad_in, grad_params = pullback(tree_seed.astype(jnp.float32))
        totals = tuple((running + grad_part for running, grad_part in zip(totals, grad_params)))
        return (totals, (result.astype(jnp.bfloat16), grad_in.astype(jnp.bfloat16)))
    zeros = tuple((jnp.zeros_like(stacked) for stacked in params))
    totals, (outputs, grads_in) = lax.scan(one_tree, zeros, (inputs, seeds, length_rows, parent_rows))
    return (outputs.reshape(batch_count, total_rows, width), grads_in.reshape(batch_count, total_rows, width), totals[0], totals[1], totals[2], totals[3], totals[4], totals[5], totals[6], totals[7], totals[8], totals[9], totals[10])
```

```python
import jax
import jax.numpy as jnp
from jax import lax
from jax.sharding import PartitionSpec as P

EPSILON = 1e-06
THETA = 1000000.0


def segment_table(lengths, parents):
    count = lengths.shape[0]
    starts = jnp.cumsum(lengths) - lengths
    labels = jnp.arange(count, dtype=jnp.int32)
    parent_hot = (parents[:, None] == labels[None, :]).astype(jnp.int32)
    grand_hot = jnp.dot(parent_hot, parent_hot)
    eye_hot = (labels[:, None] == labels[None, :]).astype(jnp.int32)
    ancestor = (eye_hot + parent_hot + grand_hot > 0).astype(jnp.int32)
    before = jnp.sum(ancestor * (1 - eye_hot) * lengths[None, :], axis=1)
    return (starts, before - starts, ancestor)


def row_segments(indices, starts, count):
    labels = jnp.arange(count, dtype=jnp.int32)
    member = jnp.sum((indices[:, None] >= starts[None, :]).astype(jnp.int32), axis=1) - 1
    return (member[:, None] == labels[None, :]).astype(jnp.int32)


def tree_tables(lengths, parents, first_row, query_count, tree_len, head_dim):
    count = lengths.shape[0]
    starts, offsets, ancestor = segment_table(lengths, parents)
    query_index = first_row + jnp.arange(query_count, dtype=jnp.int32)
    key_index = jnp.arange(tree_len, dtype=jnp.int32)
    query_hot = row_segments(query_index, starts, count)
    key_hot = row_segments(key_index, starts, count)
    reach = jnp.dot(jnp.dot(query_hot, ancestor), key_hot.T)
    allowed = (reach > 0) & (key_index[None, :] <= query_index[:, None])
    position = query_index + jnp.sum(query_hot * offsets[None, :], axis=1)
    half_dim = head_dim // 2
    inverse = THETA ** (-(jnp.arange(half_dim, dtype=jnp.float32) * 2.0 / head_dim))
    angle = position.astype(jnp.float32)[:, None] * inverse[None, :]
    return (allowed, jnp.cos(angle), jnp.sin(angle))


def rotate(values, cosine, sine):
    half_dim = values.shape[-1] // 2
    first_half = values[..., :half_dim]
    second_half = values[..., half_dim:]
    cos_rows = cosine[:, None, :]
    sin_rows = sine[:, None, :]
    return jnp.concatenate(
        [
            first_half * cos_rows - second_half * sin_rows,
            second_half * cos_rows + first_half * sin_rows,
        ],
        axis=-1,
    )


def rotate_back(grads, cosine, sine):
    half_dim = grads.shape[-1] // 2
    first_half = grads[..., :half_dim]
    second_half = grads[..., half_dim:]
    cos_rows = cosine[:, None, :]
    sin_rows = sine[:, None, :]
    return jnp.concatenate(
        [
            first_half * cos_rows + second_half * sin_rows,
            second_half * cos_rows - first_half * sin_rows,
        ],
        axis=-1,
    )


def norm_rows(values, gain):
    inverse = lax.rsqrt(jnp.mean(values * values, axis=-1, keepdims=True) + EPSILON)
    return (values * inverse * gain, inverse)


def norm_back(values, inverse, gain, upstream):
    unit_rows = values * inverse
    scaled = upstream * gain
    gain_grad = jnp.sum((upstream * unit_rows).reshape(-1, values.shape[-1]), axis=0)
    return (
        gain_grad,
        inverse * (scaled - unit_rows * jnp.mean(scaled * unit_rows, axis=-1, keepdims=True)),
    )


def matmul(left, right):
    return jnp.dot(left, right, preferred_element_type=jnp.float32)


def matmul_tn(left, right):
    return lax.dot_general(
        left, right, (((0,), (0,)), ((), ())), preferred_element_type=jnp.float32
    )


def matmul_nt(left, right):
    return lax.dot_general(
        left, right, (((1,), (1,)), ((), ())), preferred_element_type=jnp.float32
    )

def swaps(bit, count):
    return [(index, index ^ bit) for index in range(count)]


def across(value, bit):
    return lax.ppermute(value, "replica", swaps(bit, lax.axis_size("replica")))


def add_low(left, right):
    return (left.astype(jnp.float32) + right.astype(jnp.float32)).astype(jnp.bfloat16)


def own_quarter(shard, axis):
    size = shard.shape[axis] // lax.axis_size("replica")
    return lax.dynamic_slice_in_dim(shard, lax.axis_index("replica") * size, size, axis)


def spread(block):
    other = across(block, 2)
    return [block, other, across(block, 1), across(other, 1)]


def gather_quarters(quarter, axis):
    return spread(lax.all_gather(quarter, "fsdp", axis=axis, tiled=True))


def fold_quarters(parts, axis):
    mine = add_low(parts[0], across(parts[2], 1))
    for_other = add_low(parts[1], across(parts[3], 1))
    total = add_low(mine, across(for_other, 2))
    return spread(lax.psum_scatter(total, "fsdp", scatter_dimension=axis, tiled=True))


def in_order(pieces, axis):
    index = lax.axis_index("replica")
    far = (index & 2) > 0
    odd = (index & 1) > 0
    low_pair = [jnp.where(far, pieces[1], pieces[0]), jnp.where(far, pieces[3], pieces[2])]
    high_pair = [jnp.where(far, pieces[0], pieces[1]), jnp.where(far, pieces[2], pieces[3])]
    ordered = []
    for even_piece, odd_piece in (low_pair, high_pair):
        ordered.append(jnp.where(odd, odd_piece, even_piece))
        ordered.append(jnp.where(odd, even_piece, odd_piece))
    return jnp.concatenate(ordered, axis=axis).astype(jnp.float32)


def tensor_total(part):
    low_part = lax.optimization_barrier(part.astype(jnp.bfloat16))
    other = lax.ppermute(low_part, "tensor", swaps(1, lax.axis_size("tensor")))
    return low_part.astype(jnp.float32) + other.astype(jnp.float32)


def tree_scores(query_low, key_all, allowed, score_scale):
    scores = (
        jnp.einsum("qhgd,khd->qhgk", query_low, key_all, preferred_element_type=jnp.float32)
        * score_scale
    )
    return jnp.where(allowed[:, None, None, :], scores, -1e30)


def attend_forward(query_low, key_all, value_all, allowed, score_scale):
    scores = tree_scores(query_low, key_all, allowed, score_scale)
    top_score = jnp.max(scores, axis=-1, keepdims=True)
    log_total = top_score + jnp.log(jnp.sum(jnp.exp(scores - top_score), axis=-1, keepdims=True))
    soft_weights = jnp.exp(scores - log_total)
    attended = jnp.einsum(
        "qhgk,khd->qhgd",
        soft_weights.astype(jnp.bfloat16),
        value_all,
        preferred_element_type=jnp.float32,
    )
    return (attended, log_total)


def attend_backward(query_low, key_all, value_all, allowed, score_scale, log_total, attended_in):
    scores = tree_scores(query_low, key_all, allowed, score_scale)
    soft_weights = jnp.exp(scores - log_total)
    grad_soft = jnp.einsum(
        "qhgd,khd->qhgk", attended_in, value_all, preferred_element_type=jnp.float32
    )
    grad_scores = (
        soft_weights * (grad_soft - jnp.sum(soft_weights * grad_soft, axis=-1, keepdims=True))
    ).astype(jnp.bfloat16)
    soft_low = soft_weights.astype(jnp.bfloat16)
    grad_query_rot = (
        jnp.einsum("qhgk,khd->qhgd", grad_scores, key_all, preferred_element_type=jnp.float32)
        * score_scale
    )
    grad_key_part = (
        jnp.einsum("qhgk,qhgd->khd", grad_scores, query_low, preferred_element_type=jnp.float32)
        * score_scale
    )
    grad_value_part = jnp.einsum(
        "qhgk,qhgd->khd", soft_low, attended_in, preferred_element_type=jnp.float32
    )
    return (grad_query_rot, grad_key_part, grad_value_part)


def total_of(terms):
    total = terms[0]
    for term in terms[1:]:
        total = total + term
    return total


def local(
    tokens,
    cotangent,
    lengths,
    parents,
    attn_gain,
    qk_gain,
    w_query,
    key_weight_matrix,
    value_weight_matrix,
    w_headgate,
    w_out,
    mlp_gain,
    w_gate,
    w_up,
    w_down,
):
    batch_count, row_count, width = tokens.shape
    head_dim = qk_gain.shape[-1]
    tree_shards = lax.axis_size("fsdp")
    tree_len = row_count * tree_shards
    first_row = lax.axis_index("fsdp") * row_count
    score_scale = head_dim ** (-0.5)
    attn_gain, qk_gain, mlp_gain = attn_gain[0], qk_gain[0], mlp_gain[0]
    tables = [
        tree_tables(
            lengths[index, 0], parents[index, 0], first_row, row_count, tree_len, head_dim
        )
        for index in range(batch_count)
    ]
    cosine = jnp.concatenate([table[1] for table in tables], axis=0)
    sine = jnp.concatenate([table[2] for table in tables], axis=0)

    pieces = [
        own_quarter(member[0], 1)
        for member in (w_query, key_weight_matrix, value_weight_matrix, w_headgate)
    ]
    query_width, key_width, value_width, gate_width = [piece.shape[1] for piece in pieces]
    at_key = query_width
    at_value = at_key + key_width
    at_gate = at_value + value_width
    packed_width = at_gate + head_dim
    pad = jnp.zeros((pieces[0].shape[0], head_dim - gate_width), jnp.bfloat16)
    packed = gather_quarters(jnp.concatenate(pieces + [pad], axis=1), 0)
    out_w = gather_quarters(own_quarter(w_out[0], 0), 1)
    gate_w = gather_quarters(own_quarter(w_gate[0], 1), 0)
    up_w = gather_quarters(own_quarter(w_up[0], 1), 0)
    down_w = gather_quarters(own_quarter(w_down[0], 0), 1)
    groups = len(packed)
    group_size = query_width // head_dim
    kv_group = key_width // head_dim
    kv_count = groups * kv_group
    head_count = groups * group_size
    per_kv = head_count // kv_count
    all_rows = batch_count * row_count

    def of_tree(value, index):
        return value[index * row_count : (index + 1) * row_count]

    stream = tokens.reshape(all_rows, width).astype(jnp.float32)
    normed, inverse_attn = norm_rows(stream, attn_gain)
    normed_low = normed.astype(jnp.bfloat16)
    raw = [matmul(normed_low, member) for member in packed]
    query_raw = jnp.concatenate([part[:, :at_key] for part in raw], axis=1).reshape(
        all_rows, head_count, head_dim
    )
    key_raw = jnp.concatenate([part[:, at_key:at_value] for part in raw], axis=1).reshape(
        all_rows, kv_count, head_dim
    )
    value_low = jnp.concatenate([part[:, at_value:at_gate] for part in raw], axis=1).astype(
        jnp.bfloat16
    )
    gate_value = jax.nn.sigmoid(
        jnp.concatenate([part[:, at_gate : at_gate + gate_width] for part in raw], axis=1)
    )
    query_unit, query_inverse = norm_rows(query_raw, qk_gain[0])
    key_unit, key_inverse = norm_rows(key_raw, qk_gain[1])
    query_low = (
        rotate(query_unit, cosine, sine)
        .astype(jnp.bfloat16)
        .reshape(all_rows, kv_count, per_kv, head_dim)
    )
    key_low = (
        rotate(key_unit, cosine, sine).astype(jnp.bfloat16).reshape(all_rows, kv_count * head_dim)
    )
    key_value = jnp.concatenate([key_low, value_low], axis=1)
    kv_width = kv_count * head_dim
    key_all, value_all, log_total, attended, mixed, middle = [], [], [], [], [], []
    for index in range(batch_count):
        both = lax.all_gather(of_tree(key_value, index), "fsdp", axis=0, tiled=True)
        key_all.append(both[:, :kv_width].reshape(tree_len, kv_count, head_dim))
        value_all.append(both[:, kv_width:].reshape(tree_len, kv_count, head_dim))
        tree_out, tree_log = attend_forward(
            of_tree(query_low, index),
            key_all[index],
            value_all[index],
            tables[index][0],
            score_scale,
        )
        tree_out = tree_out.reshape(row_count, head_count, head_dim)
        attended.append(tree_out)
        log_total.append(tree_log)
        tree_mixed = (
            (of_tree(gate_value, index)[:, :, None] * tree_out)
            .astype(jnp.bfloat16)
            .reshape(row_count, head_count * head_dim)
        )
        mixed.append(tree_mixed)
        part = total_of(
            [
                matmul(tree_mixed[:, k * at_key : (k + 1) * at_key], out_w[k])
                for k in range(groups)
            ]
        )
        middle.append(of_tree(stream, index) + tensor_total(part))
    middle = jnp.concatenate(middle, axis=0)
    mixed = jnp.concatenate(mixed, axis=0)
    normed_mlp, inverse_mlp = norm_rows(middle, mlp_gain)
    mlp_low = normed_mlp.astype(jnp.bfloat16)
    upstream = cotangent.reshape(all_rows, width).astype(jnp.float32)
    down_in = cotangent.reshape(all_rows, width)
    gate_in, up_in, hidden, grad_down = [], [], [], []
    for k in range(groups):
        gate_pre = matmul(mlp_low, gate_w[k])
        up_pre = matmul(mlp_low, up_w[k])
        sigmoid_gate = jax.nn.sigmoid(gate_pre)
        silu_gate = gate_pre * sigmoid_gate
        hidden.append((silu_gate * up_pre).astype(jnp.bfloat16))
        grad_hidden = matmul_nt(down_in, down_w[k])
        gate_in.append(
            (
                grad_hidden * up_pre * sigmoid_gate * (1.0 + gate_pre * (1.0 - sigmoid_gate))
            ).astype(jnp.bfloat16)
        )
        up_in.append((grad_hidden * silu_gate).astype(jnp.bfloat16))
        grad_down.append(matmul_tn(hidden[k], down_in).astype(jnp.bfloat16))
    grad_normed_mlp = jnp.concatenate(
        [
            tensor_total(
                total_of(
                    [
                        matmul_nt(of_tree(gate_in[k], index), gate_w[k])
                        + matmul_nt(of_tree(up_in[k], index), up_w[k])
                        for k in range(groups)
                    ]
                )
            )
            for index in range(batch_count)
        ],
        axis=0,
    )
    down_shard = fold_quarters(grad_down, 1)
    gate_shard = fold_quarters(
        [matmul_tn(mlp_low, member).astype(jnp.bfloat16) for member in gate_in], 0
    )
    up_shard = fold_quarters(
        [matmul_tn(mlp_low, member).astype(jnp.bfloat16) for member in up_in], 0
    )
    result = middle + tensor_total(total_of([matmul(hidden[k], down_w[k]) for k in range(groups)]))
    grad_mlp_gain, back_mlp = norm_back(middle, inverse_mlp, mlp_gain, grad_normed_mlp)
    grad_middle = upstream + back_mlp
    out_in = grad_middle.astype(jnp.bfloat16)
    out_shard = fold_quarters(
        [
            matmul_tn(mixed[:, k * at_key : (k + 1) * at_key], out_in).astype(jnp.bfloat16)
            for k in range(groups)
        ],
        1,
    )
    grad_query_rot, key_grads, logit_in = [], [], []
    for index in range(batch_count):
        grad_mixed = jnp.concatenate(
            [matmul_nt(of_tree(out_in, index), out_w[k]) for k in range(groups)], axis=1
        ).reshape(row_count, head_count, head_dim)
        tree_gate = of_tree(gate_value, index)
        logit_in.append(
            (
                jnp.sum(grad_mixed * attended[index], axis=-1) * tree_gate * (1.0 - tree_gate)
            ).astype(jnp.bfloat16)
        )
        attended_in = (
            (grad_mixed * tree_gate[:, :, None])
            .astype(jnp.bfloat16)
            .reshape(row_count, kv_count, per_kv, head_dim)
        )
        tree_query, tree_key, tree_value = attend_backward(
            of_tree(query_low, index),
            key_all[index],
            value_all[index],
            tables[index][0],
            score_scale,
            log_total[index],
            attended_in,
        )
        grad_query_rot.append(tree_query.reshape(row_count, head_count, head_dim))
        key_grads.append(
            lax.psum_scatter(
                jnp.concatenate(
                    [tree_key.reshape(tree_len, -1), tree_value.reshape(tree_len, -1)], axis=1
                ).astype(jnp.bfloat16),
                "fsdp",
                scatter_dimension=0,
                tiled=True,
            )
        )
    key_grads = jnp.concatenate(key_grads, axis=0)
    grad_query_rot = jnp.concatenate(grad_query_rot, axis=0)
    logit_in = jnp.concatenate(logit_in, axis=0)
    grad_key_rot = key_grads[:, :kv_width].astype(jnp.float32)
    grad_key_rot = grad_key_rot.reshape(all_rows, kv_count, head_dim)
    value_in = key_grads[:, kv_width:]
    grad_qk_query, grad_query = norm_back(
        query_raw, query_inverse, qk_gain[0], rotate_back(grad_query_rot, cosine, sine)
    )
    grad_qk_key, grad_key = norm_back(
        key_raw, key_inverse, qk_gain[1], rotate_back(grad_key_rot, cosine, sine)
    )
    query_in = grad_query.astype(jnp.bfloat16).reshape(all_rows, head_count * head_dim)
    key_in = grad_key.astype(jnp.bfloat16).reshape(all_rows, kv_width)
    pad_in = jnp.zeros((all_rows, head_dim - gate_width), jnp.bfloat16)
    packed_in = [
        jnp.concatenate(
            [
                query_in[:, k * query_width : (k + 1) * query_width],
                key_in[:, k * key_width : (k + 1) * key_width],
                value_in[:, k * value_width : (k + 1) * value_width],
                logit_in[:, k * gate_width : (k + 1) * gate_width],
                pad_in,
            ],
            axis=1,
        )
        for k in range(groups)
    ]
    packed_shard = fold_quarters(
        [matmul_tn(normed_low, member).astype(jnp.bfloat16) for member in packed_in], 0
    )
    grad_normed = tensor_total(
        total_of([matmul_nt(packed_in[k], packed[k]) for k in range(groups)])
    )
    grad_attn_gain, back_attn = norm_back(stream, inverse_attn, attn_gain, grad_normed)
    input_grad = grad_middle + back_attn
    gain_sum = lax.psum(jnp.concatenate([grad_attn_gain, grad_mlp_gain]), ("replica", "fsdp"))
    qk_sum = lax.psum(
        jnp.stack([grad_qk_query, grad_qk_key]), ("replica", "fsdp", "tensor")
    )

    def own_slice(value, axis):
        size = value.shape[axis] // tree_shards
        return lax.dynamic_slice_in_dim(value, lax.axis_index("fsdp") * size, size, axis)[None]

    def packed_part(start, size):
        return in_order([piece[:, start : start + size] for piece in packed_shard], 1)[None]

    return (
        result.astype(jnp.bfloat16).reshape(tokens.shape),
        input_grad.astype(jnp.bfloat16).reshape(tokens.shape),
        own_slice(gain_sum[:width], 0),
        own_slice(qk_sum, 1),
        packed_part(0, query_width),
        packed_part(at_key, key_width),
        packed_part(at_value, value_width),
        packed_part(at_gate, gate_width),
        in_order(out_shard, 0)[None],
        own_slice(gain_sum[width:], 0),
        in_order(gate_shard, 1)[None],
        in_order(up_shard, 1)[None],
        in_order(down_shard, 0)[None],
    )


def solution(mesh):
    placed = (
        P(None, ("replica", "fsdp"), None),
        P(None, ("replica", "fsdp"), None),
        P(None, "replica", None),
        P(None, "replica", None),
        P(),
        P(),
        P(None, "fsdp", "tensor"),
        P(None, "fsdp", "tensor"),
        P(None, "fsdp", "tensor"),
        P(None, "fsdp", "tensor"),
        P(None, "tensor", "fsdp"),
        P(),
        P(None, "fsdp", "tensor"),
        P(None, "fsdp", "tensor"),
        P(None, "tensor", "fsdp"),
    )
    return jax.shard_map(
        local,
        mesh=mesh,
        in_specs=placed,
        out_specs=(
            P(None, ("replica", "fsdp"), None),
            P(None, ("replica", "fsdp"), None),
            P(None, "fsdp"),
            P(None, None, "fsdp"),
            P(None, "fsdp", "tensor"),
            P(None, "fsdp", "tensor"),
            P(None, "fsdp", "tensor"),
            P(None, "fsdp", "tensor"),
            P(None, "tensor", "fsdp"),
            P(None, "fsdp"),
            P(None, "fsdp", "tensor"),
            P(None, "fsdp", "tensor"),
            P(None, "tensor", "fsdp"),
        ),
        check_vma=False,
    )
```

```python
import functools

import jax
import jax.numpy as jnp
from jax import lax
from jax.experimental import pallas as pl
from jax.experimental.pallas import tpu as pltpu
from jax.sharding import PartitionSpec as P

EPSILON = 1e-06
THETA = 1000000.0
LOG2_E = 1.4426950408889634
LANES = 128
EXTRA_AT = 16
VMEM_BYTES = 48 * 1024 * 1024


def segment_table(lengths, parents):
    count = lengths.shape[0]
    starts = jnp.cumsum(lengths) - lengths
    labels = jnp.arange(count, dtype=jnp.int32)
    parent_hot = (parents[:, None] == labels[None, :]).astype(jnp.int32)
    grand_hot = jnp.dot(parent_hot, parent_hot)
    eye_hot = (labels[:, None] == labels[None, :]).astype(jnp.int32)
    ancestor = (eye_hot + parent_hot + grand_hot > 0).astype(jnp.int32)
    before = jnp.sum(ancestor * (1 - eye_hot) * lengths[None, :], axis=1)
    return (starts, before - starts, ancestor)


def row_segments(indices, starts, count):
    labels = jnp.arange(count, dtype=jnp.int32)
    member = jnp.sum((indices[:, None] >= starts[None, :]).astype(jnp.int32), axis=1) - 1
    return (member[:, None] == labels[None, :]).astype(jnp.int32)


def swaps(bit, count):
    return [(index, index ^ bit) for index in range(count)]


def across(value, bit):
    return lax.ppermute(value, "replica", swaps(bit, lax.axis_size("replica")))


def own_quarter(shard, axis):
    size = shard.shape[axis] // lax.axis_size("replica")
    return lax.dynamic_slice_in_dim(shard, lax.axis_index("replica") * size, size, axis)


def spread(block):
    other = across(block, 2)
    return [block, other, across(block, 1), across(other, 1)]


def gather_quarters(quarter, axis):
    return spread(lax.all_gather(quarter, "fsdp", axis=axis, tiled=True))


def fold_quarters(make_part, axis):
    low = jnp.bfloat16
    arrived_far = across(make_part(3).astype(low), 1).astype(jnp.float32)
    for_other = (make_part(1) + arrived_far).astype(low)
    arrived_near = across(make_part(2).astype(low), 1).astype(jnp.float32)
    mine = make_part(0) + arrived_near
    total = (mine + across(for_other, 2).astype(jnp.float32)).astype(low)
    return spread(lax.psum_scatter(total, "fsdp", scatter_dimension=axis, tiled=True))


def tensor_other(low_part):
    return lax.ppermute(low_part, "tensor", swaps(1, lax.axis_size("tensor")))


def relay_forward(block, count):
    blocks = [block]
    for _ in range(1, count):
        blocks.append(
            lax.ppermute(blocks[-1], "fsdp", [(index, index + 1) for index in range(count - 1)])
        )
    return blocks


def relay_back(parts, count):
    carry = parts[count - 1]
    for step in reversed(range(1, count)):
        arrived = lax.ppermute(carry, "fsdp", [(index, index - 1) for index in range(1, count)])
        carry = (parts[step - 1].astype(jnp.float32) + arrived.astype(jnp.float32)).astype(
            jnp.bfloat16
        )
    return carry


def params():
    return pltpu.CompilerParams(vmem_limit_bytes=VMEM_BYTES)


def cost(flops, moved, special=0):
    return pl.CostEstimate(
        flops=int(flops), bytes_accessed=int(moved), transcendentals=int(special)
    )


def whole_block(shape):
    return pl.BlockSpec(shape, lambda *index: (0,) * len(shape))


def dot_nn(left, right):
    return jnp.dot(left, right, preferred_element_type=jnp.float32)


def dot_nt(left, right):
    return lax.dot_general(
        left, right, (((1,), (1,)), ((), ())), preferred_element_type=jnp.float32
    )


def dot_tn(left, right):
    return lax.dot_general(
        left, right, (((0,), (0,)), ((), ())), preferred_element_type=jnp.float32
    )


def three_parts(value):
    first = value.astype(jnp.bfloat16)
    rest = value - first.astype(jnp.float32)
    second = rest.astype(jnp.bfloat16)
    third = (rest - second.astype(jnp.float32)).astype(jnp.bfloat16)
    return (first, second, third)


def put_lanes(base, parts):
    lane = lax.broadcasted_iota(jnp.int32, base.shape, 1)
    value = base.astype(jnp.float32)
    for offset, part in enumerate(parts):
        value = jnp.where(lane == EXTRA_AT + offset, part.astype(jnp.float32), value)
    return value.astype(jnp.bfloat16)


def rope(values, cos_rows, sin_rows):
    return values * cos_rows + pltpu.roll(values, LANES // 2, 1) * sin_rows


def rope_back(grads, cos_rows, sin_rows):
    return grads * cos_rows - pltpu.roll(grads, LANES // 2, 1) * sin_rows


def unit_of(raw):
    inverse = lax.rsqrt(jnp.mean(raw * raw, axis=-1, keepdims=True) + EPSILON)
    return (raw * inverse, inverse)


def unit_back(raw, gain, grads):
    unit, inverse = unit_of(raw)
    scaled = grads * gain
    gain_part = jnp.sum(grads * unit, axis=0, keepdims=True)
    return (
        gain_part,
        inverse * (scaled - unit * jnp.mean(scaled * unit, axis=-1, keepdims=True)),
    )


def key_value_kernel(groups, x_ref, cos_ref, sin_ref, gain_ref, *refs):
    weights, (kv_ref, raw_ref) = refs[:groups], refs[groups:]
    for k in range(groups):
        part = dot_nn(x_ref[...], weights[k][...])
        raw = part[:, :LANES]
        unit, _ = unit_of(raw)
        raw_ref[:, k * LANES : (k + 1) * LANES] = raw
        kv_ref[:, k * LANES : (k + 1) * LANES] = rope(
            unit * gain_ref[...], cos_ref[...], sin_ref[...]
        ).astype(jnp.bfloat16)
        at = (groups + k) * LANES
        kv_ref[:, at : at + LANES] = part[:, LANES:].astype(jnp.bfloat16)


def key_value_heads(normed_low, weights, cos_rows, sin_rows, gain):
    rows, width = normed_low.shape
    groups, block = len(weights), min(256, rows)
    return pl.pallas_call(
        functools.partial(key_value_kernel, groups),
        grid=(rows // block,),
        in_specs=[
            pl.BlockSpec((block, width), lambda m: (m, 0)),
            pl.BlockSpec((block, LANES), lambda m: (m, 0)),
            pl.BlockSpec((block, LANES), lambda m: (m, 0)),
            whole_block((1, LANES)),
        ]
        + [whole_block(weight.shape) for weight in weights],
        out_specs=[
            pl.BlockSpec((block, 2 * groups * LANES), lambda m: (m, 0)),
            pl.BlockSpec((block, groups * LANES), lambda m: (m, 0)),
        ],
        out_shape=[
            jax.ShapeDtypeStruct((rows, 2 * groups * LANES), jnp.bfloat16),
            jax.ShapeDtypeStruct((rows, groups * LANES), jnp.float32),
        ],
        compiler_params=params(),
        cost_estimate=cost(4 * rows * width * groups * LANES, 4 * rows * width),
        name="key_value_heads",
    )(normed_low, cos_rows, sin_rows, gain, *weights)


def query_kernel(groups, per_kv, x_ref, cos_ref, sin_ref, gain_ref, *refs):
    weights, (low_ref, raw_ref, gate_ref) = refs[:groups], refs[groups:]
    for k in range(groups):
        part = dot_nn(x_ref[...], weights[k][...])
        for head in range(per_kv):
            raw = part[:, head * LANES : (head + 1) * LANES]
            unit, _ = unit_of(raw)
            at = (k * per_kv + head) * LANES
            raw_ref[:, at : at + LANES] = raw
            low_ref[:, at : at + LANES] = rope(
                unit * gain_ref[...], cos_ref[...], sin_ref[...]
            ).astype(jnp.bfloat16)
        gate_ref[k] = jax.nn.sigmoid(part[:, per_kv * LANES :])


def query_heads(normed_low, weights, cos_rows, sin_rows, gain, per_kv):
    rows, width = normed_low.shape
    groups, block = len(weights), min(256, rows)
    wide = groups * per_kv * LANES
    return pl.pallas_call(
        functools.partial(query_kernel, groups, per_kv),
        grid=(rows // block,),
        in_specs=[
            pl.BlockSpec((block, width), lambda m: (m, 0)),
            pl.BlockSpec((block, LANES), lambda m: (m, 0)),
            pl.BlockSpec((block, LANES), lambda m: (m, 0)),
            whole_block((1, LANES)),
        ]
        + [whole_block(weight.shape) for weight in weights],
        out_specs=[
            pl.BlockSpec((block, wide), lambda m: (m, 0)),
            pl.BlockSpec((block, wide), lambda m: (m, 0)),
            pl.BlockSpec((groups, block, LANES), lambda m: (0, m, 0)),
        ],
        out_shape=[
            jax.ShapeDtypeStruct((rows, wide), jnp.bfloat16),
            jax.ShapeDtypeStruct((rows, wide), jnp.float32),
            jax.ShapeDtypeStruct((groups, rows, LANES), jnp.float32),
        ],
        compiler_params=params(),
        cost_estimate=cost(2 * rows * width * groups * (per_kv + 1) * LANES, 4 * rows * width),
        name="query_heads",
    )(normed_low, cos_rows, sin_rows, gain, *weights)


def tiles_of(row_count):
    block = min(256, row_count)
    return (block, row_count // block)


def tree_need(lengths, parents, shard, row_count, shards):
    count = lengths.shape[0]
    starts, offsets, ancestor = segment_table(lengths, parents)
    block, tiles = tiles_of(row_count)
    query_index = shard * row_count + jnp.arange(row_count, dtype=jnp.int32)
    query_hot = row_segments(query_index, starts, count)
    reach = jnp.sum(query_hot[:, :, None] * ancestor[None, :, :], axis=1)
    position = query_index + jnp.sum(query_hot * offsets[None, :], axis=1)
    back = jnp.arange(shards, dtype=jnp.int32)[:, None]
    key_index = (shard - back) * row_count + jnp.arange(row_count, dtype=jnp.int32)[None, :]
    key_hot = row_segments(key_index.reshape(-1), starts, count)
    query_has = jnp.max(reach.reshape(tiles, block, count), axis=1)
    key_has = jnp.max(key_hot.reshape(shards, tiles, block, count), axis=2)
    need = jnp.sum(query_has[:, None, None, :] * key_has[None], axis=-1) > 0
    wall = jnp.where(reach > 0, 0.0, -1e30)
    query_mask = jnp.pad(wall, ((0, 0), (0, LANES - count))).astype(jnp.bfloat16)
    lane = jnp.arange(LANES)[None, :]
    ones = ((lane >= EXTRA_AT) & (lane < EXTRA_AT + 3)).astype(jnp.float32)
    key_mask = jnp.pad(key_hot.astype(jnp.float32), ((0, 0), (0, LANES - count))) + ones
    return (need.astype(jnp.int32).reshape(-1), query_mask, key_mask.astype(jnp.bfloat16), position)


def forward_kernel(
    shards, per_kv, factor, need_ref, q_ref, qmask_ref, gate_ref, kmask_ref, *refs
):
    keys, values = refs[:shards], refs[shards : 2 * shards]
    mixed_ref, attended_ref, log_ref, total_ref = refs[-4:]
    rows = q_ref.shape[0]
    block, tiles = tiles_of(rows)
    lane = lax.broadcasted_iota(jnp.int32, (block, LANES), 1)
    for qi in range(tiles):
        span = slice(qi * block, (qi + 1) * block)
        total_ref[...] = jnp.zeros_like(total_ref)
        for shard in range(shards):
            for ci in range(tiles):
                if shard == 0 and ci > qi:
                    continue
                part = slice(ci * block, (ci + 1) * block)

                @pl.when(need_ref[(qi * shards + shard) * tiles + ci] > 0)
                def _(shard=shard, ci=ci, part=part):
                    at = shard * rows + ci * block
                    key_mask = kmask_ref[at : at + block]
                    key_wide = jnp.concatenate([keys[shard][part], key_mask], axis=1)
                    value_wide = jnp.concatenate(
                        [values[shard][part], jnp.ones((block, LANES), jnp.bfloat16)], axis=1
                    )
                    for head in range(per_kv):
                        query_wide = jnp.concatenate(
                            [q_ref[span, head * LANES : (head + 1) * LANES], qmask_ref[span]],
                            axis=1,
                        )
                        scores = dot_nt(query_wide, key_wide)
                        if shard == 0 and ci == qi:
                            row = lax.broadcasted_iota(jnp.int32, (block, block), 0)
                            column = lax.broadcasted_iota(jnp.int32, (block, block), 1)
                            scores = jnp.where(column <= row, scores, -1e30)
                        weights = jnp.exp2(scores * factor).astype(jnp.bfloat16)
                        total_ref[head] += dot_nn(weights, value_wide)

        logs = jnp.zeros((block, LANES), jnp.float32)
        for head in range(per_kv):
            summed = total_ref[head][:, LANES:]
            tree_out = total_ref[head][:, :LANES] / summed
            columns = slice(head * LANES, (head + 1) * LANES)
            attended_ref[span, columns] = tree_out
            gate = gate_ref[0, span, head : head + 1]
            mixed_ref[span, columns] = (gate * tree_out).astype(jnp.bfloat16)
            logs = jnp.where(lane == head, jnp.log(summed), logs)
        log_ref[0, span] = logs


def attend_forward(index, batches, tables, query_low, gates, blocks, per_kv):
    need, query_mask, key_mask = tables
    all_rows, wide = query_low.shape
    rows = all_rows // batches
    shards = len(blocks)
    groups = wide // (per_kv * LANES)
    own = per_kv * LANES
    block, _ = tiles_of(rows)
    tree_spec = pl.BlockSpec((rows, own), lambda g, need: (0, g))
    log_spec = pl.BlockSpec((1, rows, LANES), lambda g, need: (g, 0, 0))
    return pl.pallas_call(
        functools.partial(forward_kernel, shards, per_kv, LANES ** (-0.5) * LOG2_E),
        grid_spec=pltpu.PrefetchScalarGridSpec(
            num_scalar_prefetch=1,
            grid=(groups,),
            in_specs=[
                pl.BlockSpec((rows, own), lambda g, need: (index, g)),
                whole_block(query_mask.shape),
                pl.BlockSpec((1, rows, LANES), lambda g, need: (g, index, 0)),
                whole_block(key_mask.shape),
            ]
            + [pl.BlockSpec((rows, LANES), lambda g, need: (0, g))] * shards
            + [pl.BlockSpec((rows, LANES), lambda g, need: (0, groups + g))] * shards,
            out_specs=[tree_spec, tree_spec, log_spec],
            scratch_shapes=[pltpu.VMEM((per_kv, block, 2 * LANES), jnp.float32)],
        ),
        out_shape=[
            jax.ShapeDtypeStruct((rows, wide), jnp.bfloat16),
            jax.ShapeDtypeStruct((rows, wide), jnp.float32),
            jax.ShapeDtypeStruct((groups, rows, LANES), jnp.float32),
        ],
        compiler_params=params(),
        cost_estimate=cost(
            6 * rows * rows * shards * wide,
            8 * rows * wide + 2 * shards * rows * wide,
            rows * rows * shards * groups * per_kv,
        ),
        name="attend_forward",
    )(need, query_low, query_mask, gates, key_mask, *blocks, *blocks)


def backward_kernel(
    shards,
    per_kv,
    need_ref,
    out_in_ref,
    w_out_ref,
    q_ref,
    qmask_ref,
    gate_ref,
    kmask_ref,
    log_ref,
    attended_ref,
    raw_ref,
    cos_ref,
    sin_ref,
    gain_ref,
    *refs,
):
    scale = LANES ** (-0.5)
    factor = scale * LOG2_E
    keys, values = refs[:shards], refs[shards : 2 * shards]
    query_in_ref, gain_grad_ref = refs[2 * shards : 2 * shards + 2]
    block_grads = refs[2 * shards + 2 : 3 * shards + 2]
    dq_ref, dk_ref, dv_ref, qwide_ref, dwide_ref = refs[3 * shards + 2 :]
    rows = q_ref.shape[0]
    block, tiles = tiles_of(rows)
    grad_mixed = dot_nt(out_in_ref[...], w_out_ref[...])
    lane = lax.broadcasted_iota(jnp.int32, (rows, LANES), 1)
    logits = jnp.zeros((rows, LANES), jnp.float32)
    for head in range(per_kv):
        columns = slice(head * LANES, (head + 1) * LANES)
        attended = attended_ref[:, columns]
        gate = gate_ref[0, :, head : head + 1]
        mixed_grad = grad_mixed[:, columns]
        logit = jnp.sum(mixed_grad * attended, axis=-1, keepdims=True) * gate * (1.0 - gate)
        logits = jnp.where(lane == head, logit, logits)
        attended_in = (mixed_grad * gate).astype(jnp.bfloat16)
        delta = jnp.sum(attended_in.astype(jnp.float32) * attended, axis=-1, keepdims=True)
        dwide_ref[head, :, :LANES] = attended_in
        dwide_ref[head, :, LANES:] = put_lanes(
            jnp.zeros((rows, LANES), jnp.bfloat16), three_parts(-delta)
        )
        qwide_ref[head, :, :LANES] = q_ref[:, columns]
        qwide_ref[head, :, LANES:] = put_lanes(
            qmask_ref[...], three_parts(log_ref[0, :, head : head + 1] * (-1.0 / scale))
        )
    query_in_ref[:, per_kv * LANES :] = logits.astype(jnp.bfloat16)
    dq_ref[...] = jnp.zeros_like(dq_ref)
    for shard in range(shards):
        for ci in range(tiles):
            part = slice(ci * block, (ci + 1) * block)
            at = shard * rows + ci * block
            dk_ref[...] = jnp.zeros_like(dk_ref)
            dv_ref[...] = jnp.zeros_like(dv_ref)
            for qi in range(tiles):
                if shard == 0 and ci > qi:
                    continue
                span = slice(qi * block, (qi + 1) * block)

                @pl.when(need_ref[(qi * shards + shard) * tiles + ci] > 0)
                def _(shard=shard, ci=ci, qi=qi, at=at, part=part, span=span):
                    key_low = keys[shard][part]
                    key_mask = kmask_ref[at : at + block]
                    key_wide = jnp.concatenate([key_low, key_mask], axis=1)
                    value_wide = jnp.concatenate([values[shard][part], key_mask], axis=1)
                    for head in range(per_kv):
                        scores = dot_nt(key_wide, qwide_ref[head, span])
                        if shard == 0 and ci == qi:
                            row = lax.broadcasted_iota(jnp.int32, (block, block), 0)
                            column = lax.broadcasted_iota(jnp.int32, (block, block), 1)
                            scores = jnp.where(row <= column, scores, -1e30)
                        weights = jnp.exp2(scores * factor)
                        change = dot_nt(value_wide, dwide_ref[head, span])
                        grad_scores = (weights * change).astype(jnp.bfloat16)
                        weights = weights.astype(jnp.bfloat16)
                        dv_ref[...] += dot_nn(weights, dwide_ref[head, span, :LANES])
                        dk_ref[...] += dot_nn(grad_scores, qwide_ref[head, span, :LANES])
                        dq_ref[head, span] += dot_tn(grad_scores, key_low)

            block_grads[shard][0, part] = (dk_ref[...] * scale).astype(jnp.bfloat16)
            block_grads[shard][1, part] = dv_ref[...].astype(jnp.bfloat16)
    gain_total = jnp.zeros((1, LANES), jnp.float32)
    for head in range(per_kv):
        columns = slice(head * LANES, (head + 1) * LANES)
        grads = rope_back(dq_ref[head] * scale, cos_ref[...], sin_ref[...])
        gain_part, query_grad = unit_back(raw_ref[:, columns], gain_ref[...], grads)
        gain_total += gain_part
        query_in_ref[:, columns] = query_grad.astype(jnp.bfloat16)

    @pl.when(pl.program_id(0) == 0)
    def _():
        gain_grad_ref[...] = jnp.zeros_like(gain_grad_ref)

    gain_grad_ref[0:1] += gain_total


def attend_backward(
    index,
    batches,
    tables,
    out_in,
    w_out,
    query_low,
    gates,
    logs,
    attended,
    query_raw,
    cos_rows,
    sin_rows,
    gain,
    blocks,
    per_kv,
):
    need, query_mask, key_mask = tables
    all_rows, wide = query_low.shape
    width = out_in.shape[1]
    rows = all_rows // batches
    shards = len(blocks)
    groups = wide // (per_kv * LANES)
    own = per_kv * LANES
    block, _ = tiles_of(rows)
    merged_spec = pl.BlockSpec((rows, own), lambda g, need: (index, g))
    table_spec = pl.BlockSpec((rows, LANES), lambda g, need: (index, 0))
    return pl.pallas_call(
        functools.partial(backward_kernel, shards, per_kv),
        grid_spec=pltpu.PrefetchScalarGridSpec(
            num_scalar_prefetch=1,
            grid=(groups,),
            in_specs=[
                whole_block(out_in.shape),
                pl.BlockSpec((own, width), lambda g, need: (g, 0)),
                merged_spec,
                whole_block(query_mask.shape),
                pl.BlockSpec((1, rows, LANES), lambda g, need: (g, index, 0)),
                whole_block(key_mask.shape),
                pl.BlockSpec((1, rows, LANES), lambda g, need: (g, 0, 0)),
                pl.BlockSpec((rows, own), lambda g, need: (0, g)),
                merged_spec,
                table_spec,
                table_spec,
                whole_block((1, LANES)),
            ]
            + [pl.BlockSpec((rows, LANES), lambda g, need: (0, g))] * shards
            + [pl.BlockSpec((rows, LANES), lambda g, need: (0, groups + g))] * shards,
            out_specs=[
                pl.BlockSpec((rows, own + LANES), lambda g, need: (0, g)),
                whole_block((8, LANES)),
            ]
            + [pl.BlockSpec((2, rows, LANES), lambda g, need: (0, 0, g))] * shards,
            scratch_shapes=[
                pltpu.VMEM((per_kv, rows, LANES), jnp.float32),
                pltpu.VMEM((block, LANES), jnp.float32),
                pltpu.VMEM((block, LANES), jnp.float32),
                pltpu.VMEM((per_kv, rows, 2 * LANES), jnp.bfloat16),
                pltpu.VMEM((per_kv, rows, 2 * LANES), jnp.bfloat16),
            ],
        ),
        out_shape=[
            jax.ShapeDtypeStruct((rows, groups * (own + LANES)), jnp.bfloat16),
            jax.ShapeDtypeStruct((8, LANES), jnp.float32),
        ]
        + [jax.ShapeDtypeStruct((2, rows, groups * LANES), jnp.bfloat16)] * shards,
        compiler_params=params(),
        cost_estimate=cost(
            14 * rows * rows * shards * wide,
            20 * rows * wide + 4 * shards * rows * wide,
            rows * rows * shards * groups * per_kv,
        ),
        name="attend_backward",
    )(
        need,
        out_in,
        w_out,
        query_low,
        query_mask,
        gates,
        key_mask,
        logs,
        attended,
        query_raw,
        cos_rows,
        sin_rows,
        gain,
        *blocks,
        *blocks,
    )


def key_back_kernel(groups, batches, raw_ref, cos_ref, sin_ref, gain_ref, *refs):
    grads_refs, (out_ref, gain_grad_ref) = refs[:batches], refs[batches:]
    rows = raw_ref.shape[0] // batches
    gain_total = jnp.zeros((1, LANES), jnp.float32)
    for index in range(batches):
        span = slice(index * rows, (index + 1) * rows)
        for k in range(groups):
            columns = slice(k * LANES, (k + 1) * LANES)
            grads = rope_back(
                grads_refs[index][0, :, columns].astype(jnp.float32),
                cos_ref[span],
                sin_ref[span],
            )
            gain_part, key_grad = unit_back(raw_ref[span, columns], gain_ref[...], grads)
            gain_total += gain_part
            out_ref[span, 2 * k * LANES : (2 * k + 1) * LANES] = key_grad.astype(jnp.bfloat16)
            out_ref[span, (2 * k + 1) * LANES : (2 * k + 2) * LANES] = grads_refs[index][
                1, :, columns
            ]
    gain_grad_ref[...] = jnp.broadcast_to(gain_total, gain_grad_ref.shape)


def key_back(key_raw, cos_rows, sin_rows, gain, key_grads):
    rows, wide = key_raw.shape
    batches = len(key_grads)
    return pl.pallas_call(
        functools.partial(key_back_kernel, wide // LANES, batches),
        out_shape=[
            jax.ShapeDtypeStruct((rows, 2 * wide), jnp.bfloat16),
            jax.ShapeDtypeStruct((8, LANES), jnp.float32),
        ],
        compiler_params=params(),
        cost_estimate=cost(30 * rows * wide, 12 * rows * wide),
        name="key_back",
    )(key_raw, cos_rows, sin_rows, gain, *key_grads)


def sum_kernel(count, transposed, *refs):
    lefts, rights, out_ref = refs[:count], refs[count : 2 * count], refs[2 * count]
    dot = dot_nt if transposed else dot_nn
    total = dot(lefts[0][...], rights[0][...])
    for left, right in zip(lefts[1:], rights[1:]):
        total += dot(left[...], right[...])
    out_ref[...] = total.astype(jnp.bfloat16)


def sum_of_products(rows, lefts, rights, transposed):
    def left_spec(place):
        _, depth, row_block, column_block = place
        return pl.BlockSpec((rows, depth), lambda n: (row_block, column_block))

    columns = rights[0].shape[0 if transposed else 1]
    block = min(256, columns)
    depth_total = sum(place[1] for place in lefts)
    right_specs = [
        pl.BlockSpec((block, right.shape[1]), lambda n: (n, 0))
        if transposed
        else pl.BlockSpec((right.shape[0], block), lambda n: (0, n))
        for right in rights
    ]
    return pl.pallas_call(
        functools.partial(sum_kernel, len(lefts), transposed),
        grid=(columns // block,),
        in_specs=[left_spec(place) for place in lefts] + right_specs,
        out_specs=pl.BlockSpec((rows, block), lambda n: (0, n)),
        out_shape=jax.ShapeDtypeStruct((rows, columns), jnp.bfloat16),
        compiler_params=params(),
        cost_estimate=cost(
            2 * rows * depth_total * columns,
            2 * depth_total * (rows + columns) + 2 * rows * columns,
        ),
        name="sum_of_products",
    )(*[place[0] for place in lefts], *rights)


def mlp_kernel(batches, down_in_ref, *refs):
    inputs = refs[:batches]
    gate_w, up_w, down_w, hidden_ref, gate_in_ref, up_in_ref = refs[batches:]
    rows = inputs[0].shape[0]
    for index in range(batches):
        span = slice(index * rows, (index + 1) * rows)
        gate_pre = dot_nn(inputs[index][...], gate_w[...])
        up_pre = dot_nn(inputs[index][...], up_w[...])
        grad_hidden = dot_nt(down_in_ref[span], down_w[...])
        sigmoid_gate = jax.nn.sigmoid(gate_pre)
        silu_gate = gate_pre * sigmoid_gate
        hidden_ref[span] = (silu_gate * up_pre).astype(jnp.bfloat16)
        up_in_ref[span] = (grad_hidden * silu_gate).astype(jnp.bfloat16)
        gate_in_ref[span] = (
            grad_hidden * up_pre * sigmoid_gate * (1.0 + gate_pre * (1.0 - sigmoid_gate))
        ).astype(jnp.bfloat16)


def mlp_units(inputs, down_in, gate_w, up_w, down_w):
    rows, width = down_in.shape
    units = gate_w.shape[1]
    block = min(256, units)
    out_spec = pl.BlockSpec((rows, block), lambda n: (0, n))
    return pl.pallas_call(
        functools.partial(mlp_kernel, len(inputs)),
        grid=(units // block,),
        in_specs=[whole_block(down_in.shape)]
        + [whole_block(part.shape) for part in inputs]
        + [
            pl.BlockSpec((width, block), lambda n: (0, n)),
            pl.BlockSpec((width, block), lambda n: (0, n)),
            pl.BlockSpec((block, width), lambda n: (n, 0)),
        ],
        out_specs=[out_spec] * 3,
        out_shape=[jax.ShapeDtypeStruct((rows, units), jnp.bfloat16)] * 3,
        compiler_params=params(),
        cost_estimate=cost(
            6 * rows * width * units, 4 * rows * width + 6 * width * units + 6 * rows * units
        ),
        name="mlp_units",
    )(down_in, *inputs, gate_w, up_w, down_w)


def add_norm_kernel(stream_ref, low_ref, other_ref, gain_ref, middle_ref, normed_ref):
    middle = (
        stream_ref[...].astype(jnp.float32)
        + (low_ref[...].astype(jnp.float32) + other_ref[...].astype(jnp.float32))
    )
    unit, _ = unit_of(middle)
    middle_ref[...] = middle
    normed_ref[...] = (unit * gain_ref[...]).astype(jnp.bfloat16)


def add_norm(index, stream, low_part, other_part, gain):
    rows, width = low_part.shape
    block = min(128, rows)
    first = index * (rows // block)
    spec = pl.BlockSpec((block, width), lambda m: (m, 0))
    return pl.pallas_call(
        add_norm_kernel,
        grid=(rows // block,),
        in_specs=[
            pl.BlockSpec((block, width), lambda m: (first + m, 0)),
            spec,
            spec,
            whole_block((1, width)),
        ],
        out_specs=[spec, spec],
        out_shape=[
            jax.ShapeDtypeStruct((rows, width), jnp.float32),
            jax.ShapeDtypeStruct((rows, width), jnp.bfloat16),
        ],
        compiler_params=params(),
        cost_estimate=cost(8 * rows * width, 12 * rows * width),
        name="add_norm",
    )(stream, low_part, other_part, gain)


def norm_back_kernel(values_ref, low_ref, other_ref, gain_ref, up_ref, *outs):
    grads = low_ref[...].astype(jnp.float32) + other_ref[...].astype(jnp.float32)
    gain_part, back = unit_back(values_ref[...].astype(jnp.float32), gain_ref[...], grads)
    total = up_ref[...].astype(jnp.float32) + back
    outs[0][...] = total.astype(jnp.bfloat16)
    for out_ref in outs[2:]:
        out_ref[...] = total

    @pl.when(pl.program_id(0) == 0)
    def _():
        outs[1][...] = jnp.zeros_like(outs[1])

    outs[1][0:1] += gain_part


def norm_back(values, values_at, low_part, other_part, gain, upstream, up_at, keep):
    rows, width = low_part.shape
    block = min(128, rows)
    steps = rows // block
    spec = pl.BlockSpec((block, width), lambda m: (m, 0))
    return pl.pallas_call(
        norm_back_kernel,
        grid=(steps,),
        in_specs=[
            pl.BlockSpec((block, width), lambda m: (values_at * steps + m, 0)),
            spec,
            spec,
            whole_block((1, width)),
            pl.BlockSpec((block, width), lambda m: (up_at * steps + m, 0)),
        ],
        out_specs=[spec, whole_block((8, width))] + [spec] * keep,
        out_shape=[
            jax.ShapeDtypeStruct((rows, width), jnp.bfloat16),
            jax.ShapeDtypeStruct((8, width), jnp.float32),
        ]
        + [jax.ShapeDtypeStruct((rows, width), jnp.float32)] * keep,
        compiler_params=params(),
        cost_estimate=cost(16 * rows * width, 16 * rows * width),
        name="norm_back",
    )(values, low_part, other_part, gain, upstream)


def order_kernel(own_ref, *refs):
    pieces, out_ref = refs[:-1], refs[-1]
    for place, piece in enumerate(pieces):

        @pl.when(pl.program_id(0) == place)
        def _(piece=piece):
            out_ref[...] = piece[...].astype(jnp.float32)


def in_order(pieces, axis, column=0, size=None):
    rows, width = pieces[0].shape
    size = width if size is None else size
    count = len(pieces)
    own = lax.axis_index("replica").astype(jnp.int32).reshape(1)

    def place_of(step, own):
        quarter = jnp.bitwise_xor(own[0], jnp.where(step == 1, 2, jnp.where(step == 2, 1, step)))
        return (quarter, 0) if axis == 0 else (0, quarter)

    shape = (count * rows, size) if axis == 0 else (rows, count * size)
    return pl.pallas_call(
        order_kernel,
        grid_spec=pltpu.PrefetchScalarGridSpec(
            num_scalar_prefetch=1,
            grid=(count,),
            in_specs=[pl.BlockSpec((rows, size), lambda step, own: (0, column))] * count,
            out_specs=pl.BlockSpec((rows, size), place_of),
        ),
        out_shape=jax.ShapeDtypeStruct(shape, jnp.float32),
        compiler_params=params(),
        cost_estimate=cost(count * rows * size, 6 * count * rows * size),
        name="in_order",
    )(own, *pieces)


def local(
    tokens,
    cotangent,
    lengths,
    parents,
    attn_gain,
    qk_gain,
    w_query,
    key_weight_matrix,
    value_weight_matrix,
    w_headgate,
    w_out,
    mlp_gain,
    w_gate,
    w_up,
    w_down,
):
    batches, rows, width = tokens.shape
    shards = lax.axis_size("fsdp")
    shard = lax.axis_index("fsdp")
    query_gain, key_gain = qk_gain[0, 0:1], qk_gain[0, 1:2]
    low = jnp.bfloat16

    query_piece = own_quarter(w_query[0], 1)
    gate_piece = own_quarter(w_headgate[0], 1)
    per_kv = query_piece.shape[1] // LANES
    own = per_kv * LANES
    pad = jnp.zeros((query_piece.shape[0], LANES - gate_piece.shape[1]), low)
    key_value_w = gather_quarters(
        jnp.concatenate(
            [own_quarter(key_weight_matrix[0], 1), own_quarter(value_weight_matrix[0], 1)], axis=1
        ),
        0,
    )
    query_w = gather_quarters(jnp.concatenate([query_piece, gate_piece, pad], axis=1), 0)
    out_w = jnp.concatenate(gather_quarters(own_quarter(w_out[0], 0), 1), axis=0)
    gate_w = gather_quarters(own_quarter(w_gate[0], 1), 0)
    up_w = gather_quarters(own_quarter(w_up[0], 1), 0)
    down_w = gather_quarters(own_quarter(w_down[0], 0), 1)
    groups = len(query_w)

    tables, positions = [], []
    for index in range(batches):
        need, query_mask, key_mask, position = tree_need(
            lengths[index, 0], parents[index, 0], shard, rows, shards
        )
        tables.append((need, query_mask, key_mask))
        positions.append(position)
    half = LANES // 2
    frequency = THETA ** (-(jnp.arange(half, dtype=jnp.float32) * 2.0 / LANES))
    angle = jnp.concatenate(positions).astype(jnp.float32)[:, None] * frequency[None, :]
    cosine, sine = jnp.cos(angle), jnp.sin(angle)
    cos_rows = jnp.concatenate([cosine, cosine], axis=1)
    sin_rows = jnp.concatenate([-sine, sine], axis=1)

    stream = tokens.reshape(batches * rows, width)
    down_in = cotangent.reshape(batches * rows, width)
    normed_low = (unit_of(stream.astype(jnp.float32))[0] * attn_gain).astype(low)
    key_value, key_raw = key_value_heads(normed_low, key_value_w, cos_rows, sin_rows, key_gain)
    query_low, query_raw, gates = query_heads(
        normed_low, query_w, cos_rows, sin_rows, query_gain, per_kv
    )
    blocks, mixed, attended, logs, middle, mlp_low = [], [], [], [], [], []
    for index in range(batches):
        blocks.append(relay_forward(key_value[index * rows : (index + 1) * rows], shards))
        tree_mixed, tree_out, tree_log = attend_forward(
            index, batches, tables[index], query_low, gates, blocks[index], per_kv
        )
        mixed.append(tree_mixed)
        attended.append(tree_out)
        logs.append(tree_log)
        part = sum_of_products(rows, [(tree_mixed, groups * own, 0, 0)], [out_w], False)
        tree_middle, tree_normed = add_norm(index, stream, part, tensor_other(part), mlp_gain)
        middle.append(tree_middle)
        mlp_low.append(tree_normed)

    units = [mlp_units(mlp_low, down_in, gate_w[k], up_w[k], down_w[k]) for k in range(groups)]
    hidden = [unit[0] for unit in units]
    gate_in = [unit[1] for unit in units]
    up_in = [unit[2] for unit in units]
    unit_width = hidden[0].shape[1]
    mlp_gain_grad, grad_middle, out_in = [], [], []
    for index in range(batches):
        part = sum_of_products(
            rows,
            [(member, unit_width, index, 0) for member in gate_in + up_in],
            gate_w + up_w,
            True,
        )
        low_out, gain_part, full = norm_back(
            middle[index], 0, part, tensor_other(part), mlp_gain, down_in, index, 1
        )
        out_in.append(low_out)
        mlp_gain_grad.append(gain_part)
        grad_middle.append(full)
    mlp_all = jnp.concatenate(mlp_low, axis=0)
    down_shard = fold_quarters(lambda k: dot_tn(hidden[k], down_in), 1)
    gate_shard = fold_quarters(lambda k: dot_tn(mlp_all, gate_in[k]), 0)
    up_shard = fold_quarters(lambda k: dot_tn(mlp_all, up_in[k]), 0)
    results = []
    for index in range(batches):
        part = sum_of_products(
            rows, [(member, unit_width, index, 0) for member in hidden], down_w, False
        )
        results.append(
            (
                middle[index]
                + (part.astype(jnp.float32) + tensor_other(part).astype(jnp.float32))
            ).astype(low)
        )

    query_in, query_gain_grad, key_grads = [], [], []
    for index in range(batches):
        tree_in, gain_part, *parts = attend_backward(
            index,
            batches,
            tables[index],
            out_in[index],
            out_w,
            query_low,
            gates,
            logs[index],
            attended[index],
            query_raw,
            cos_rows,
            sin_rows,
            query_gain,
            blocks[index],
            per_kv,
        )
        query_in.append(tree_in)
        query_gain_grad.append(gain_part)
        key_grads.append(relay_back(parts, shards))
    mixed_all = jnp.concatenate(mixed, axis=0)
    out_in_all = jnp.concatenate(out_in, axis=0)
    query_in_all = jnp.concatenate(query_in, axis=0)
    out_shard = fold_quarters(
        lambda k: dot_tn(mixed_all[:, k * own : (k + 1) * own], out_in_all), 1
    )
    query_block = own + LANES
    query_shard = fold_quarters(
        lambda k: dot_tn(normed_low, query_in_all[:, k * query_block : (k + 1) * query_block]), 0
    )
    key_in, key_gain_grad = key_back(key_raw, cos_rows, sin_rows, key_gain, key_grads)
    key_block = 2 * LANES
    key_shard = fold_quarters(
        lambda k: dot_tn(normed_low, key_in[:, k * key_block : (k + 1) * key_block]), 0
    )
    attn_gain_grad, input_grad = [], []
    for index in range(batches):
        part = sum_of_products(
            rows,
            [(query_in[index], query_block, 0, k) for k in range(groups)]
            + [(key_in, key_block, index, k) for k in range(groups)],
            query_w + key_value_w,
            True,
        )
        low_out, gain_part = norm_back(
            stream, index, part, tensor_other(part), attn_gain, grad_middle[index], 0, 0
        )
        input_grad.append(low_out)
        attn_gain_grad.append(gain_part)

    first = lax.axis_index("tensor") == 0
    attn_sum, mlp_sum = [
        jnp.where(first, jnp.sum(jnp.stack(parts), axis=0)[0], 0.0)
        for parts in (attn_gain_grad, mlp_gain_grad)
    ]
    query_sum = jnp.sum(jnp.stack(query_gain_grad), axis=0)[0]
    gain_sum = lax.psum(
        jnp.concatenate([attn_sum, mlp_sum, query_sum, key_gain_grad[0]]),
        ("replica", "fsdp", "tensor"),
    )

    def own_slice(value, axis):
        size = value.shape[axis] // shards
        return lax.dynamic_slice_in_dim(value, shard * size, size, axis)[None]

    gate_grad = in_order([piece[:, own:] for piece in query_shard], 1)
    gate_count = gate_piece.shape[1]
    gate_grad = gate_grad.reshape(gate_grad.shape[0], groups, LANES)[:, :, :gate_count]
    return (
        jnp.stack(results),
        jnp.stack(input_grad),
        own_slice(gain_sum[:width], 0),
        own_slice(gain_sum[2 * width :].reshape(2, LANES), 1),
        in_order([piece[:, :own] for piece in query_shard], 1)[None],
        in_order(key_shard, 1, 0, LANES)[None],
        in_order(key_shard, 1, 1, LANES)[None],
        gate_grad.reshape(1, gate_grad.shape[0], groups * gate_count),
        in_order(out_shard, 0)[None],
        own_slice(gain_sum[width : 2 * width], 0),
        in_order(gate_shard, 1)[None],
        in_order(up_shard, 1)[None],
        in_order(down_shard, 0)[None],
    )


def solution(mesh):
    placed = (
        P(None, ("replica", "fsdp"), None),
        P(None, ("replica", "fsdp"), None),
        P(None, "replica", None),
        P(None, "replica", None),
        P(),
        P(),
        P(None, "fsdp", "tensor"),
        P(None, "fsdp", "tensor"),
        P(None, "fsdp", "tensor"),
        P(None, "fsdp", "tensor"),
        P(None, "tensor", "fsdp"),
        P(),
        P(None, "fsdp", "tensor"),
        P(None, "fsdp", "tensor"),
        P(None, "tensor", "fsdp"),
    )
    return jax.shard_map(
        local,
        mesh=mesh,
        in_specs=placed,
        out_specs=(
            P(None, ("replica", "fsdp"), None),
            P(None, ("replica", "fsdp"), None),
            P(None, "fsdp"),
            P(None, None, "fsdp"),
            P(None, "fsdp", "tensor"),
            P(None, "fsdp", "tensor"),
            P(None, "fsdp", "tensor"),
            P(None, "fsdp", "tensor"),
            P(None, "tensor", "fsdp"),
            P(None, "fsdp"),
            P(None, "fsdp", "tensor"),
            P(None, "fsdp", "tensor"),
            P(None, "tensor", "fsdp"),
        ),
        check_vma=False,
    )
```

```python
import functools

import jax
import jax.numpy as jnp
from jax import lax
from jax.experimental import pallas as pl
from jax.experimental.pallas import tpu as pltpu
from jax.sharding import PartitionSpec as P

EPSILON = 1e-06
THETA = 1000000.0
LOG2_E = 1.4426950408889634
LANES = 128
EXTRA_AT = 16
VMEM_BYTES = 36 * 1024 * 1024
COST_SHARE = 0.22
GATHER_AFTER = 2


def segment_table(lengths, parents):
    count = lengths.shape[0]
    starts = jnp.cumsum(lengths) - lengths
    labels = jnp.arange(count, dtype=jnp.int32)
    parent_hot = (parents[:, None] == labels[None, :]).astype(jnp.int32)
    grand_hot = jnp.dot(parent_hot, parent_hot)
    eye_hot = (labels[:, None] == labels[None, :]).astype(jnp.int32)
    ancestor = (eye_hot + parent_hot + grand_hot > 0).astype(jnp.int32)
    before = jnp.sum(ancestor * (1 - eye_hot) * lengths[None, :], axis=1)
    return (starts, before - starts, ancestor)


def row_segments(indices, starts, count):
    labels = jnp.arange(count, dtype=jnp.int32)
    member = jnp.sum((indices[:, None] >= starts[None, :]).astype(jnp.int32), axis=1) - 1
    return (member[:, None] == labels[None, :]).astype(jnp.int32)


def swaps(bit, count):
    return [(index, index ^ bit) for index in range(count)]


def across(value, bit):
    return lax.ppermute(value, "replica", swaps(bit, lax.axis_size("replica")))


def own_quarter(shard, axis):
    size = shard.shape[axis] // lax.axis_size("replica")
    return lax.dynamic_slice_in_dim(shard, lax.axis_index("replica") * size, size, axis)


def spread(block):
    other = across(block, 2)
    return [block, other, across(block, 1), across(other, 1)]


def after(value, *earlier):
    return lax.optimization_barrier((value, *earlier))[0] if earlier else value


class Line:
    def __init__(self, depth):
        self.depth = depth
        self.sent = []
        self.held = []

    def before(self):
        last = [self.sent[-self.depth]] if len(self.sent) >= self.depth else []
        held, self.held = self.held, []
        return last + held

    def hold(self, *values):
        self.held += values

    def run(self, function, value, *rest):
        result = function(after(value, *self.before()), *rest)
        self.sent.append(result[0] if isinstance(result, (list, tuple)) else result)
        return result


def gather_shards(value):
    return lax.all_gather(value, "fsdp", axis=0, tiled=True)


def gather_stacked(value):
    return lax.all_gather(value, "fsdp", axis=0, tiled=False)


def scatter_rows(value):
    return lax.psum_scatter(value, "fsdp", scatter_dimension=0, tiled=True)


def to_far(value):
    return across(value, 2)


def spread(block, far_line):
    other = far_line.run(to_far, block)
    return [block, other, across(block, 1), across(other, 1)]


def axis_sum(value, axis):
    size, bit = lax.axis_size(axis), 1
    while bit < size:
        if bit * 4 <= size:
            near, far, both = [
                lax.ppermute(value, axis, swaps(bit * flip, size)) for flip in (1, 2, 3)
            ]
            value, bit = (value + near) + (far + both), bit * 4
        else:
            value, bit = value + lax.ppermute(value, axis, swaps(bit, size)), bit * 2
    return value


def tensor_other(low_part):
    return lax.ppermute(low_part, "tensor", swaps(1, lax.axis_size("tensor")))


class Relay:
    def __init__(self, block, count):
        self.blocks, self.count, self.held = [block], count, []
        self.latest = block

    def hold(self, *values):
        self.held += values

    def advance(self):
        if len(self.blocks) < self.count:
            value = after(self.blocks[-1], *self.held) if self.held else self.blocks[-1]
            self.held = []
            pairs = [(index, index + 1) for index in range(self.count - 1)]
            self.blocks.append(lax.ppermute(value, "fsdp", pairs))
            self.latest = self.blocks[-1]


def relay_back(parts, count):
    carry, steps = parts[count - 1], []
    for step in reversed(range(1, count)):
        arrived = lax.ppermute(carry, "fsdp", [(index, index - 1) for index in range(1, count)])
        carry = (parts[step - 1].astype(jnp.float32) + arrived.astype(jnp.float32)).astype(
            jnp.bfloat16
        )
        steps.append(carry)
    return steps


def params():
    return pltpu.CompilerParams(vmem_limit_bytes=VMEM_BYTES)


def cost(flops, moved, rate=0.56):
    return pl.CostEstimate(
        flops=int(flops * COST_SHARE / rate),
        bytes_accessed=int(moved * COST_SHARE / 0.6),
        transcendentals=0,
    )


def whole_block(shape):
    return pl.BlockSpec(shape, lambda *index: (0,) * len(shape), pipeline_mode=pl.Buffered(1))


def sum_block(shape):
    return pl.BlockSpec(shape, lambda *index: (0,) * len(shape))


def dot_nn(left, right):
    return jnp.dot(left, right, preferred_element_type=jnp.float32)


def dot_nt(left, right):
    return lax.dot_general(
        left, right, (((1,), (1,)), ((), ())), preferred_element_type=jnp.float32
    )


def dot_tn(left, right):
    return lax.dot_general(
        left, right, (((0,), (0,)), ((), ())), preferred_element_type=jnp.float32
    )


def three_parts(value):
    first = value.astype(jnp.bfloat16)
    rest = value - first.astype(jnp.float32)
    second = rest.astype(jnp.bfloat16)
    third = (rest - second.astype(jnp.float32)).astype(jnp.bfloat16)
    return (first, second, third)


def put_lanes(base, parts):
    lane = lax.broadcasted_iota(jnp.int32, base.shape, 1)
    value = base.astype(jnp.float32)
    for offset, part in enumerate(parts):
        value = jnp.where(lane == EXTRA_AT + offset, part.astype(jnp.float32), value)
    return value.astype(jnp.bfloat16)


def rope(values, cos_rows, sin_rows):
    return values * cos_rows + pltpu.roll(values, LANES // 2, 1) * sin_rows


def rope_back(grads, cos_rows, sin_rows):
    return grads * cos_rows - pltpu.roll(grads, LANES // 2, 1) * sin_rows


def unit_of(raw):
    inverse = lax.rsqrt(jnp.mean(raw * raw, axis=-1, keepdims=True) + EPSILON)
    return (raw * inverse, inverse)


def unit_back(raw, gain, grads):
    unit, inverse = unit_of(raw)
    scaled = grads * gain
    gain_part = jnp.sum(grads * unit, axis=0, keepdims=True)
    return (
        gain_part,
        inverse * (scaled - unit * jnp.mean(scaled * unit, axis=-1, keepdims=True)),
    )


def key_value_kernel(groups, x_ref, cos_ref, sin_ref, gain_ref, *refs):
    weights, (kv_ref, raw_ref) = refs[:groups], refs[groups:]
    for k in range(groups):
        part = dot_nn(x_ref[...], weights[k][...])
        raw = part[:, :LANES]
        unit, _ = unit_of(raw)
        raw_ref[:, k * LANES : (k + 1) * LANES] = raw
        kv_ref[:, k * LANES : (k + 1) * LANES] = rope(
            unit * gain_ref[...], cos_ref[...], sin_ref[...]
        ).astype(jnp.bfloat16)
        at = (groups + k) * LANES
        kv_ref[:, at : at + LANES] = part[:, LANES:].astype(jnp.bfloat16)


def key_value_heads(normed_low, weights, cos_rows, sin_rows, gain):
    rows, width = normed_low.shape
    groups, block = len(weights), min(256, rows)
    return pl.pallas_call(
        functools.partial(key_value_kernel, groups),
        grid=(rows // block,),
        in_specs=[
            pl.BlockSpec((block, width), lambda m: (m, 0)),
            pl.BlockSpec((block, LANES), lambda m: (m, 0)),
            pl.BlockSpec((block, LANES), lambda m: (m, 0)),
            whole_block((1, LANES)),
        ]
        + [whole_block(weight.shape) for weight in weights],
        out_specs=[
            pl.BlockSpec((block, 2 * groups * LANES), lambda m: (m, 0)),
            pl.BlockSpec((block, groups * LANES), lambda m: (m, 0)),
        ],
        out_shape=[
            jax.ShapeDtypeStruct((rows, 2 * groups * LANES), jnp.bfloat16),
            jax.ShapeDtypeStruct((rows, groups * LANES), jnp.float32),
        ],
        compiler_params=params(),
        cost_estimate=cost(4 * rows * width * groups * LANES, 4 * rows * width),
        name="key_value_heads",
    )(normed_low, cos_rows, sin_rows, gain, *weights)


def query_kernel(groups, per_kv, x_ref, cos_ref, sin_ref, gain_ref, *refs):
    weights, (low_ref, raw_ref, gate_ref) = refs[:groups], refs[groups:]
    for k in range(groups):
        part = dot_nn(x_ref[...], weights[k][...])
        for head in range(per_kv):
            raw = part[:, head * LANES : (head + 1) * LANES]
            unit, _ = unit_of(raw)
            at = (k * per_kv + head) * LANES
            raw_ref[:, at : at + LANES] = raw
            low_ref[:, at : at + LANES] = rope(
                unit * gain_ref[...], cos_ref[...], sin_ref[...]
            ).astype(jnp.bfloat16)
        gate_ref[k] = jax.nn.sigmoid(part[:, per_kv * LANES :])


def query_heads(normed_low, weights, cos_rows, sin_rows, gain, per_kv):
    rows, width = normed_low.shape
    groups, block = len(weights), min(256, rows)
    wide = groups * per_kv * LANES
    return pl.pallas_call(
        functools.partial(query_kernel, groups, per_kv),
        grid=(rows // block,),
        in_specs=[
            pl.BlockSpec((block, width), lambda m: (m, 0)),
            pl.BlockSpec((block, LANES), lambda m: (m, 0)),
            pl.BlockSpec((block, LANES), lambda m: (m, 0)),
            whole_block((1, LANES)),
        ]
        + [whole_block(weight.shape) for weight in weights],
        out_specs=[
            pl.BlockSpec((block, wide), lambda m: (m, 0)),
            pl.BlockSpec((block, wide), lambda m: (m, 0)),
            pl.BlockSpec((groups, block, LANES), lambda m: (0, m, 0)),
        ],
        out_shape=[
            jax.ShapeDtypeStruct((rows, wide), jnp.bfloat16),
            jax.ShapeDtypeStruct((rows, wide), jnp.float32),
            jax.ShapeDtypeStruct((groups, rows, LANES), jnp.float32),
        ],
        compiler_params=params(),
        cost_estimate=cost(2 * rows * width * groups * (per_kv + 1) * LANES, 4 * rows * width),
        name="query_heads",
    )(normed_low, cos_rows, sin_rows, gain, *weights)


def tiles_of(row_count):
    block = min(256, row_count)
    return (block, row_count // block)


def tree_need(lengths, parents, shard, row_count, shards):
    count = lengths.shape[0]
    starts, offsets, ancestor = segment_table(lengths, parents)
    block, tiles = tiles_of(row_count)
    query_index = shard * row_count + jnp.arange(row_count, dtype=jnp.int32)
    query_hot = row_segments(query_index, starts, count)
    reach = jnp.sum(query_hot[:, :, None] * ancestor[None, :, :], axis=1)
    position = query_index + jnp.sum(query_hot * offsets[None, :], axis=1)
    back = jnp.arange(shards, dtype=jnp.int32)[:, None]
    key_index = (shard - back) * row_count + jnp.arange(row_count, dtype=jnp.int32)[None, :]
    key_hot = row_segments(key_index.reshape(-1), starts, count)
    query_has = jnp.max(reach.reshape(tiles, block, count), axis=1)
    key_has = jnp.max(key_hot.reshape(shards, tiles, block, count), axis=2)
    need = jnp.sum(query_has[:, None, None, :] * key_has[None], axis=-1) > 0
    wall = jnp.where(reach > 0, 0.0, -1e30)
    query_mask = jnp.pad(wall, ((0, 0), (0, LANES - count))).astype(jnp.bfloat16)
    lane = jnp.arange(LANES)[None, :]
    ones = ((lane >= EXTRA_AT) & (lane < EXTRA_AT + 3)).astype(jnp.float32)
    key_mask = jnp.pad(key_hot.astype(jnp.float32), ((0, 0), (0, LANES - count))) + ones
    return (need.astype(jnp.int32).reshape(-1), query_mask, key_mask.astype(jnp.bfloat16), position)


def forward_kernel(
    shards, per_kv, factor, need_ref, q_ref, qmask_ref, gate_ref, kmask_ref, *refs
):
    keys, values = refs[:shards], refs[shards : 2 * shards]
    mixed_ref, attended_ref, log_ref, total_ref = refs[-4:]
    rows = q_ref.shape[0]
    block, tiles = tiles_of(rows)
    lane = lax.broadcasted_iota(jnp.int32, (block, LANES), 1)
    for qi in range(tiles):
        span = slice(qi * block, (qi + 1) * block)
        total_ref[...] = jnp.zeros_like(total_ref)
        for shard in range(shards):
            for ci in range(tiles):
                if shard == 0 and ci > qi:
                    continue
                part = slice(ci * block, (ci + 1) * block)

                @pl.when(need_ref[(qi * shards + shard) * tiles + ci] > 0)
                def _(shard=shard, ci=ci, part=part):
                    at = shard * rows + ci * block
                    key_mask = kmask_ref[at : at + block]
                    key_wide = jnp.concatenate([keys[shard][part], key_mask], axis=1)
                    value_wide = jnp.concatenate(
                        [values[shard][part], jnp.ones((block, LANES), jnp.bfloat16)], axis=1
                    )
                    for head in range(per_kv):
                        query_wide = jnp.concatenate(
                            [q_ref[span, head * LANES : (head + 1) * LANES], qmask_ref[span]],
                            axis=1,
                        )
                        scores = dot_nt(query_wide, key_wide)
                        if shard == 0 and ci == qi:
                            row = lax.broadcasted_iota(jnp.int32, (block, block), 0)
                            column = lax.broadcasted_iota(jnp.int32, (block, block), 1)
                            scores = jnp.where(column <= row, scores, -1e30)
                        weights = jnp.exp2(scores * factor).astype(jnp.bfloat16)
                        total_ref[head] += dot_nn(weights, value_wide)

        logs = jnp.zeros((block, LANES), jnp.float32)
        for head in range(per_kv):
            summed = total_ref[head][:, LANES:]
            tree_out = total_ref[head][:, :LANES] / summed
            columns = slice(head * LANES, (head + 1) * LANES)
            attended_ref[span, columns] = tree_out
            gate = gate_ref[0, span, head : head + 1]
            mixed_ref[span, columns] = (gate * tree_out).astype(jnp.bfloat16)
            logs = jnp.where(lane == head, jnp.log(summed), logs)
        log_ref[0, span] = logs


def attend_forward(index, batches, tables, query_low, gates, blocks, per_kv):
    need, query_mask, key_mask = tables
    all_rows, wide = query_low.shape
    rows = all_rows // batches
    shards = len(blocks)
    groups = wide // (per_kv * LANES)
    own = per_kv * LANES
    block, _ = tiles_of(rows)
    tree_spec = pl.BlockSpec((rows, own), lambda g, need: (0, g))
    log_spec = pl.BlockSpec((1, rows, LANES), lambda g, need: (g, 0, 0))
    return pl.pallas_call(
        functools.partial(forward_kernel, shards, per_kv, LANES ** (-0.5) * LOG2_E),
        grid_spec=pltpu.PrefetchScalarGridSpec(
            num_scalar_prefetch=1,
            grid=(groups,),
            in_specs=[
                pl.BlockSpec((rows, own), lambda g, need: (index, g)),
                whole_block(query_mask.shape),
                pl.BlockSpec((1, rows, LANES), lambda g, need: (g, index, 0)),
                whole_block(key_mask.shape),
            ]
            + [pl.BlockSpec((rows, LANES), lambda g, need: (0, g))] * shards
            + [pl.BlockSpec((rows, LANES), lambda g, need: (0, groups + g))] * shards,
            out_specs=[tree_spec, tree_spec, log_spec],
            scratch_shapes=[pltpu.VMEM((per_kv, block, 2 * LANES), jnp.float32)],
        ),
        out_shape=[
            jax.ShapeDtypeStruct((rows, wide), jnp.bfloat16),
            jax.ShapeDtypeStruct((rows, wide), jnp.float32),
            jax.ShapeDtypeStruct((groups, rows, LANES), jnp.float32),
        ],
        compiler_params=params(),
        cost_estimate=cost(
            4 * rows * rows * shards * wide,
            8 * rows * wide + 2 * shards * rows * wide,
            0.19,
        ),
        name="attend_forward",
    )(need, query_low, query_mask, gates, key_mask, *blocks, *blocks)


def backward_kernel(
    shards,
    per_kv,
    need_ref,
    out_in_ref,
    w_out_ref,
    q_ref,
    qmask_ref,
    gate_ref,
    kmask_ref,
    log_ref,
    attended_ref,
    raw_ref,
    cos_ref,
    sin_ref,
    gain_ref,
    *refs,
):
    scale = LANES ** (-0.5)
    factor = scale * LOG2_E
    keys, values = refs[:shards], refs[shards : 2 * shards]
    query_in_ref, gain_grad_ref = refs[2 * shards : 2 * shards + 2]
    block_grads = refs[2 * shards + 2 : 3 * shards + 2]
    dq_ref, dk_ref, dv_ref, qwide_ref, dwide_ref = refs[3 * shards + 2 :]
    rows = q_ref.shape[0]
    block, tiles = tiles_of(rows)
    grad_mixed = split_dot_nt(out_in_ref[...], w_out_ref)
    lane = lax.broadcasted_iota(jnp.int32, (rows, LANES), 1)
    logits = jnp.zeros((rows, LANES), jnp.float32)
    for head in range(per_kv):
        columns = slice(head * LANES, (head + 1) * LANES)
        attended = attended_ref[:, columns]
        gate = gate_ref[0, :, head : head + 1]
        mixed_grad = grad_mixed[:, columns]
        logit = jnp.sum(mixed_grad * attended, axis=-1, keepdims=True) * gate * (1.0 - gate)
        logits = jnp.where(lane == head, logit, logits)
        attended_in = (mixed_grad * gate).astype(jnp.bfloat16)
        delta = jnp.sum(attended_in.astype(jnp.float32) * attended, axis=-1, keepdims=True)
        dwide_ref[head, :, :LANES] = attended_in
        dwide_ref[head, :, LANES:] = put_lanes(
            jnp.zeros((rows, LANES), jnp.bfloat16), three_parts(-delta)
        )
        qwide_ref[head, :, :LANES] = q_ref[:, columns]
        qwide_ref[head, :, LANES:] = put_lanes(
            qmask_ref[...], three_parts(log_ref[0, :, head : head + 1] * (-1.0 / scale))
        )
    query_in_ref[:, per_kv * LANES :] = logits.astype(jnp.bfloat16)
    dq_ref[...] = jnp.zeros_like(dq_ref)
    for shard in range(shards):
        for ci in range(tiles):
            part = slice(ci * block, (ci + 1) * block)
            at = shard * rows + ci * block
            dk_ref[...] = jnp.zeros_like(dk_ref)
            dv_ref[...] = jnp.zeros_like(dv_ref)
            for qi in range(tiles):
                if shard == 0 and ci > qi:
                    continue
                span = slice(qi * block, (qi + 1) * block)

                @pl.when(need_ref[(qi * shards + shard) * tiles + ci] > 0)
                def _(shard=shard, ci=ci, qi=qi, at=at, part=part, span=span):
                    key_low = keys[shard][part]
                    key_mask = kmask_ref[at : at + block]
                    key_wide = jnp.concatenate([key_low, key_mask], axis=1)
                    value_wide = jnp.concatenate([values[shard][part], key_mask], axis=1)
                    for head in range(per_kv):
                        scores = dot_nt(key_wide, qwide_ref[head, span])
                        if shard == 0 and ci == qi:
                            row = lax.broadcasted_iota(jnp.int32, (block, block), 0)
                            column = lax.broadcasted_iota(jnp.int32, (block, block), 1)
                            scores = jnp.where(row <= column, scores, -1e30)
                        weights = jnp.exp2(scores * factor)
                        change = dot_nt(value_wide, dwide_ref[head, span])
                        grad_scores = (weights * change).astype(jnp.bfloat16)
                        weights = weights.astype(jnp.bfloat16)
                        dv_ref[...] += dot_nn(weights, dwide_ref[head, span, :LANES])
                        dk_ref[...] += dot_nn(grad_scores, qwide_ref[head, span, :LANES])
                        dq_ref[head, span] += dot_tn(grad_scores, key_low)

            block_grads[shard][0, part] = (dk_ref[...] * scale).astype(jnp.bfloat16)
            block_grads[shard][1, part] = dv_ref[...].astype(jnp.bfloat16)
    gain_total = jnp.zeros((1, LANES), jnp.float32)
    for head in range(per_kv):
        columns = slice(head * LANES, (head + 1) * LANES)
        grads = rope_back(dq_ref[head] * scale, cos_ref[...], sin_ref[...])
        gain_part, query_grad = unit_back(raw_ref[:, columns], gain_ref[...], grads)
        gain_total += gain_part
        query_in_ref[:, columns] = query_grad.astype(jnp.bfloat16)

    @pl.when(pl.program_id(0) == 0)
    def _():
        gain_grad_ref[...] = jnp.zeros_like(gain_grad_ref)

    gain_grad_ref[0:1] += gain_total


def attend_backward(
    index,
    batches,
    tables,
    out_in,
    w_out,
    query_low,
    gates,
    logs,
    attended,
    query_raw,
    cos_rows,
    sin_rows,
    gain,
    blocks,
    per_kv,
):
    need, query_mask, key_mask = tables
    all_rows, wide = query_low.shape
    rows = all_rows // batches
    shards = len(blocks)
    groups = wide // (per_kv * LANES)
    own = per_kv * LANES
    block, _ = tiles_of(rows)
    merged_spec = pl.BlockSpec((rows, own), lambda g, need: (index, g))
    table_spec = pl.BlockSpec((rows, LANES), lambda g, need: (index, 0))
    return pl.pallas_call(
        functools.partial(backward_kernel, shards, per_kv),
        grid_spec=pltpu.PrefetchScalarGridSpec(
            num_scalar_prefetch=1,
            grid=(groups,),
            in_specs=[
                whole_block(out_in.shape),
                pl.BlockSpec((None,) + w_out.shape[1:], lambda g, need: (g, 0, 0, 0)),
                merged_spec,
                whole_block(query_mask.shape),
                pl.BlockSpec((1, rows, LANES), lambda g, need: (g, index, 0)),
                whole_block(key_mask.shape),
                pl.BlockSpec((1, rows, LANES), lambda g, need: (g, 0, 0)),
                pl.BlockSpec((rows, own), lambda g, need: (0, g)),
                merged_spec,
                table_spec,
                table_spec,
                whole_block((1, LANES)),
            ]
            + [pl.BlockSpec((rows, LANES), lambda g, need: (0, g))] * shards
            + [pl.BlockSpec((rows, LANES), lambda g, need: (0, groups + g))] * shards,
            out_specs=[
                pl.BlockSpec((rows, own + LANES), lambda g, need: (0, g)),
                sum_block((8, LANES)),
            ]
            + [pl.BlockSpec((2, rows, LANES), lambda g, need: (0, 0, g))] * shards,
            scratch_shapes=[
                pltpu.VMEM((per_kv, rows, LANES), jnp.float32),
                pltpu.VMEM((block, LANES), jnp.float32),
                pltpu.VMEM((block, LANES), jnp.float32),
                pltpu.VMEM((per_kv, rows, 2 * LANES), jnp.bfloat16),
                pltpu.VMEM((per_kv, rows, 2 * LANES), jnp.bfloat16),
            ],
        ),
        out_shape=[
            jax.ShapeDtypeStruct((rows, groups * (own + LANES)), jnp.bfloat16),
            jax.ShapeDtypeStruct((8, LANES), jnp.float32),
        ]
        + [jax.ShapeDtypeStruct((2, rows, groups * LANES), jnp.bfloat16)] * shards,
        compiler_params=params(),
        cost_estimate=cost(
            14 * rows * rows * shards * wide,
            20 * rows * wide + 4 * shards * rows * wide,
            0.21,
        ),
        name="attend_backward",
    )(
        need,
        out_in,
        w_out,
        query_low,
        query_mask,
        gates,
        key_mask,
        logs,
        attended,
        query_raw,
        cos_rows,
        sin_rows,
        gain,
        *blocks,
        *blocks,
    )


def key_back_kernel(groups, raw_ref, cos_ref, sin_ref, gain_ref, grads_ref, out_ref, gain_grad_ref):
    gain_total = jnp.zeros((1, LANES), jnp.float32)
    for k in range(groups):
        columns = slice(k * LANES, (k + 1) * LANES)
        grads = rope_back(grads_ref[0, :, columns].astype(jnp.float32), cos_ref[...], sin_ref[...])
        gain_part, key_grad = unit_back(raw_ref[:, columns], gain_ref[...], grads)
        gain_total += gain_part
        out_ref[:, 2 * k * LANES : (2 * k + 1) * LANES] = key_grad.astype(jnp.bfloat16)
        out_ref[:, (2 * k + 1) * LANES : (2 * k + 2) * LANES] = grads_ref[1, :, columns]
    gain_grad_ref[...] = jnp.broadcast_to(gain_total, gain_grad_ref.shape)


def key_back(index, key_raw, cos_rows, sin_rows, gain, key_grad):
    _, rows, wide = key_grad.shape
    table_spec = pl.BlockSpec((rows, LANES), lambda m: (index, 0))
    return pl.pallas_call(
        functools.partial(key_back_kernel, wide // LANES),
        grid=(1,),
        in_specs=[
            pl.BlockSpec((rows, wide), lambda m: (index, 0)),
            table_spec,
            table_spec,
            sum_block((1, LANES)),
            sum_block(key_grad.shape),
        ],
        out_specs=[sum_block((rows, 2 * wide)), sum_block((8, LANES))],
        out_shape=[
            jax.ShapeDtypeStruct((rows, 2 * wide), jnp.bfloat16),
            jax.ShapeDtypeStruct((8, LANES), jnp.float32),
        ],
        compiler_params=params(),
        cost_estimate=cost(30 * rows * wide, 12 * rows * wide),
        name="key_back",
    )(key_raw, cos_rows, sin_rows, gain, key_grad)


def sum_kernel(count, transposed, *refs):
    lefts, rights, out_ref = refs[:count], refs[count : 2 * count], refs[2 * count]
    dot = dot_nt if transposed else dot_nn
    total = dot(lefts[0][...], rights[0][...])
    for left, right in zip(lefts[1:], rights[1:]):
        total += dot(left[...], right[...])
    out_ref[...] = total.astype(jnp.bfloat16)


def sum_of_products(rows, lefts, rights, transposed):
    def left_spec(place):
        _, depth, row_block, column_block = place
        return pl.BlockSpec(
            (rows, depth), lambda n: (row_block, column_block), pipeline_mode=pl.Buffered(1)
        )

    depth_total = sum(place[1] for place in lefts)
    if transposed:
        columns = rights[0].shape[0]
        block = min(256, columns)
        right_specs = [pl.BlockSpec((block, right.shape[1]), lambda n: (n, 0)) for right in rights]
    else:
        shards, _, part = rights[0].shape
        columns = shards * part
        block = min(256, part)
        per = part // block
        right_specs = [
            pl.BlockSpec((None, right.shape[1], block), lambda n: (n // per, 0, n % per))
            for right in rights
        ]
    return pl.pallas_call(
        functools.partial(sum_kernel, len(lefts), transposed),
        grid=(columns // block,),
        in_specs=[left_spec(place) for place in lefts] + right_specs,
        out_specs=pl.BlockSpec((rows, block), lambda n: (0, n)),
        out_shape=jax.ShapeDtypeStruct((rows, columns), jnp.bfloat16),
        compiler_params=params(),
        cost_estimate=cost(
            2 * rows * depth_total * columns,
            2 * depth_total * (rows + columns) + 2 * rows * columns,
        ),
        name="sum_of_products",
    )(*[place[0] for place in lefts], *rights)


def gradient_kernel(counts, *refs):
    out_ref = refs[-1]
    columns = 0
    parts = []
    at = 0
    for count in counts:
        lefts, rights = refs[at : at + count], refs[at + count : at + 2 * count]
        at += 2 * count
        total = dot_tn(lefts[0][...], rights[0][...])
        for left, right in zip(lefts[1:], rights[1:]):
            total += dot_tn(left[...], right[...])
        parts.append(total)
    for total in parts:
        span = slice(columns, columns + total.shape[1])
        for item in refs[at:-1]:
            total += item[:, span].astype(jnp.float32)
        out_ref[:, span] = total.astype(jnp.bfloat16)
        columns += total.shape[1]


def weight_gradient(rows, terms, arrived):
    def left_spec(row_block):
        return pl.BlockSpec((rows, block), lambda m: (row_block, m))

    def right_spec(size, row_block, column_block):
        return pl.BlockSpec(
            (rows, size), lambda m: (row_block, column_block), pipeline_mode=pl.Buffered(1)
        )

    width = terms[0][0][0][0].shape[1]
    block = min(512, width)
    total = sum(size for _, _, size in terms)
    out_spec = pl.BlockSpec((block, total), lambda m: (m, 0))
    specs, operands, work = [], [], 0
    for lefts, rights, size in terms:
        specs += [left_spec(place[1]) for place in lefts]
        specs += [right_spec(size, place[1], place[2]) for place in rights]
        operands += [place[0] for place in lefts] + [place[0] for place in rights]
        work += 2 * len(lefts) * rows * width * size
    return pl.pallas_call(
        functools.partial(gradient_kernel, [len(lefts) for lefts, _, _ in terms]),
        grid=(width // block,),
        in_specs=specs + [out_spec] * len(arrived),
        out_specs=out_spec,
        out_shape=jax.ShapeDtypeStruct((width, total), jnp.bfloat16),
        compiler_params=params(),
        cost_estimate=cost(work, 4 * width * total),
        name="weight_gradient",
    )(*operands, *arrived)


def split_dot_nt(left, rights):
    part = rights.shape[2]
    total = dot_nt(left[:, :part], rights[0])
    for index in range(1, rights.shape[0]):
        total += dot_nt(left[:, index * part : (index + 1) * part], rights[index])
    return total


def mlp_kernel(batches, down_in_ref, *refs):
    inputs = refs[:batches]
    pair_w, down_w, hidden_ref, pair_in_ref = refs[batches:]
    rows = inputs[0].shape[0]
    block = hidden_ref.shape[1]
    for index in range(batches):
        span = slice(index * rows, (index + 1) * rows)
        gate_pre = dot_nn(inputs[index][...], pair_w[:, :block])
        up_pre = dot_nn(inputs[index][...], pair_w[:, block:])
        grad_hidden = split_dot_nt(down_in_ref[span], down_w)
        sigmoid_gate = jax.nn.sigmoid(gate_pre)
        silu_gate = gate_pre * sigmoid_gate
        hidden_ref[span] = (silu_gate * up_pre).astype(jnp.bfloat16)
        pair_in_ref[span, block:] = (grad_hidden * silu_gate).astype(jnp.bfloat16)
        pair_in_ref[span, :block] = (
            grad_hidden * up_pre * sigmoid_gate * (1.0 + gate_pre * (1.0 - sigmoid_gate))
        ).astype(jnp.bfloat16)


def mlp_units(inputs, down_in, pair_w, down_w, block):
    rows, width = down_in.shape
    shards, units, part = down_w.shape
    return pl.pallas_call(
        functools.partial(mlp_kernel, len(inputs)),
        grid=(units // block,),
        in_specs=[whole_block(down_in.shape)]
        + [whole_block(item.shape) for item in inputs]
        + [
            pl.BlockSpec((width, 2 * block), lambda n: (0, n)),
            pl.BlockSpec((shards, block, part), lambda n: (0, n, 0)),
        ],
        out_specs=[
            pl.BlockSpec((rows, block), lambda n: (0, n)),
            pl.BlockSpec((rows, 2 * block), lambda n: (0, n)),
        ],
        out_shape=[
            jax.ShapeDtypeStruct((rows, units), jnp.bfloat16),
            jax.ShapeDtypeStruct((rows, 2 * units), jnp.bfloat16),
        ],
        compiler_params=params(),
        cost_estimate=cost(
            6 * rows * width * units, 4 * rows * width + 6 * width * units + 6 * rows * units
        ),
        name="mlp_units",
    )(down_in, *inputs, pair_w, down_w)


def add_norm_kernel(stream_ref, low_ref, other_ref, gain_ref, middle_ref, normed_ref):
    middle = (
        stream_ref[...].astype(jnp.float32)
        + (low_ref[...].astype(jnp.float32) + other_ref[...].astype(jnp.float32))
    )
    unit, _ = unit_of(middle)
    middle_ref[...] = middle
    normed_ref[...] = (unit * gain_ref[...]).astype(jnp.bfloat16)


def add_norm(index, stream, low_part, other_part, gain):
    rows, width = low_part.shape
    block = min(128, rows)
    first = index * (rows // block)
    spec = pl.BlockSpec((block, width), lambda m: (m, 0))
    return pl.pallas_call(
        add_norm_kernel,
        grid=(rows // block,),
        in_specs=[
            pl.BlockSpec((block, width), lambda m: (first + m, 0)),
            spec,
            spec,
            whole_block((1, width)),
        ],
        out_specs=[spec, spec],
        out_shape=[
            jax.ShapeDtypeStruct((rows, width), jnp.float32),
            jax.ShapeDtypeStruct((rows, width), jnp.bfloat16),
        ],
        compiler_params=params(),
        cost_estimate=cost(8 * rows * width, 12 * rows * width),
        name="add_norm",
    )(stream, low_part, other_part, gain)


def norm_back_kernel(values_ref, low_ref, other_ref, gain_ref, up_ref, *outs):
    grads = low_ref[...].astype(jnp.float32) + other_ref[...].astype(jnp.float32)
    gain_part, back = unit_back(values_ref[...].astype(jnp.float32), gain_ref[...], grads)
    total = up_ref[...].astype(jnp.float32) + back
    outs[0][...] = total.astype(jnp.bfloat16)
    for out_ref in outs[2:]:
        out_ref[...] = total

    @pl.when(pl.program_id(0) == 0)
    def _():
        outs[1][...] = jnp.zeros_like(outs[1])

    outs[1][0:1] += gain_part


def norm_back(values, values_at, low_part, other_part, gain, upstream, up_at, keep):
    rows, width = low_part.shape
    block = min(128, rows)
    steps = rows // block
    spec = pl.BlockSpec((block, width), lambda m: (m, 0))
    return pl.pallas_call(
        norm_back_kernel,
        grid=(steps,),
        in_specs=[
            pl.BlockSpec((block, width), lambda m: (values_at * steps + m, 0)),
            spec,
            spec,
            whole_block((1, width)),
            pl.BlockSpec((block, width), lambda m: (up_at * steps + m, 0)),
        ],
        out_specs=[spec, sum_block((8, width))] + [spec] * keep,
        out_shape=[
            jax.ShapeDtypeStruct((rows, width), jnp.bfloat16),
            jax.ShapeDtypeStruct((8, width), jnp.float32),
        ]
        + [jax.ShapeDtypeStruct((rows, width), jnp.float32)] * keep,
        compiler_params=params(),
        cost_estimate=cost(16 * rows * width, 16 * rows * width),
        name="norm_back",
    )(values, low_part, other_part, gain, upstream)


def order_kernel(per_quarter, turned, own_ref, *refs):
    pieces, out_ref = refs[:-1], refs[-1]
    step = pl.program_id(0)
    places = len(pieces) // per_quarter
    for index, piece in enumerate(pieces):

        @pl.when(step == index % places * per_quarter + index // places)
        def _(piece=piece):
            value = piece[...].astype(jnp.float32)
            out_ref[...] = value.T if turned else value


def in_order(chunks, block, column, turned=False):
    rows = chunks[0][0].shape[0]
    places, per_quarter = len(chunks[0]), len(chunks)
    own = lax.axis_index("replica").astype(jnp.int32).reshape(1)

    def out_of(step, own):
        place = step // per_quarter
        flip = jnp.where(place == 1, 2, jnp.where(place == 2, 1, place))
        at = jnp.bitwise_xor(own[0], flip) * per_quarter + step % per_quarter
        return (at, 0) if turned else (0, at)

    total = places * per_quarter * block
    pieces = [piece for chunk in chunks for piece in chunk]
    return pl.pallas_call(
        functools.partial(order_kernel, per_quarter, turned),
        grid_spec=pltpu.PrefetchScalarGridSpec(
            num_scalar_prefetch=1,
            grid=(places * per_quarter,),
            in_specs=[pl.BlockSpec((rows, block), lambda step, own: (0, column))] * len(pieces),
            out_specs=pl.BlockSpec((block, rows) if turned else (rows, block), out_of),
        ),
        out_shape=jax.ShapeDtypeStruct((total, rows) if turned else (rows, total), jnp.float32),
        compiler_params=params(),
        cost_estimate=cost(rows * total, 6 * rows * total),
        name="in_order",
    )(own, *pieces)


class Fold:
    def __init__(self, make_part, far, shards, far_end):
        self.make_part, self.far, self.shards = make_part, far, shards
        self.far_end = far_end

    def step3(self):
        self.from_third = across(self.make_part(3), 1)

    def step1(self):
        self.from_far = self.far.run(to_far, self.make_part(1, self.from_third))

    def step2(self):
        self.from_near = across(self.make_part(2), 1)

    def step0(self):
        total = self.make_part(0, self.from_near, self.from_far)
        self.shard = self.shards.run(scatter_rows, total)

    def end(self):
        return spread(self.shard, self.far_end)


def local(
    tokens,
    cotangent,
    lengths,
    parents,
    attn_gain,
    qk_gain,
    w_query,
    key_weight_matrix,
    value_weight_matrix,
    w_headgate,
    w_out,
    mlp_gain,
    w_gate,
    w_up,
    w_down,
):
    batches, rows, width = tokens.shape
    shards = lax.axis_size("fsdp")
    shard = lax.axis_index("fsdp")
    query_gain, key_gain = qk_gain[0, 0:1], qk_gain[0, 1:2]
    low = jnp.bfloat16

    query_piece = own_quarter(w_query[0], 1)
    head_piece = own_quarter(w_headgate[0], 1)
    per_kv = query_piece.shape[1] // LANES
    own = per_kv * LANES
    pad = jnp.zeros((query_piece.shape[0], LANES - head_piece.shape[1]), low)
    gate_piece, up_piece = own_quarter(w_gate[0], 1), own_quarter(w_up[0], 1)
    down_piece = own_quarter(w_down[0], 0)
    unit_block = min(256, gate_piece.shape[1])
    unit_blocks = gate_piece.shape[1] // unit_block
    def unit_span(value, block, axis):
        return lax.slice_in_dim(value, block * unit_block, (block + 1) * unit_block, axis=axis)

    far_in, far_out, far_end = Line(2), Line(2), Line(2)
    key_value_w = spread(
        gather_shards(
            jnp.concatenate(
                [own_quarter(key_weight_matrix[0], 1), own_quarter(value_weight_matrix[0], 1)],
                axis=1,
            ),
        ),
        far_in,
    )
    query_part = gather_shards(jnp.concatenate([query_piece, head_piece, pad], axis=1))
    out_part = gather_stacked(own_quarter(w_out[0], 0))
    groups = len(key_value_w)
    chunk_of = range(unit_blocks)

    tables, positions = [], []
    for index in range(batches):
        need, query_mask, key_mask, position = tree_need(
            lengths[index, 0], parents[index, 0], shard, rows, shards
        )
        tables.append((need, query_mask, key_mask))
        positions.append(position)
    half = LANES // 2
    frequency = THETA ** (-(jnp.arange(half, dtype=jnp.float32) * 2.0 / LANES))
    angle = jnp.concatenate(positions).astype(jnp.float32)[:, None] * frequency[None, :]
    cosine, sine = jnp.cos(angle), jnp.sin(angle)
    cos_rows = jnp.concatenate([cosine, cosine], axis=1)
    sin_rows = jnp.concatenate([-sine, sine], axis=1)

    core = Line(1)
    stream = tokens.reshape(batches * rows, width)
    down_in = cotangent.reshape(batches * rows, width)
    normed_low = (unit_of(stream.astype(jnp.float32))[0] * attn_gain).astype(low)
    key_value, key_raw = core.run(
        key_value_heads, normed_low, key_value_w, cos_rows, sin_rows, key_gain
    )
    query_w = spread(after(query_part, key_value), far_in)
    query_low, query_raw, gates = core.run(
        query_heads, normed_low, query_w, cos_rows, sin_rows, query_gain, per_kv
    )
    out_w = jnp.stack(spread(after(out_part, key_value), far_in))
    relays = [Relay(key_value[index * rows : (index + 1) * rows], shards) for index in range(batches)]
    for _ in range(1, shards):
        for index, relay in enumerate(relays):
            if index > 0:
                relay.hold(relays[index - 1].latest)
            relay.advance()
    blocks = [relay.blocks for relay in relays]
    tie = blocks[-1][min(GATHER_AFTER, shards - 1)]
    pair_w, down_w, pair_parts = [], [], []
    for chunk in chunk_of:
        piece = jnp.concatenate(
            [unit_span(gate_piece, chunk, 1), unit_span(up_piece, chunk, 1)], axis=1
        )
        pair_parts.append(gather_shards(after(piece, tie, query_low, out_part)))
    down_part = gather_stacked(after(down_piece, tie, query_low, out_part))
    pair_parts[0] = after(pair_parts[0], blocks[0][-1])
    pair_w.append(spread(pair_parts[0], far_in))
    mixed, attended, logs, middle, mlp_low, parts = [], [], [], [], [], []
    for index in range(batches):
        tree_mixed, tree_out, tree_log = core.run(
            lambda query: attend_forward(
                index, batches, tables[index], query, gates, blocks[index], per_kv
            ),
            query_low,
        )
        mixed.append(tree_mixed)
        attended.append(tree_out)
        logs.append(tree_log)
        if index == 0:
            down_part = after(down_part, tree_mixed)
            for chunk in chunk_of:
                down_w.append(spread(unit_span(down_part, chunk, 1), far_in))
            for part in pair_parts[1:]:
                pair_w.append(spread(after(part, tree_mixed), far_in))
        core.hold((pair_w if index == 0 else down_w)[0][1])
        part = core.run(
            lambda left: sum_of_products(
                rows,
                [(left, own, 0, k) for k in range(groups)],
                [out_w[k] for k in range(groups)],
                False,
            ),
            tree_mixed,
        )
        parts.append((part, tensor_other(part)))
    for index in range(batches):
        core.hold(down_w[min(index + 1, unit_blocks - 1)][1])
        tree_middle, tree_normed = core.run(
            lambda part: add_norm(index, stream, part, parts[index][1], mlp_gain), parts[index][0]
        )
        middle.append(tree_middle)
        mlp_low.append(tree_normed)

    hidden = [[None] * groups for _ in chunk_of]
    pair_in = [[None] * groups for _ in chunk_of]

    def do_units(chunk, members):
        for k in members:
            hidden[chunk][k], pair_in[chunk][k] = core.run(
                lambda upstream: mlp_units(
                    mlp_low, upstream, pair_w[chunk][k], down_w[chunk][k], unit_block
                ),
                down_in,
            )

    shard_line = Line(99)

    def fold(terms_of):
        def make_part(k, *arrived):
            def work(first):
                terms = terms_of(k)
                lefts, rights, size = terms[0]
                lefts = [(first,) + lefts[0][1:]] + lefts[1:]
                return weight_gradient(rows, [(lefts, rights, size)] + terms[1:], arrived)

            return core.run(work, terms_of(k)[0][0][0][0])

        return Fold(make_part, far_out, shard_line, far_end)

    def both(value, column=0):
        return [(value, index, column) for index in range(batches)]

    def apart(values, column=0):
        return [(value, 0, column) for value in values]

    unit_folds = [
        fold(
            lambda k, c=c: [
                (apart(mlp_low), both(pair_in[c][k]), 2 * unit_block),
                (both(down_in), both(hidden[c][k]), unit_block),
            ]
        )
        for c in chunk_of
    ]

    middle_parts = []

    def do_middle_part(index):
        part = core.run(
            lambda left: sum_of_products(
                rows,
                [
                    (left if (c, k) == (0, 0) else pair_in[c][k], 2 * unit_block, index, 0)
                    for c in chunk_of
                    for k in range(groups)
                ],
                [pair_w[c][k] for c in chunk_of for k in range(groups)],
                True,
            ),
            pair_in[0][0],
        )
        middle_parts.append((part, tensor_other(part)))

    mlp_gain_grad, grad_middle, out_in = [], [], []
    query_in, query_gain_grad, key_grads = [], [], []

    def do_norm_back(index):
        low_out, gain_part, full = core.run(
            lambda part: norm_back(
                middle[index], 0, part, middle_parts[index][1], mlp_gain, down_in, index, 1
            ),
            middle_parts[index][0],
        )
        out_in.append(low_out)
        mlp_gain_grad.append(gain_part)
        grad_middle.append(full)

    def do_attention_back(index):
        tree_in, gain_part, *grads = core.run(
            lambda upstream: attend_backward(
                index,
                batches,
                tables[index],
                upstream,
                out_w,
                query_low,
                gates,
                logs[index],
                attended[index],
                query_raw,
                cos_rows,
                sin_rows,
                query_gain,
                blocks[index],
                per_kv,
            ),
            out_in[index],
        )
        query_in.append(tree_in)
        query_gain_grad.append(gain_part)
        key_grads.append(relay_back(grads, shards))

    result_parts = []

    def do_result_part(index):
        part = core.run(
            lambda left: sum_of_products(
                rows,
                [
                    (left if (c, k) == (0, 0) else hidden[c][k], unit_block, index, 0)
                    for c in chunk_of
                    for k in range(groups)
                ],
                [down_w[c][k] for c in chunk_of for k in range(groups)],
                False,
            ),
            hidden[0][0],
        )
        result_parts.append((part, tensor_other(part)))

    final = unit_blocks - 1
    for chunk in chunk_of:
        do_units(chunk, (0, 2, 1, 3))
        if chunk < final:
            core.hold(pair_w[chunk + 1][1])
        if chunk > 0:
            unit_folds[chunk - 1].step1()
        unit_folds[chunk].step3()
        unit_folds[chunk].step2()
    do_middle_part(0)
    for chunk in range(0, final - 1):
        unit_folds[chunk].step0()
    unit_folds[final].step1()
    for index in range(1, batches):
        do_middle_part(index)
    do_norm_back(0)
    if final > 0:
        core.hold(unit_folds[final - 1].from_far)
    do_attention_back(0)
    core.hold(unit_folds[final].from_far)
    for index in range(1, batches):
        do_norm_back(index)
    do_result_part(0)
    if final > 0:
        unit_folds[final - 1].step0()
    unit_folds[final].step0()
    for index in range(1, batches):
        do_result_part(index)
    unit_ends = [unit_folds[0].end()]
    core.hold(key_grads[0][0], unit_ends[0][1], unit_ends[0][3])
    for index in range(1, batches):
        do_attention_back(index)
    query_block = own + LANES
    wide_fold = fold(
        lambda k: [
            (apart(out_in), apart(mixed, k), own),
            (both(normed_low), apart(query_in, k), query_block),
        ]
    )
    core.hold(*[part[1] for part in result_parts])
    wide_fold.step3()
    wide_fold.step2()
    wide_fold.step1()
    key_block = 2 * LANES
    key_in, key_gain_grad, stream_parts = [], [], []

    def do_key_back(index):
        tree_in, gain_part = core.run(
            lambda raw: key_back(index, raw, cos_rows, sin_rows, key_gain, key_grads[index][-1]),
            key_raw,
        )
        key_in.append(tree_in)
        key_gain_grad.append(gain_part)

    def do_stream_part(index):
        part = core.run(
            lambda left: sum_of_products(
                rows,
                [(query_in[index], query_block, 0, k) for k in range(groups)]
                + [(left, key_block, 0, k) for k in range(groups)],
                query_w + key_value_w,
                True,
            ),
            key_in[index],
        )
        stream_parts.append((part, tensor_other(part)))

    attn_gain_grad, input_grad = [], []

    def do_stream_back(index):
        part, other = stream_parts[index]
        low_out, gain_part = core.run(
            lambda part: norm_back(
                stream, index, part, other, attn_gain, grad_middle[index], 0, 0
            ),
            part,
        )
        input_grad.append(low_out)
        attn_gain_grad.append(gain_part)

    do_key_back(0)
    unit_ends += [item.end() for item in unit_folds[1:]]
    for pieces in unit_ends[1:]:
        core.hold(pieces[1], pieces[3])
    do_stream_part(0)
    core.hold(key_grads[-1][min(1, shards - 2)])

    def do_order(column):
        return core.run(
            lambda first: in_order(
                [[first] + unit_ends[0][1:]] + unit_ends[1:], unit_block, column, column == 2
            ),
            unit_ends[0][0],
        )

    gate_order = do_order(0)
    for index in range(1, batches):
        do_key_back(index)
    key_fold = fold(lambda k: [(both(normed_low), apart(key_in, k), key_block)])
    key_fold.step3()
    key_fold.step2()
    for index in range(1, batches):
        do_stream_part(index)
    key_fold.step1()
    wide_fold.step0()
    core.hold(stream_parts[0][1])
    up_order = do_order(1)
    do_stream_back(0)
    key_fold.step0()
    down_order = do_order(2)
    for index in range(1, batches):
        do_stream_back(index)
    results = [
        (
            middle[index]
            + (part.astype(jnp.float32) + other.astype(jnp.float32))
        ).astype(low)
        for index, (part, other) in enumerate(result_parts)
    ]
    wide_shards = wide_fold.end()
    key_shards = key_fold.end()
    query_sum, key_sum = [
        jnp.sum(jnp.stack(items), axis=0)[0] for items in (query_gain_grad, key_gain_grad)
    ]
    wide_sums = [
        jnp.sum(jnp.stack(items), axis=0)[0] for items in (attn_gain_grad, mlp_gain_grad)
    ]
    gain_sum = axis_sum(
        axis_sum(jnp.concatenate(wide_sums + [query_sum, key_sum]), "replica"), "fsdp"
    )
    head_sum = axis_sum(gain_sum[2 * width :], "tensor")

    def own_slice(value, axis):
        size = value.shape[axis] // shards
        return lax.dynamic_slice_in_dim(value, shard * size, size, axis)[None]

    gate_count = head_piece.shape[1]
    gate_grad = in_order([wide_shards], LANES, 2 * per_kv)
    gate_grad = gate_grad.reshape(gate_grad.shape[0], groups, LANES)[:, :, :gate_count]
    return (
        jnp.stack(results),
        jnp.stack(input_grad),
        own_slice(gain_sum[:width], 0),
        own_slice(head_sum.reshape(2, LANES), 1),
        in_order([wide_shards], own, 1)[None],
        in_order([key_shards], LANES, 0)[None],
        in_order([key_shards], LANES, 1)[None],
        gate_grad.reshape(1, gate_grad.shape[0], groups * gate_count),
        in_order([wide_shards], own, 0, turned=True)[None],
        own_slice(gain_sum[width : 2 * width], 0),
        gate_order[None],
        up_order[None],
        down_order[None],
    )


def solution(mesh):
    placed = (
        P(None, ("replica", "fsdp"), None),
        P(None, ("replica", "fsdp"), None),
        P(None, "replica", None),
        P(None, "replica", None),
        P(),
        P(),
        P(None, "fsdp", "tensor"),
        P(None, "fsdp", "tensor"),
        P(None, "fsdp", "tensor"),
        P(None, "fsdp", "tensor"),
        P(None, "tensor", "fsdp"),
        P(),
        P(None, "fsdp", "tensor"),
        P(None, "fsdp", "tensor"),
        P(None, "tensor", "fsdp"),
    )
    return jax.shard_map(
        local,
        mesh=mesh,
        in_specs=placed,
        out_specs=(
            P(None, ("replica", "fsdp"), None),
            P(None, ("replica", "fsdp"), None),
            P(None, "fsdp"),
            P(None, None, "fsdp"),
            P(None, "fsdp", "tensor"),
            P(None, "fsdp", "tensor"),
            P(None, "fsdp", "tensor"),
            P(None, "fsdp", "tensor"),
            P(None, "tensor", "fsdp"),
            P(None, "fsdp"),
            P(None, "fsdp", "tensor"),
            P(None, "fsdp", "tensor"),
            P(None, "tensor", "fsdp"),
        ),
        check_vma=False,
    )
```

```python
import functools

import jax
import jax.numpy as jnp
from jax import lax
from jax.experimental import pallas as pl
from jax.experimental.pallas import tpu as pltpu
from jax.sharding import PartitionSpec as P

EPSILON = 1e-06
THETA = 1000000.0
LOG2_E = 1.4426950408889634
LANES = 128
EXTRA_AT = 16
VMEM_BYTES = 58 * 1024 * 1024
COST_SHARE = 0.22


def segment_table(lengths, parents):
    count = lengths.shape[0]
    starts = jnp.cumsum(lengths) - lengths
    labels = jnp.arange(count, dtype=jnp.int32)
    parent_hot = (parents[:, None] == labels[None, :]).astype(jnp.int32)
    grand_hot = jnp.dot(parent_hot, parent_hot)
    eye_hot = (labels[:, None] == labels[None, :]).astype(jnp.int32)
    ancestor = (eye_hot + parent_hot + grand_hot > 0).astype(jnp.int32)
    before = jnp.sum(ancestor * (1 - eye_hot) * lengths[None, :], axis=1)
    return (starts, before - starts, ancestor)


def row_segments(indices, starts, count):
    labels = jnp.arange(count, dtype=jnp.int32)
    member = jnp.sum((indices[:, None] >= starts[None, :]).astype(jnp.int32), axis=1) - 1
    return (member[:, None] == labels[None, :]).astype(jnp.int32)


def swaps(bit, count):
    return [(index, index ^ bit) for index in range(count)]


def across(value, bit):
    return lax.ppermute(value, "replica", swaps(bit, lax.axis_size("replica")))


def own_quarter(shard, axis):
    size = shard.shape[axis] // lax.axis_size("replica")
    return lax.dynamic_slice_in_dim(shard, lax.axis_index("replica") * size, size, axis)


def spread(block):
    other = across(block, 2)
    return [block, other, across(block, 1), across(other, 1)]


def after(value, *earlier):
    return lax.optimization_barrier((value, *earlier))[0] if earlier else value


class Line:
    def __init__(self, depth):
        self.depth = depth
        self.sent = []
        self.held = []

    def before(self):
        last = [self.sent[-self.depth]] if len(self.sent) >= self.depth else []
        held, self.held = self.held, []
        return last + held

    def hold(self, *values):
        self.held += values

    def run(self, function, value, *rest):
        result = function(after(value, *self.before()), *rest)
        self.sent.append(result[0] if isinstance(result, (list, tuple)) else result)
        return result


def gather_shards(value):
    return lax.all_gather(value, "fsdp", axis=0, tiled=True)


def gather_stacked(value):
    return lax.all_gather(value, "fsdp", axis=0, tiled=False)


def scatter_rows(value):
    return lax.psum_scatter(value, "fsdp", scatter_dimension=0, tiled=True)


def to_far(value):
    return across(value, 2)


def spread(block, far_line):
    other = far_line.run(to_far, block)
    return [block, other, across(block, 1), across(other, 1)]


def axis_sum(value, axis):
    size, bit = lax.axis_size(axis), 1
    while bit < size:
        if bit * 4 <= size:
            near, far, both = [
                lax.ppermute(value, axis, swaps(bit * flip, size)) for flip in (1, 2, 3)
            ]
            value, bit = (value + near) + (far + both), bit * 4
        else:
            value, bit = value + lax.ppermute(value, axis, swaps(bit, size)), bit * 2
    return value


def tensor_other(low_part):
    return lax.ppermute(low_part, "tensor", swaps(1, lax.axis_size("tensor")))


class Relay:
    def __init__(self, block, count):
        self.blocks, self.count, self.held = [block], count, []
        self.latest = block

    def hold(self, *values):
        self.held += values

    def advance(self):
        if len(self.blocks) < self.count:
            value = after(self.blocks[-1], *self.held) if self.held else self.blocks[-1]
            self.held = []
            pairs = [(index, index + 1) for index in range(self.count - 1)]
            self.blocks.append(lax.ppermute(value, "fsdp", pairs))
            self.latest = self.blocks[-1]


def params():
    return pltpu.CompilerParams(vmem_limit_bytes=VMEM_BYTES)


def cost(flops, moved, rate=0.56):
    return pl.CostEstimate(
        flops=int(flops * COST_SHARE / rate),
        bytes_accessed=int(moved * COST_SHARE / 0.6),
        transcendentals=0,
    )


def whole_block(shape):
    return pl.BlockSpec(shape, lambda *index: (0,) * len(shape), pipeline_mode=pl.Buffered(1))


def sum_block(shape):
    return pl.BlockSpec(shape, lambda *index: (0,) * len(shape))


def dot_nn(left, right):
    return jnp.dot(left, right, preferred_element_type=jnp.float32)


def dot_nt(left, right):
    return lax.dot_general(
        left, right, (((1,), (1,)), ((), ())), preferred_element_type=jnp.float32
    )


def dot_tn(left, right):
    return lax.dot_general(
        left, right, (((0,), (0,)), ((), ())), preferred_element_type=jnp.float32
    )


def three_parts(value):
    first = value.astype(jnp.bfloat16)
    rest = value - first.astype(jnp.float32)
    second = rest.astype(jnp.bfloat16)
    third = (rest - second.astype(jnp.float32)).astype(jnp.bfloat16)
    return (first, second, third)


def put_lanes(base, parts):
    lane = lax.broadcasted_iota(jnp.int32, base.shape, 1)
    value = base.astype(jnp.float32)
    for offset, part in enumerate(parts):
        value = jnp.where(lane == EXTRA_AT + offset, part.astype(jnp.float32), value)
    return value.astype(jnp.bfloat16)


def rope(values, cos_rows, sin_rows):
    return values * cos_rows + pltpu.roll(values, LANES // 2, 1) * sin_rows


def rope_back(grads, cos_rows, sin_rows):
    return grads * cos_rows - pltpu.roll(grads, LANES // 2, 1) * sin_rows


def unit_of(raw):
    inverse = lax.rsqrt(jnp.mean(raw * raw, axis=-1, keepdims=True) + EPSILON)
    return (raw * inverse, inverse)


def unit_back(raw, gain, grads):
    unit, inverse = unit_of(raw)
    scaled = grads * gain
    gain_part = jnp.sum(grads * unit, axis=0, keepdims=True)
    return (
        gain_part,
        inverse * (scaled - unit * jnp.mean(scaled * unit, axis=-1, keepdims=True)),
    )


def key_value_kernel(groups, x_ref, cos_ref, sin_ref, gain_ref, *refs):
    weights, (kv_ref, raw_ref) = refs[:groups], refs[groups:]
    for k in range(groups):
        part = dot_nn(x_ref[...], weights[k][...])
        raw = part[:, :LANES]
        unit, _ = unit_of(raw)
        raw_ref[:, k * LANES : (k + 1) * LANES] = raw
        kv_ref[:, k * LANES : (k + 1) * LANES] = rope(
            unit * gain_ref[...], cos_ref[...], sin_ref[...]
        ).astype(jnp.bfloat16)
        at = (groups + k) * LANES
        kv_ref[:, at : at + LANES] = part[:, LANES:].astype(jnp.bfloat16)


def key_value_heads(normed_low, weights, cos_rows, sin_rows, gain):
    rows, width = normed_low.shape
    groups, block = len(weights), min(256, rows)
    return pl.pallas_call(
        functools.partial(key_value_kernel, groups),
        grid=(rows // block,),
        in_specs=[
            pl.BlockSpec((block, width), lambda m: (m, 0)),
            pl.BlockSpec((block, LANES), lambda m: (m, 0)),
            pl.BlockSpec((block, LANES), lambda m: (m, 0)),
            whole_block((1, LANES)),
        ]
        + [whole_block(weight.shape) for weight in weights],
        out_specs=[
            pl.BlockSpec((block, 2 * groups * LANES), lambda m: (m, 0)),
            pl.BlockSpec((block, groups * LANES), lambda m: (m, 0)),
        ],
        out_shape=[
            jax.ShapeDtypeStruct((rows, 2 * groups * LANES), jnp.bfloat16),
            jax.ShapeDtypeStruct((rows, groups * LANES), jnp.float32),
        ],
        compiler_params=params(),
        cost_estimate=cost(4 * rows * width * groups * LANES, 4 * rows * width),
        name="key_value_heads",
    )(normed_low, cos_rows, sin_rows, gain, *weights)


def query_kernel(groups, per_kv, x_ref, cos_ref, sin_ref, gain_ref, *refs):
    weights, (low_ref, raw_ref, gate_ref) = refs[:groups], refs[groups:]
    for k in range(groups):
        part = dot_nn(x_ref[...], weights[k][...])
        for head in range(per_kv):
            raw = part[:, head * LANES : (head + 1) * LANES]
            unit, _ = unit_of(raw)
            at = (k * per_kv + head) * LANES
            raw_ref[:, at : at + LANES] = raw
            low_ref[:, at : at + LANES] = rope(
                unit * gain_ref[...], cos_ref[...], sin_ref[...]
            ).astype(jnp.bfloat16)
        gate_ref[k] = jax.nn.sigmoid(part[:, per_kv * LANES :])


def query_heads(normed_low, weights, cos_rows, sin_rows, gain, per_kv):
    rows, width = normed_low.shape
    groups, block = len(weights), min(256, rows)
    wide = groups * per_kv * LANES
    return pl.pallas_call(
        functools.partial(query_kernel, groups, per_kv),
        grid=(rows // block,),
        in_specs=[
            pl.BlockSpec((block, width), lambda m: (m, 0)),
            pl.BlockSpec((block, LANES), lambda m: (m, 0)),
            pl.BlockSpec((block, LANES), lambda m: (m, 0)),
            whole_block((1, LANES)),
        ]
        + [whole_block(weight.shape) for weight in weights],
        out_specs=[
            pl.BlockSpec((block, wide), lambda m: (m, 0)),
            pl.BlockSpec((block, wide), lambda m: (m, 0)),
            pl.BlockSpec((groups, block, LANES), lambda m: (0, m, 0)),
        ],
        out_shape=[
            jax.ShapeDtypeStruct((rows, wide), jnp.bfloat16),
            jax.ShapeDtypeStruct((rows, wide), jnp.float32),
            jax.ShapeDtypeStruct((groups, rows, LANES), jnp.float32),
        ],
        compiler_params=params(),
        cost_estimate=cost(2 * rows * width * groups * (per_kv + 1) * LANES, 4 * rows * width),
        name="query_heads",
    )(normed_low, cos_rows, sin_rows, gain, *weights)


def tiles_of(row_count):
    block = min(256, row_count)
    return (block, row_count // block)


def tree_need(lengths, parents, shard, row_count, shards):
    count = lengths.shape[0]
    starts, offsets, ancestor = segment_table(lengths, parents)
    block, tiles = tiles_of(row_count)
    query_index = shard * row_count + jnp.arange(row_count, dtype=jnp.int32)
    query_hot = row_segments(query_index, starts, count)
    reach = jnp.sum(query_hot[:, :, None] * ancestor[None, :, :], axis=1)
    position = query_index + jnp.sum(query_hot * offsets[None, :], axis=1)
    back = jnp.arange(shards, dtype=jnp.int32)[:, None]
    key_index = (shard - back) * row_count + jnp.arange(row_count, dtype=jnp.int32)[None, :]
    key_hot = row_segments(key_index.reshape(-1), starts, count)
    query_has = jnp.max(reach.reshape(tiles, block, count), axis=1)
    key_has = jnp.max(key_hot.reshape(shards, tiles, block, count), axis=2)
    need = jnp.sum(query_has[:, None, None, :] * key_has[None], axis=-1) > 0
    wall = jnp.where(reach > 0, 0.0, -1e30)
    query_mask = jnp.pad(wall, ((0, 0), (0, LANES - count))).astype(jnp.bfloat16)
    lane = jnp.arange(LANES)[None, :]
    ones = ((lane >= EXTRA_AT) & (lane < EXTRA_AT + 3)).astype(jnp.float32)
    key_mask = jnp.pad(key_hot.astype(jnp.float32), ((0, 0), (0, LANES - count))) + ones
    return (need.astype(jnp.int32).reshape(-1), query_mask, key_mask.astype(jnp.bfloat16), position)


def forward_kernel(
    shards, per_kv, factor, need_ref, q_ref, qmask_ref, gate_ref, kmask_ref, *refs
):
    keys, values = refs[:shards], refs[shards : 2 * shards]
    mixed_ref, attended_ref, log_ref, total_ref = refs[-4:]
    rows = q_ref.shape[0]
    block, tiles = tiles_of(rows)
    lane = lax.broadcasted_iota(jnp.int32, (block, LANES), 1)
    for qi in range(tiles):
        span = slice(qi * block, (qi + 1) * block)
        total_ref[...] = jnp.zeros_like(total_ref)
        for shard in range(shards):
            for ci in range(tiles):
                if shard == 0 and ci > qi:
                    continue
                part = slice(ci * block, (ci + 1) * block)

                @pl.when(need_ref[(qi * shards + shard) * tiles + ci] > 0)
                def _(shard=shard, ci=ci, part=part):
                    at = shard * rows + ci * block
                    key_mask = kmask_ref[at : at + block]
                    key_wide = jnp.concatenate([keys[shard][part], key_mask], axis=1)
                    value_wide = jnp.concatenate(
                        [values[shard][part], jnp.ones((block, LANES), jnp.bfloat16)], axis=1
                    )
                    for head in range(per_kv):
                        query_wide = jnp.concatenate(
                            [q_ref[span, head * LANES : (head + 1) * LANES], qmask_ref[span]],
                            axis=1,
                        )
                        scores = dot_nt(query_wide, key_wide)
                        if shard == 0 and ci == qi:
                            row = lax.broadcasted_iota(jnp.int32, (block, block), 0)
                            column = lax.broadcasted_iota(jnp.int32, (block, block), 1)
                            scores = jnp.where(column <= row, scores, -1e30)
                        weights = jnp.exp2(scores * factor).astype(jnp.bfloat16)
                        total_ref[head] += dot_nn(weights, value_wide)

        logs = jnp.zeros((block, LANES), jnp.float32)
        for head in range(per_kv):
            summed = total_ref[head][:, LANES:]
            tree_out = total_ref[head][:, :LANES] / summed
            columns = slice(head * LANES, (head + 1) * LANES)
            attended_ref[span, columns] = tree_out
            gate = gate_ref[0, span, head : head + 1]
            mixed_ref[span, columns] = (gate * tree_out).astype(jnp.bfloat16)
            logs = jnp.where(lane == head, jnp.log(summed), logs)
        log_ref[0, span] = logs


def attend_forward(index, batches, tables, query_low, gates, blocks, per_kv):
    need, query_mask, key_mask = tables
    all_rows, wide = query_low.shape
    rows = all_rows // batches
    shards = len(blocks)
    groups = wide // (per_kv * LANES)
    own = per_kv * LANES
    block, _ = tiles_of(rows)
    tree_spec = pl.BlockSpec((rows, own), lambda g, need: (0, g))
    log_spec = pl.BlockSpec((1, rows, LANES), lambda g, need: (g, 0, 0))
    return pl.pallas_call(
        functools.partial(forward_kernel, shards, per_kv, LANES ** (-0.5) * LOG2_E),
        grid_spec=pltpu.PrefetchScalarGridSpec(
            num_scalar_prefetch=1,
            grid=(groups,),
            in_specs=[
                pl.BlockSpec((rows, own), lambda g, need: (index, g)),
                whole_block(query_mask.shape),
                pl.BlockSpec((1, rows, LANES), lambda g, need: (g, index, 0)),
                whole_block(key_mask.shape),
            ]
            + [pl.BlockSpec((rows, LANES), lambda g, need: (0, g))] * shards
            + [pl.BlockSpec((rows, LANES), lambda g, need: (0, groups + g))] * shards,
            out_specs=[tree_spec, tree_spec, log_spec],
            scratch_shapes=[pltpu.VMEM((per_kv, block, 2 * LANES), jnp.float32)],
        ),
        out_shape=[
            jax.ShapeDtypeStruct((rows, wide), jnp.bfloat16),
            jax.ShapeDtypeStruct((rows, wide), jnp.float32),
            jax.ShapeDtypeStruct((groups, rows, LANES), jnp.float32),
        ],
        compiler_params=params(),
        cost_estimate=cost(
            4 * rows * rows * shards * wide,
            8 * rows * wide + 2 * shards * rows * wide,
            0.19,
        ),
        name="attend_forward",
    )(need, query_low, query_mask, gates, key_mask, *blocks, *blocks)


def backward_kernel(
    shards,
    per_kv,
    need_ref,
    out_in_ref,
    w_out_ref,
    q_ref,
    qmask_ref,
    gate_ref,
    kmask_ref,
    log_ref,
    attended_ref,
    raw_ref,
    cos_ref,
    sin_ref,
    gain_ref,
    *refs,
):
    scale = LANES ** (-0.5)
    factor = scale * LOG2_E
    keys, values = refs[:shards], refs[shards : 2 * shards]
    query_in_ref, gain_grad_ref = refs[2 * shards : 2 * shards + 2]
    block_grads = refs[2 * shards + 2 : 3 * shards + 2]
    dq_ref, dk_ref, dv_ref, qwide_ref, dwide_ref = refs[3 * shards + 2 :]
    rows = q_ref.shape[0]
    block, tiles = tiles_of(rows)
    grad_mixed = split_dot_nt(out_in_ref[...], w_out_ref)
    lane = lax.broadcasted_iota(jnp.int32, (rows, LANES), 1)
    logits = jnp.zeros((rows, LANES), jnp.float32)
    for head in range(per_kv):
        columns = slice(head * LANES, (head + 1) * LANES)
        attended = attended_ref[:, columns]
        gate = gate_ref[0, :, head : head + 1]
        mixed_grad = grad_mixed[:, columns]
        logit = jnp.sum(mixed_grad * attended, axis=-1, keepdims=True) * gate * (1.0 - gate)
        logits = jnp.where(lane == head, logit, logits)
        attended_in = (mixed_grad * gate).astype(jnp.bfloat16)
        delta = jnp.sum(attended_in.astype(jnp.float32) * attended, axis=-1, keepdims=True)
        dwide_ref[head, :, :LANES] = attended_in
        dwide_ref[head, :, LANES:] = put_lanes(
            jnp.zeros((rows, LANES), jnp.bfloat16), three_parts(-delta)
        )
        qwide_ref[head, :, :LANES] = q_ref[:, columns]
        qwide_ref[head, :, LANES:] = put_lanes(
            qmask_ref[...], three_parts(log_ref[0, :, head : head + 1] * (-1.0 / scale))
        )
    query_in_ref[:, per_kv * LANES :] = logits.astype(jnp.bfloat16)
    dq_ref[...] = jnp.zeros_like(dq_ref)
    for shard in range(shards):
        for ci in range(tiles):
            part = slice(ci * block, (ci + 1) * block)
            at = shard * rows + ci * block
            dk_ref[...] = jnp.zeros_like(dk_ref)
            dv_ref[...] = jnp.zeros_like(dv_ref)
            for qi in range(tiles):
                if shard == 0 and ci > qi:
                    continue
                span = slice(qi * block, (qi + 1) * block)

                @pl.when(need_ref[(qi * shards + shard) * tiles + ci] > 0)
                def _(shard=shard, ci=ci, qi=qi, at=at, part=part, span=span):
                    key_low = keys[shard][part]
                    key_mask = kmask_ref[at : at + block]
                    key_wide = jnp.concatenate([key_low, key_mask], axis=1)
                    value_wide = jnp.concatenate([values[shard][part], key_mask], axis=1)
                    for head in range(per_kv):
                        scores = dot_nt(key_wide, qwide_ref[head, span])
                        if shard == 0 and ci == qi:
                            row = lax.broadcasted_iota(jnp.int32, (block, block), 0)
                            column = lax.broadcasted_iota(jnp.int32, (block, block), 1)
                            scores = jnp.where(row <= column, scores, -1e30)
                        weights = jnp.exp2(scores * factor)
                        change = dot_nt(value_wide, dwide_ref[head, span])
                        grad_scores = (weights * change).astype(jnp.bfloat16)
                        weights = weights.astype(jnp.bfloat16)
                        dv_ref[...] += dot_nn(weights, dwide_ref[head, span, :LANES])
                        dk_ref[...] += dot_nn(grad_scores, qwide_ref[head, span, :LANES])
                        dq_ref[head, span] += dot_tn(grad_scores, key_low)

            block_grads[shard][0, part] = (dk_ref[...] * scale).astype(jnp.bfloat16)
            block_grads[shard][1, part] = dv_ref[...].astype(jnp.bfloat16)
    gain_total = jnp.zeros((1, LANES), jnp.float32)
    for head in range(per_kv):
        columns = slice(head * LANES, (head + 1) * LANES)
        grads = rope_back(dq_ref[head] * scale, cos_ref[...], sin_ref[...])
        gain_part, query_grad = unit_back(raw_ref[:, columns], gain_ref[...], grads)
        gain_total += gain_part
        query_in_ref[:, columns] = query_grad.astype(jnp.bfloat16)

    @pl.when(pl.program_id(0) == 0)
    def _():
        gain_grad_ref[...] = jnp.zeros_like(gain_grad_ref)

    gain_grad_ref[0:1] += gain_total


def attend_backward(
    index,
    batches,
    tables,
    out_in,
    w_out,
    query_low,
    gates,
    logs,
    attended,
    query_raw,
    cos_rows,
    sin_rows,
    gain,
    blocks,
    per_kv,
):
    need, query_mask, key_mask = tables
    all_rows, wide = query_low.shape
    rows = all_rows // batches
    shards = len(blocks)
    groups = wide // (per_kv * LANES)
    own = per_kv * LANES
    block, _ = tiles_of(rows)
    merged_spec = pl.BlockSpec((rows, own), lambda g, need: (index, g))
    table_spec = pl.BlockSpec((rows, LANES), lambda g, need: (index, 0))
    return pl.pallas_call(
        functools.partial(backward_kernel, shards, per_kv),
        grid_spec=pltpu.PrefetchScalarGridSpec(
            num_scalar_prefetch=1,
            grid=(groups,),
            in_specs=[
                whole_block(out_in.shape),
                pl.BlockSpec((None,) + w_out.shape[1:], lambda g, need: (g, 0, 0, 0)),
                merged_spec,
                whole_block(query_mask.shape),
                pl.BlockSpec((1, rows, LANES), lambda g, need: (g, index, 0)),
                whole_block(key_mask.shape),
                pl.BlockSpec((1, rows, LANES), lambda g, need: (g, 0, 0)),
                pl.BlockSpec((rows, own), lambda g, need: (0, g)),
                merged_spec,
                table_spec,
                table_spec,
                whole_block((1, LANES)),
            ]
            + [pl.BlockSpec((rows, LANES), lambda g, need: (0, g))] * shards
            + [pl.BlockSpec((rows, LANES), lambda g, need: (0, groups + g))] * shards,
            out_specs=[
                pl.BlockSpec((rows, own + LANES), lambda g, need: (0, g)),
                sum_block((8, LANES)),
            ]
            + [pl.BlockSpec((2, rows, LANES), lambda g, need: (0, 0, g))] * shards,
            scratch_shapes=[
                pltpu.VMEM((per_kv, rows, LANES), jnp.float32),
                pltpu.VMEM((block, LANES), jnp.float32),
                pltpu.VMEM((block, LANES), jnp.float32),
                pltpu.VMEM((per_kv, rows, 2 * LANES), jnp.bfloat16),
                pltpu.VMEM((per_kv, rows, 2 * LANES), jnp.bfloat16),
            ],
        ),
        out_shape=[
            jax.ShapeDtypeStruct((rows, groups * (own + LANES)), jnp.bfloat16),
            jax.ShapeDtypeStruct((8, LANES), jnp.float32),
        ]
        + [jax.ShapeDtypeStruct((2, rows, groups * LANES), jnp.bfloat16)] * shards,
        compiler_params=params(),
        cost_estimate=cost(
            14 * rows * rows * shards * wide,
            20 * rows * wide + 4 * shards * rows * wide,
            0.21,
        ),
        name="attend_backward",
    )(
        need,
        out_in,
        w_out,
        query_low,
        query_mask,
        gates,
        key_mask,
        logs,
        attended,
        query_raw,
        cos_rows,
        sin_rows,
        gain,
        *blocks,
        *blocks,
    )


def key_back_kernel(groups, raw_ref, cos_ref, sin_ref, gain_ref, grads_ref, out_ref, gain_grad_ref):
    gain_total = jnp.zeros((1, LANES), jnp.float32)
    for k in range(groups):
        columns = slice(k * LANES, (k + 1) * LANES)
        grads = rope_back(grads_ref[0, :, columns].astype(jnp.float32), cos_ref[...], sin_ref[...])
        gain_part, key_grad = unit_back(raw_ref[:, columns], gain_ref[...], grads)
        gain_total += gain_part
        out_ref[:, 2 * k * LANES : (2 * k + 1) * LANES] = key_grad.astype(jnp.bfloat16)
        out_ref[:, (2 * k + 1) * LANES : (2 * k + 2) * LANES] = grads_ref[1, :, columns]
    gain_grad_ref[...] = jnp.broadcast_to(gain_total, gain_grad_ref.shape)


def key_back(index, key_raw, cos_rows, sin_rows, gain, key_grad):
    _, rows, wide = key_grad.shape
    table_spec = pl.BlockSpec((rows, LANES), lambda m: (index, 0))
    return pl.pallas_call(
        functools.partial(key_back_kernel, wide // LANES),
        grid=(1,),
        in_specs=[
            pl.BlockSpec((rows, wide), lambda m: (index, 0)),
            table_spec,
            table_spec,
            sum_block((1, LANES)),
            sum_block(key_grad.shape),
        ],
        out_specs=[sum_block((rows, 2 * wide)), sum_block((8, LANES))],
        out_shape=[
            jax.ShapeDtypeStruct((rows, 2 * wide), jnp.bfloat16),
            jax.ShapeDtypeStruct((8, LANES), jnp.float32),
        ],
        compiler_params=params(),
        cost_estimate=cost(30 * rows * wide, 12 * rows * wide),
        name="key_back",
    )(key_raw, cos_rows, sin_rows, gain, key_grad)


def sum_kernel(count, transposed, *refs):
    lefts, rights, out_ref = refs[:count], refs[count : 2 * count], refs[2 * count]
    dot = dot_nt if transposed else dot_nn
    total = dot(lefts[0][...], rights[0][...])
    for left, right in zip(lefts[1:], rights[1:]):
        total += dot(left[...], right[...])
    out_ref[...] = total.astype(jnp.bfloat16)


def sum_of_products(rows, lefts, rights, transposed):
    def left_spec(place):
        _, depth, row_block, column_block = place
        return pl.BlockSpec(
            (rows, depth), lambda n: (row_block, column_block), pipeline_mode=pl.Buffered(1)
        )

    depth_total = sum(place[1] for place in lefts)
    if transposed:
        columns = rights[0].shape[0]
        block = min(512, columns)
        right_specs = [pl.BlockSpec((block, right.shape[1]), lambda n: (n, 0)) for right in rights]
    else:
        shards, _, part = rights[0].shape
        columns = shards * part
        block = min(256, part)
        per = part // block
        right_specs = [
            pl.BlockSpec((None, right.shape[1], block), lambda n: (n // per, 0, n % per))
            for right in rights
        ]
    return pl.pallas_call(
        functools.partial(sum_kernel, len(lefts), transposed),
        grid=(columns // block,),
        in_specs=[left_spec(place) for place in lefts] + right_specs,
        out_specs=pl.BlockSpec((rows, block), lambda n: (0, n)),
        out_shape=jax.ShapeDtypeStruct((rows, columns), jnp.bfloat16),
        compiler_params=params(),
        cost_estimate=cost(
            2 * rows * depth_total * columns,
            2 * depth_total * (rows + columns) + 2 * rows * columns,
        ),
        name="sum_of_products",
    )(*[place[0] for place in lefts], *rights)


def gradient_kernel(counts, sizes, arrivals, *refs):
    lefts, at = [], 0
    for count in counts:
        lefts.append(refs[at : at + count])
        at += count
    outs = refs[len(refs) - len(arrivals) :]
    for arrived_count, out_ref in zip(arrivals, outs):
        totals = []
        for term in lefts:
            rights = refs[at : at + len(term)]
            at += len(term)
            total = dot_tn(term[0][...], rights[0][...])
            for left, right in zip(term[1:], rights[1:]):
                total += dot_tn(left[...], right[...])
            totals.append(total)
        arrived = refs[at : at + arrived_count]
        at += arrived_count
        column = 0
        for total, size in zip(totals, sizes):
            span = slice(column, column + size)
            for item in arrived:
                total += item[:, span].astype(jnp.float32)
            out_ref[:, span] = total.astype(jnp.bfloat16)
            column += size


def weight_gradients(rows, lefts, sizes, parts):
    def right_spec(size, row_block, column_block):
        return pl.BlockSpec(
            (rows, size), lambda m: (row_block, column_block), pipeline_mode=pl.Buffered(1)
        )

    def left_spec(row_block):
        return pl.BlockSpec((rows, block), lambda m: (row_block, m))

    width = lefts[0][0][0].shape[1]
    block = min(512, width)
    total = sum(sizes)
    out_spec = pl.BlockSpec((block, total), lambda m: (m, 0))
    specs = [left_spec(place[1]) for term in lefts for place in term]
    operands = [place[0] for term in lefts for place in term]
    for rights, arrived in parts:
        for size, term in zip(sizes, rights):
            specs += [right_spec(size, place[1], place[2]) for place in term]
            operands += [place[0] for place in term]
        specs += [out_spec] * len(arrived)
        operands += list(arrived)
    depth = rows * max(len(term) for term in lefts)
    return pl.pallas_call(
        functools.partial(
            gradient_kernel,
            [len(term) for term in lefts],
            sizes,
            [len(arrived) for _, arrived in parts],
        ),
        grid=(width // block,),
        in_specs=specs,
        out_specs=[out_spec] * len(parts),
        out_shape=[jax.ShapeDtypeStruct((width, total), jnp.bfloat16)] * len(parts),
        compiler_params=params(),
        cost_estimate=cost(
            2 * len(parts) * depth * width * total, 2 * depth * width + 4 * len(parts) * width * total
        ),
        name="weight_gradients",
    )(*operands)


def split_dot_nt(left, rights):
    part = rights.shape[2]
    total = dot_nt(left[:, :part], rights[0])
    for index in range(1, rights.shape[0]):
        total += dot_nt(left[:, index * part : (index + 1) * part], rights[index])
    return total


def mlp_kernel(batches, count, down_in_ref, *refs):
    inputs = refs[:batches]
    pair_ws = refs[batches : batches + count]
    down_ws = refs[batches + count : batches + 2 * count]
    hiddens = refs[batches + 2 * count : batches + 3 * count]
    pair_ins = refs[batches + 3 * count :]
    block = hiddens[0].shape[1]
    for index in range(batches):

        @pl.when(pl.program_id(0) == index)
        def _(index=index):
            for k in range(count):
                gate_pre = dot_nn(inputs[index][...], pair_ws[k][:, :block])
                up_pre = dot_nn(inputs[index][...], pair_ws[k][:, block:])
                grad_hidden = split_dot_nt(down_in_ref[...], down_ws[k])
                sigmoid_gate = jax.nn.sigmoid(gate_pre)
                silu_gate = gate_pre * sigmoid_gate
                hiddens[k][...] = (silu_gate * up_pre).astype(jnp.bfloat16)
                pair_ins[k][:, block:] = (grad_hidden * silu_gate).astype(jnp.bfloat16)
                pair_ins[k][:, :block] = (
                    grad_hidden * up_pre * sigmoid_gate * (1.0 + gate_pre * (1.0 - sigmoid_gate))
                ).astype(jnp.bfloat16)


def mlp_units(inputs, down_in, pair_ws, down_ws):
    all_rows, width = down_in.shape
    batches, count = len(inputs), len(pair_ws)
    rows, units = all_rows // batches, pair_ws[0].shape[1] // 2
    return pl.pallas_call(
        functools.partial(mlp_kernel, batches, count),
        grid=(batches,),
        in_specs=[pl.BlockSpec((rows, width), lambda m: (m, 0))]
        + [whole_block(item.shape) for item in list(inputs) + pair_ws + down_ws],
        out_specs=[pl.BlockSpec((rows, units), lambda m: (m, 0))] * count
        + [pl.BlockSpec((rows, 2 * units), lambda m: (m, 0))] * count,
        out_shape=[jax.ShapeDtypeStruct((all_rows, units), jnp.bfloat16)] * count
        + [jax.ShapeDtypeStruct((all_rows, 2 * units), jnp.bfloat16)] * count,
        compiler_params=params(),
        cost_estimate=cost(
            6 * count * all_rows * width * units, 4 * all_rows * width + 6 * count * width * units
        ),
        name="mlp_units",
    )(down_in, *inputs, *pair_ws, *down_ws)


def add_norm_kernel(stream_ref, low_ref, other_ref, gain_ref, middle_ref, normed_ref):
    middle = (
        stream_ref[...].astype(jnp.float32)
        + (low_ref[...].astype(jnp.float32) + other_ref[...].astype(jnp.float32))
    )
    unit, _ = unit_of(middle)
    middle_ref[...] = middle
    normed_ref[...] = (unit * gain_ref[...]).astype(jnp.bfloat16)


def add_norm(index, stream, low_part, other_part, gain):
    rows, width = low_part.shape
    block = min(128, rows)
    first = index * (rows // block)
    spec = pl.BlockSpec((block, width), lambda m: (m, 0))
    return pl.pallas_call(
        add_norm_kernel,
        grid=(rows // block,),
        in_specs=[
            pl.BlockSpec((block, width), lambda m: (first + m, 0)),
            spec,
            spec,
            whole_block((1, width)),
        ],
        out_specs=[spec, spec],
        out_shape=[
            jax.ShapeDtypeStruct((rows, width), jnp.float32),
            jax.ShapeDtypeStruct((rows, width), jnp.bfloat16),
        ],
        compiler_params=params(),
        cost_estimate=cost(8 * rows * width, 12 * rows * width),
        name="add_norm",
    )(stream, low_part, other_part, gain)


def norm_back_kernel(values_ref, low_ref, other_ref, gain_ref, up_ref, *outs):
    grads = low_ref[...].astype(jnp.float32) + other_ref[...].astype(jnp.float32)
    gain_part, back = unit_back(values_ref[...].astype(jnp.float32), gain_ref[...], grads)
    total = up_ref[...].astype(jnp.float32) + back
    outs[0][...] = total.astype(jnp.bfloat16)
    for out_ref in outs[2:]:
        out_ref[...] = total

    @pl.when(pl.program_id(0) == 0)
    def _():
        outs[1][...] = jnp.zeros_like(outs[1])

    outs[1][0:1] += gain_part


def norm_back(values, values_at, low_part, other_part, gain, upstream, up_at, keep):
    rows, width = low_part.shape
    block = min(128, rows)
    steps = rows // block
    spec = pl.BlockSpec((block, width), lambda m: (m, 0))
    return pl.pallas_call(
        norm_back_kernel,
        grid=(steps,),
        in_specs=[
            pl.BlockSpec((block, width), lambda m: (values_at * steps + m, 0)),
            spec,
            spec,
            whole_block((1, width)),
            pl.BlockSpec((block, width), lambda m: (up_at * steps + m, 0)),
        ],
        out_specs=[spec, sum_block((8, width))] + [spec] * keep,
        out_shape=[
            jax.ShapeDtypeStruct((rows, width), jnp.bfloat16),
            jax.ShapeDtypeStruct((8, width), jnp.float32),
        ]
        + [jax.ShapeDtypeStruct((rows, width), jnp.float32)] * keep,
        compiler_params=params(),
        cost_estimate=cost(16 * rows * width, 16 * rows * width),
        name="norm_back",
    )(values, low_part, other_part, gain, upstream)


def order_kernel(per_quarter, turned, own_ref, *refs):
    pieces, out_ref = refs[:-1], refs[-1]
    step = pl.program_id(0)
    places = len(pieces) // per_quarter
    for index, piece in enumerate(pieces):

        @pl.when(step == index % places * per_quarter + index // places)
        def _(piece=piece):
            value = piece[...].astype(jnp.float32)
            out_ref[...] = value.T if turned else value


def in_order(chunks, block, column, turned=False):
    rows = chunks[0][0].shape[0]
    places, per_quarter = len(chunks[0]), len(chunks)
    own = lax.axis_index("replica").astype(jnp.int32).reshape(1)

    def out_of(step, own):
        place = step // per_quarter
        flip = jnp.where(place == 1, 2, jnp.where(place == 2, 1, place))
        at = jnp.bitwise_xor(own[0], flip) * per_quarter + step % per_quarter
        return (at, 0) if turned else (0, at)

    total = places * per_quarter * block
    pieces = [piece for chunk in chunks for piece in chunk]
    return pl.pallas_call(
        functools.partial(order_kernel, per_quarter, turned),
        grid_spec=pltpu.PrefetchScalarGridSpec(
            num_scalar_prefetch=1,
            grid=(places * per_quarter,),
            in_specs=[pl.BlockSpec((rows, block), lambda step, own: (0, column))] * len(pieces),
            out_specs=pl.BlockSpec((block, rows) if turned else (rows, block), out_of),
        ),
        out_shape=jax.ShapeDtypeStruct((total, rows) if turned else (rows, total), jnp.float32),
        compiler_params=params(),
        cost_estimate=cost(rows * total, 6 * rows * total),
        name="in_order",
    )(own, *pieces)


class Fold:
    def __init__(self, make_parts, far, far_end, direct):
        self.make_parts, self.far, self.far_end, self.direct = make_parts, far, far_end, direct

    def steps32(self):
        third, second = self.make_parts((3,), (2,))
        self.from_third, self.from_near = across(third, 1), across(second, 1)

    def step1(self):
        (part,) = self.make_parts((1, self.from_third))
        self.from_far = self.far.run(to_far, part)

    def step0(self):
        (part,) = self.make_parts((0, self.from_near, self.from_far))
        self.shard = scatter_rows(part)

    def steps10(self):
        first, own = self.make_parts((1, self.from_third), (0, self.from_near))
        self.far_shard, self.shard = scatter_rows(first), scatter_rows(own)

    def end(self):
        if self.direct:
            arrived = self.far_end.run(to_far, self.far_shard)
            total = self.shard.astype(jnp.float32) + arrived.astype(jnp.float32)
            self.shard = total.astype(jnp.bfloat16)
        return spread(self.shard, self.far_end)


class RelayBack:
    def __init__(self, parts):
        self.parts, self.steps = parts, []

    def advance(self, *earlier):
        at = len(self.parts) - 1 - len(self.steps)
        if at > 0:
            carry = self.steps[-1] if self.steps else self.parts[at]
            carry = after(carry, *earlier) if earlier else carry
            pairs = [(index, index - 1) for index in range(1, len(self.parts))]
            arrived = lax.ppermute(carry, "fsdp", pairs).astype(jnp.float32)
            total = self.parts[at - 1].astype(jnp.float32) + arrived
            self.steps.append(total.astype(jnp.bfloat16))
        return self.steps[-1]

    def finish(self):
        while len(self.steps) < len(self.parts) - 1:
            self.advance()
        return self.steps[-1]


def local(
    tokens,
    cotangent,
    lengths,
    parents,
    attn_gain,
    qk_gain,
    w_query,
    key_weight_matrix,
    value_weight_matrix,
    w_headgate,
    w_out,
    mlp_gain,
    w_gate,
    w_up,
    w_down,
):
    batches, rows, width = tokens.shape
    shards = lax.axis_size("fsdp")
    shard = lax.axis_index("fsdp")
    query_gain, key_gain = qk_gain[0, 0:1], qk_gain[0, 1:2]
    low = jnp.bfloat16

    query_piece = own_quarter(w_query[0], 1)
    head_piece = own_quarter(w_headgate[0], 1)
    per_kv = query_piece.shape[1] // LANES
    own = per_kv * LANES
    pad = jnp.zeros((query_piece.shape[0], LANES - head_piece.shape[1]), low)
    gate_piece, up_piece = own_quarter(w_gate[0], 1), own_quarter(w_up[0], 1)
    down_piece = own_quarter(w_down[0], 0)
    unit_block = min(256, gate_piece.shape[1])
    unit_blocks = gate_piece.shape[1] // unit_block
    def unit_span(value, block, axis):
        return lax.slice_in_dim(value, block * unit_block, (block + 1) * unit_block, axis=axis)

    far_in, far_out, far_end = Line(2), Line(2), Line(2)
    key_value_w = spread(
        gather_shards(
            jnp.concatenate(
                [own_quarter(key_weight_matrix[0], 1), own_quarter(value_weight_matrix[0], 1)],
                axis=1,
            ),
        ),
        far_in,
    )
    query_part = gather_shards(jnp.concatenate([query_piece, head_piece, pad], axis=1))
    out_part = gather_stacked(own_quarter(w_out[0], 0))
    groups = len(key_value_w)
    chunk_of = range(unit_blocks)

    tables, positions = [], []
    for index in range(batches):
        need, query_mask, key_mask, position = tree_need(
            lengths[index, 0], parents[index, 0], shard, rows, shards
        )
        tables.append((need, query_mask, key_mask))
        positions.append(position)
    half = LANES // 2
    frequency = THETA ** (-(jnp.arange(half, dtype=jnp.float32) * 2.0 / LANES))
    angle = jnp.concatenate(positions).astype(jnp.float32)[:, None] * frequency[None, :]
    cosine, sine = jnp.cos(angle), jnp.sin(angle)
    cos_rows = jnp.concatenate([cosine, cosine], axis=1)
    sin_rows = jnp.concatenate([-sine, sine], axis=1)

    core = Line(1)
    stream = tokens.reshape(batches * rows, width)
    down_in = cotangent.reshape(batches * rows, width)
    normed_low = (unit_of(stream.astype(jnp.float32))[0] * attn_gain).astype(low)
    key_value, key_raw = core.run(
        key_value_heads, normed_low, key_value_w, cos_rows, sin_rows, key_gain
    )
    query_w = spread(after(query_part, key_value), far_in)
    relays = [Relay(key_value[index * rows : (index + 1) * rows], shards) for index in range(batches)]
    for index, relay in enumerate(relays):
        if index > 0:
            relay.hold(relays[index - 1].latest)
        relay.advance()
    core.hold(*[relay.latest for relay in relays[1:]])
    query_low, query_raw, gates = core.run(
        query_heads, normed_low, query_w, cos_rows, sin_rows, query_gain, per_kv
    )
    out_w = jnp.stack(spread(after(out_part, key_value), far_in))
    for _ in range(2, shards):
        relays[0].advance()
    for index in range(1, batches):
        for step in range(2, shards):
            if step == 2:
                relays[index].hold(query_low)
            relays[index].advance()
    blocks = [relay.blocks for relay in relays]
    tie = blocks[0][-1]
    pair_w, down_w, pair_parts = [], [], []
    for chunk in chunk_of:
        piece = jnp.concatenate(
            [unit_span(gate_piece, chunk, 1), unit_span(up_piece, chunk, 1)], axis=1
        )
        pair_parts.append(gather_shards(after(piece, tie, query_low, out_part)))
    down_part = gather_stacked(after(down_piece, tie, query_low, out_part))
    pair_parts[0] = after(pair_parts[0], blocks[0][-1])
    pair_w.append(spread(pair_parts[0], far_in))
    mixed, attended, logs, middle, mlp_low, parts = [], [], [], [], [], []
    for index in range(batches):
        tree_mixed, tree_out, tree_log = core.run(
            lambda query: attend_forward(
                index, batches, tables[index], query, gates, blocks[index], per_kv
            ),
            query_low,
        )
        mixed.append(tree_mixed)
        attended.append(tree_out)
        logs.append(tree_log)
        part = core.run(
            lambda left: sum_of_products(
                rows,
                [(left, own, 0, k) for k in range(groups)],
                [out_w[k] for k in range(groups)],
                False,
            ),
            tree_mixed,
        )
        parts.append((part, tensor_other(part)))
    down_part = after(down_part, part)
    for chunk in chunk_of:
        down_w.append(spread(unit_span(down_part, chunk, 1), far_in))
    for item in pair_parts[1:]:
        pair_w.append(spread(after(item, part), far_in))
    for index in range(batches):
        core.hold(pair_w[0][1], down_w[min(index, unit_blocks - 1)][1])
        tree_middle, tree_normed = core.run(
            lambda part: add_norm(index, stream, part, parts[index][1], mlp_gain), parts[index][0]
        )
        middle.append(tree_middle)
        mlp_low.append(tree_normed)

    hidden = [[None] * groups for _ in chunk_of]
    pair_in = [[None] * groups for _ in chunk_of]

    def do_units(chunk, members):
        made = core.run(
            lambda upstream: mlp_units(
                mlp_low,
                upstream,
                [pair_w[chunk][k] for k in members],
                [down_w[chunk][k] for k in members],
            ),
            down_in,
        )
        for place, k in enumerate(members):
            hidden[chunk][k], pair_in[chunk][k] = made[place], made[len(members) + place]

    def fold(lefts, sizes, rights_of, direct=False):
        def make_parts(*wanted):
            def work(first):
                own_lefts = [[(first,) + lefts[0][0][1:]] + lefts[0][1:]] + lefts[1:]
                parts = [(rights_of(k), arrived) for k, *arrived in wanted]
                return weight_gradients(rows, own_lefts, sizes, parts)

            return core.run(work, lefts[0][0][0])

        return Fold(make_parts, far_out, far_end, direct)

    def both(value, column=0):
        return [(value, index, column) for index in range(batches)]

    def apart(values, column=0):
        return [(value, 0, column) for value in values]

    unit_folds = [
        fold(
            [apart(mlp_low), both(down_in)],
            [2 * unit_block, unit_block],
            lambda k, c=c: [both(pair_in[c][k]), both(hidden[c][k])],
            direct=c == 0,
        )
        for c in chunk_of
    ]

    middle_parts = []

    def do_middle_part(index):
        part = core.run(
            lambda left: sum_of_products(
                rows,
                [
                    (left if (c, k) == (0, 0) else pair_in[c][k], 2 * unit_block, index, 0)
                    for c in chunk_of
                    for k in range(groups)
                ],
                [pair_w[c][k] for c in chunk_of for k in range(groups)],
                True,
            ),
            pair_in[0][0],
        )
        middle_parts.append((part, tensor_other(part)))

    mlp_gain_grad, grad_middle, out_in = [], [], []
    query_in, query_gain_grad, relays_back = [], [], []

    def do_norm_back(index):
        low_out, gain_part, full = core.run(
            lambda part: norm_back(
                middle[index], 0, part, middle_parts[index][1], mlp_gain, down_in, index, 1
            ),
            middle_parts[index][0],
        )
        out_in.append(low_out)
        mlp_gain_grad.append(gain_part)
        grad_middle.append(full)

    def do_attention_back(index):
        tree_in, gain_part, *grads = core.run(
            lambda upstream: attend_backward(
                index,
                batches,
                tables[index],
                upstream,
                out_w,
                query_low,
                gates,
                logs[index],
                attended[index],
                query_raw,
                cos_rows,
                sin_rows,
                query_gain,
                blocks[index],
                per_kv,
            ),
            out_in[index],
        )
        query_in.append(tree_in)
        query_gain_grad.append(gain_part)
        relays_back.append(RelayBack(grads))
        relays_back[-1].advance()

    result_parts = []

    def do_result_part(index):
        part = core.run(
            lambda left: sum_of_products(
                rows,
                [
                    (left if (c, k) == (0, 0) else hidden[c][k], unit_block, index, 0)
                    for c in chunk_of
                    for k in range(groups)
                ],
                [down_w[c][k] for c in chunk_of for k in range(groups)],
                False,
            ),
            hidden[0][0],
        )
        result_parts.append((part, tensor_other(part)))

    final = unit_blocks - 1
    for chunk in chunk_of:
        if chunk > 0:
            core.hold(pair_w[chunk][1])
        do_units(chunk, (0, 2))
        if chunk > 0:
            previous = unit_folds[chunk - 1]
            previous.steps10() if previous.direct else previous.step1()
            core.hold(pair_parts[-1])
        else:
            core.hold(down_w[-1][1])
        do_units(chunk, (1, 3))
        unit_folds[chunk].steps32()
    do_middle_part(0)
    if unit_folds[final].direct:
        unit_folds[final].steps10()
    else:
        unit_folds[final].step1()
    for index in range(1, batches):
        do_middle_part(index)
    waiting = [item for item in unit_folds if not item.direct]
    do_norm_back(0)
    for item in waiting[:-1]:
        item.step0()
    do_attention_back(0)
    core.hold(*[item.from_far for item in waiting[-1:]])
    for index in range(1, batches):
        do_norm_back(index)
    do_result_part(0)
    core.hold(relays_back[0].steps[0])
    for item in waiting[-1:]:
        item.step0()
    unit_ends = [unit_folds[0].end()]
    for index in range(1, batches):
        do_result_part(index)
    core.hold(relays_back[0].advance(), result_parts[0][1])
    for index in range(1, batches):
        do_attention_back(index)
    query_block = own + LANES
    wide_fold = fold(
        [apart(out_in), both(normed_low)],
        [own, query_block],
        lambda k: [apart(mixed, k), apart(query_in, k)],
    )
    wide_fold.steps32()
    wide_fold.step1()
    for relay in relays_back[1:]:
        relay.advance(core.sent[-1])
    key_block = 2 * LANES
    key_in, key_gain_grad, stream_parts = [], [], []

    def do_key_back(index):
        tree_in, gain_part = core.run(
            lambda raw: key_back(
                index, raw, cos_rows, sin_rows, key_gain, relays_back[index].finish()
            ),
            key_raw,
        )
        key_in.append(tree_in)
        key_gain_grad.append(gain_part)

    def do_stream_part(index):
        part = core.run(
            lambda left: sum_of_products(
                rows,
                [(query_in[index], query_block, 0, k) for k in range(groups)]
                + [(left, key_block, 0, k) for k in range(groups)],
                query_w + key_value_w,
                True,
            ),
            key_in[index],
        )
        stream_parts.append((part, tensor_other(part)))

    attn_gain_grad, input_grad = [], []

    def do_stream_back(index):
        part, other = stream_parts[index]
        low_out, gain_part = core.run(
            lambda part: norm_back(
                stream, index, part, other, attn_gain, grad_middle[index], 0, 0
            ),
            part,
        )
        input_grad.append(low_out)
        attn_gain_grad.append(gain_part)

    do_key_back(0)
    unit_ends += [item.end() for item in unit_folds[1:]]
    do_stream_part(0)
    core.hold(*[part[1] for part in result_parts])

    def do_order(column):
        return core.run(
            lambda first: in_order(
                [[first] + unit_ends[0][1:]] + unit_ends[1:], unit_block, column, column == 2
            ),
            unit_ends[0][0],
        )

    for index in range(1, batches):
        do_key_back(index)
    key_fold = fold([both(normed_low)], [key_block], lambda k: [apart(key_in, k)])
    key_fold.steps32()
    wide_fold.step0()
    key_fold.step1()
    for index in range(1, batches):
        do_stream_part(index)
    core.hold(stream_parts[0][1])
    key_fold.step0()
    do_stream_back(0)
    gate_order = do_order(0)
    up_order = do_order(1)
    down_order = do_order(2)
    for index in range(1, batches):
        do_stream_back(index)
    results = [
        (
            middle[index]
            + (part.astype(jnp.float32) + other.astype(jnp.float32))
        ).astype(low)
        for index, (part, other) in enumerate(result_parts)
    ]
    wide_shards = wide_fold.end()
    key_shards = key_fold.end()
    query_sum, key_sum = [
        jnp.sum(jnp.stack(items), axis=0)[0] for items in (query_gain_grad, key_gain_grad)
    ]
    wide_sums = [
        jnp.sum(jnp.stack(items), axis=0)[0] for items in (attn_gain_grad, mlp_gain_grad)
    ]
    gain_sum = axis_sum(
        axis_sum(jnp.concatenate(wide_sums + [query_sum, key_sum]), "replica"), "fsdp"
    )
    head_sum = axis_sum(gain_sum[2 * width :], "tensor")

    def own_slice(value, axis):
        size = value.shape[axis] // shards
        return lax.dynamic_slice_in_dim(value, shard * size, size, axis)[None]

    gate_count = head_piece.shape[1]
    gate_grad = in_order([wide_shards], LANES, 2 * per_kv)
    gate_grad = gate_grad.reshape(gate_grad.shape[0], groups, LANES)[:, :, :gate_count]
    return (
        jnp.stack(results),
        jnp.stack(input_grad),
        own_slice(gain_sum[:width], 0),
        own_slice(head_sum.reshape(2, LANES), 1),
        in_order([wide_shards], own, 1)[None],
        in_order([key_shards], LANES, 0)[None],
        in_order([key_shards], LANES, 1)[None],
        gate_grad.reshape(1, gate_grad.shape[0], groups * gate_count),
        in_order([wide_shards], own, 0, turned=True)[None],
        own_slice(gain_sum[width : 2 * width], 0),
        gate_order[None],
        up_order[None],
        down_order[None],
    )


def solution(mesh):
    placed = (
        P(None, ("replica", "fsdp"), None),
        P(None, ("replica", "fsdp"), None),
        P(None, "replica", None),
        P(None, "replica", None),
        P(),
        P(),
        P(None, "fsdp", "tensor"),
        P(None, "fsdp", "tensor"),
        P(None, "fsdp", "tensor"),
        P(None, "fsdp", "tensor"),
        P(None, "tensor", "fsdp"),
        P(),
        P(None, "fsdp", "tensor"),
        P(None, "fsdp", "tensor"),
        P(None, "tensor", "fsdp"),
    )
    return jax.shard_map(
        local,
        mesh=mesh,
        in_specs=placed,
        out_specs=(
            P(None, ("replica", "fsdp"), None),
            P(None, ("replica", "fsdp"), None),
            P(None, "fsdp"),
            P(None, None, "fsdp"),
            P(None, "fsdp", "tensor"),
            P(None, "fsdp", "tensor"),
            P(None, "fsdp", "tensor"),
            P(None, "fsdp", "tensor"),
            P(None, "tensor", "fsdp"),
            P(None, "fsdp"),
            P(None, "fsdp", "tensor"),
            P(None, "fsdp", "tensor"),
            P(None, "tensor", "fsdp"),
        ),
        check_vma=False,
    )
```

```python
import functools

import jax
import jax.numpy as jnp
from jax import lax
from jax.experimental import pallas as pl
from jax.experimental.pallas import tpu as pltpu
from jax.sharding import PartitionSpec as P

EPSILON = 1e-06
THETA = 1000000.0
LOG2_E = 1.4426950408889634
LANES = 128
EXTRA_AT = 16
VMEM_BYTES = 58 * 1024 * 1024
COST_SHARE = 0.22


def segment_table(lengths, parents):
    count = lengths.shape[0]
    starts = jnp.cumsum(lengths) - lengths
    labels = jnp.arange(count, dtype=jnp.int32)
    parent_hot = (parents[:, None] == labels[None, :]).astype(jnp.int32)
    grand_hot = jnp.dot(parent_hot, parent_hot)
    eye_hot = (labels[:, None] == labels[None, :]).astype(jnp.int32)
    ancestor = (eye_hot + parent_hot + grand_hot > 0).astype(jnp.int32)
    before = jnp.sum(ancestor * (1 - eye_hot) * lengths[None, :], axis=1)
    return (starts, before - starts, ancestor)


def row_segments(indices, starts, count):
    labels = jnp.arange(count, dtype=jnp.int32)
    member = jnp.sum((indices[:, None] >= starts[None, :]).astype(jnp.int32), axis=1) - 1
    return (member[:, None] == labels[None, :]).astype(jnp.int32)


def swaps(bit, count):
    return [(index, index ^ bit) for index in range(count)]


def across(value, bit):
    return lax.ppermute(value, "replica", swaps(bit, lax.axis_size("replica")))


def own_quarter(shard, axis):
    size = shard.shape[axis] // lax.axis_size("replica")
    return lax.dynamic_slice_in_dim(shard, lax.axis_index("replica") * size, size, axis)


def spread(block):
    other = across(block, 2)
    return [block, other, across(block, 1), across(other, 1)]


def after(value, *earlier):
    return lax.optimization_barrier((value, *earlier))[0] if earlier else value


class Line:
    def __init__(self, depth):
        self.depth = depth
        self.sent = []
        self.held = []

    def before(self):
        last = [self.sent[-self.depth]] if len(self.sent) >= self.depth else []
        held, self.held = self.held, []
        return last + held

    def hold(self, *values):
        self.held += values

    def run(self, function, value, *rest):
        result = function(after(value, *self.before()), *rest)
        self.sent.append(result[0] if isinstance(result, (list, tuple)) else result)
        return result


def gather_shards(value):
    return lax.all_gather(value, "fsdp", axis=0, tiled=True)


def gather_stacked(value):
    return lax.all_gather(value, "fsdp", axis=0, tiled=False)


def scatter_rows(value):
    return lax.psum_scatter(value, "fsdp", scatter_dimension=0, tiled=True)


def to_far(value):
    return across(value, 2)


def spread(block, far_line):
    other = far_line.run(to_far, block)
    return [block, other, across(block, 1), across(other, 1)]


def axis_sum(value, axis):
    size, bit = lax.axis_size(axis), 1
    while bit < size:
        if bit * 4 <= size:
            near, far, both = [
                lax.ppermute(value, axis, swaps(bit * flip, size)) for flip in (1, 2, 3)
            ]
            value, bit = (value + near) + (far + both), bit * 4
        else:
            value, bit = value + lax.ppermute(value, axis, swaps(bit, size)), bit * 2
    return value


def tensor_other(low_part):
    return lax.ppermute(low_part, "tensor", swaps(1, lax.axis_size("tensor")))


class Relay:
    def __init__(self, block, count):
        self.blocks, self.count, self.held = [block], count, []
        self.latest = block

    def hold(self, *values):
        self.held += values

    def advance(self):
        if len(self.blocks) < self.count:
            value = after(self.blocks[-1], *self.held) if self.held else self.blocks[-1]
            self.held = []
            pairs = [(index, index + 1) for index in range(self.count - 1)]
            self.blocks.append(lax.ppermute(value, "fsdp", pairs))
            self.latest = self.blocks[-1]


def params():
    return pltpu.CompilerParams(vmem_limit_bytes=VMEM_BYTES)


def cost(flops, moved, rate=0.56):
    return pl.CostEstimate(
        flops=int(flops * COST_SHARE / rate),
        bytes_accessed=int(moved * COST_SHARE / 0.6),
        transcendentals=0,
    )


def whole_block(shape):
    return pl.BlockSpec(shape, lambda *index: (0,) * len(shape), pipeline_mode=pl.Buffered(1))


def sum_block(shape):
    return pl.BlockSpec(shape, lambda *index: (0,) * len(shape))


def dot_nn(left, right):
    return jnp.dot(left, right, preferred_element_type=jnp.float32)


def dot_nt(left, right):
    return lax.dot_general(
        left, right, (((1,), (1,)), ((), ())), preferred_element_type=jnp.float32
    )


def dot_tn(left, right):
    return lax.dot_general(
        left, right, (((0,), (0,)), ((), ())), preferred_element_type=jnp.float32
    )


def three_parts(value):
    first = value.astype(jnp.bfloat16)
    rest = value - first.astype(jnp.float32)
    second = rest.astype(jnp.bfloat16)
    third = (rest - second.astype(jnp.float32)).astype(jnp.bfloat16)
    return (first, second, third)


def put_lanes(base, parts):
    lane = lax.broadcasted_iota(jnp.int32, base.shape, 1)
    value = base.astype(jnp.float32)
    for offset, part in enumerate(parts):
        value = jnp.where(lane == EXTRA_AT + offset, part.astype(jnp.float32), value)
    return value.astype(jnp.bfloat16)


def rope(values, cos_rows, sin_rows):
    return values * cos_rows + pltpu.roll(values, LANES // 2, 1) * sin_rows


def rope_back(grads, cos_rows, sin_rows):
    return grads * cos_rows - pltpu.roll(grads, LANES // 2, 1) * sin_rows


def unit_of(raw):
    inverse = lax.rsqrt(jnp.mean(raw * raw, axis=-1, keepdims=True) + EPSILON)
    return (raw * inverse, inverse)


def unit_back(raw, gain, grads):
    unit, inverse = unit_of(raw)
    scaled = grads * gain
    gain_part = jnp.sum(grads * unit, axis=0, keepdims=True)
    return (
        gain_part,
        inverse * (scaled - unit * jnp.mean(scaled * unit, axis=-1, keepdims=True)),
    )


def key_value_kernel(groups, x_ref, cos_ref, sin_ref, gain_ref, *refs):
    weights, (kv_ref, raw_ref) = refs[:groups], refs[groups:]
    for k in range(groups):
        part = dot_nn(x_ref[...], weights[k][...])
        raw = part[:, :LANES]
        unit, _ = unit_of(raw)
        raw_ref[:, k * LANES : (k + 1) * LANES] = raw
        kv_ref[:, k * LANES : (k + 1) * LANES] = rope(
            unit * gain_ref[...], cos_ref[...], sin_ref[...]
        ).astype(jnp.bfloat16)
        at = (groups + k) * LANES
        kv_ref[:, at : at + LANES] = part[:, LANES:].astype(jnp.bfloat16)


def key_value_heads(normed_low, weights, cos_rows, sin_rows, gain):
    rows, width = normed_low.shape
    groups, block = len(weights), min(256, rows)
    return pl.pallas_call(
        functools.partial(key_value_kernel, groups),
        grid=(rows // block,),
        in_specs=[
            pl.BlockSpec((block, width), lambda m: (m, 0)),
            pl.BlockSpec((block, LANES), lambda m: (m, 0)),
            pl.BlockSpec((block, LANES), lambda m: (m, 0)),
            whole_block((1, LANES)),
        ]
        + [whole_block(weight.shape) for weight in weights],
        out_specs=[
            pl.BlockSpec((block, 2 * groups * LANES), lambda m: (m, 0)),
            pl.BlockSpec((block, groups * LANES), lambda m: (m, 0)),
        ],
        out_shape=[
            jax.ShapeDtypeStruct((rows, 2 * groups * LANES), jnp.bfloat16),
            jax.ShapeDtypeStruct((rows, groups * LANES), jnp.float32),
        ],
        compiler_params=params(),
        cost_estimate=cost(4 * rows * width * groups * LANES, 4 * rows * width),
        name="key_value_heads",
    )(normed_low, cos_rows, sin_rows, gain, *weights)


def query_kernel(groups, per_kv, x_ref, cos_ref, sin_ref, gain_ref, *refs):
    weights, (low_ref, raw_ref, gate_ref) = refs[:groups], refs[groups:]
    for k in range(groups):
        part = dot_nn(x_ref[...], weights[k][...])
        for head in range(per_kv):
            raw = part[:, head * LANES : (head + 1) * LANES]
            unit, _ = unit_of(raw)
            at = (k * per_kv + head) * LANES
            raw_ref[:, at : at + LANES] = raw
            low_ref[:, at : at + LANES] = rope(
                unit * gain_ref[...], cos_ref[...], sin_ref[...]
            ).astype(jnp.bfloat16)
        gate_ref[k] = jax.nn.sigmoid(part[:, per_kv * LANES :])


def query_heads(normed_low, weights, cos_rows, sin_rows, gain, per_kv):
    rows, width = normed_low.shape
    groups, block = len(weights), min(256, rows)
    wide = groups * per_kv * LANES
    return pl.pallas_call(
        functools.partial(query_kernel, groups, per_kv),
        grid=(rows // block,),
        in_specs=[
            pl.BlockSpec((block, width), lambda m: (m, 0)),
            pl.BlockSpec((block, LANES), lambda m: (m, 0)),
            pl.BlockSpec((block, LANES), lambda m: (m, 0)),
            whole_block((1, LANES)),
        ]
        + [whole_block(weight.shape) for weight in weights],
        out_specs=[
            pl.BlockSpec((block, wide), lambda m: (m, 0)),
            pl.BlockSpec((block, wide), lambda m: (m, 0)),
            pl.BlockSpec((groups, block, LANES), lambda m: (0, m, 0)),
        ],
        out_shape=[
            jax.ShapeDtypeStruct((rows, wide), jnp.bfloat16),
            jax.ShapeDtypeStruct((rows, wide), jnp.float32),
            jax.ShapeDtypeStruct((groups, rows, LANES), jnp.float32),
        ],
        compiler_params=params(),
        cost_estimate=cost(2 * rows * width * groups * (per_kv + 1) * LANES, 4 * rows * width),
        name="query_heads",
    )(normed_low, cos_rows, sin_rows, gain, *weights)


def tiles_of(row_count):
    block = min(256, row_count)
    return (block, row_count // block)


def tree_need(lengths, parents, shard, row_count, shards):
    count = lengths.shape[0]
    starts, offsets, ancestor = segment_table(lengths, parents)
    block, tiles = tiles_of(row_count)
    query_index = shard * row_count + jnp.arange(row_count, dtype=jnp.int32)
    query_hot = row_segments(query_index, starts, count)
    reach = jnp.sum(query_hot[:, :, None] * ancestor[None, :, :], axis=1)
    position = query_index + jnp.sum(query_hot * offsets[None, :], axis=1)
    back = jnp.arange(shards, dtype=jnp.int32)[:, None]
    key_index = (shard - back) * row_count + jnp.arange(row_count, dtype=jnp.int32)[None, :]
    key_hot = row_segments(key_index.reshape(-1), starts, count)
    query_has = jnp.max(reach.reshape(tiles, block, count), axis=1)
    key_has = jnp.max(key_hot.reshape(shards, tiles, block, count), axis=2)
    need = jnp.sum(query_has[:, None, None, :] * key_has[None], axis=-1) > 0
    wall = jnp.where(reach > 0, 0.0, -1e30)
    query_mask = jnp.pad(wall, ((0, 0), (0, LANES - count))).astype(jnp.bfloat16)
    lane = jnp.arange(LANES)[None, :]
    ones = ((lane >= EXTRA_AT) & (lane < EXTRA_AT + 3)).astype(jnp.float32)
    key_mask = jnp.pad(key_hot.astype(jnp.float32), ((0, 0), (0, LANES - count))) + ones
    return (need.astype(jnp.int32).reshape(-1), query_mask, key_mask.astype(jnp.bfloat16), position)


def forward_kernel(
    shards, per_kv, factor, need_ref, q_ref, qmask_ref, gate_ref, kmask_ref, *refs
):
    keys, values = refs[:shards], refs[shards : 2 * shards]
    mixed_ref, attended_ref, log_ref, total_ref = refs[-4:]
    rows = q_ref.shape[0]
    block, tiles = tiles_of(rows)
    lane = lax.broadcasted_iota(jnp.int32, (block, LANES), 1)
    for qi in range(tiles):
        span = slice(qi * block, (qi + 1) * block)
        total_ref[...] = jnp.zeros_like(total_ref)
        for shard in range(shards):
            for ci in range(tiles):
                if shard == 0 and ci > qi:
                    continue
                part = slice(ci * block, (ci + 1) * block)

                @pl.when(need_ref[(qi * shards + shard) * tiles + ci] > 0)
                def _(shard=shard, ci=ci, part=part):
                    at = shard * rows + ci * block
                    key_mask = kmask_ref[at : at + block]
                    key_wide = jnp.concatenate([keys[shard][part], key_mask], axis=1)
                    value_wide = jnp.concatenate(
                        [values[shard][part], jnp.ones((block, LANES), jnp.bfloat16)], axis=1
                    )
                    for head in range(per_kv):
                        query_wide = jnp.concatenate(
                            [q_ref[span, head * LANES : (head + 1) * LANES], qmask_ref[span]],
                            axis=1,
                        )
                        scores = dot_nt(query_wide, key_wide)
                        if shard == 0 and ci == qi:
                            row = lax.broadcasted_iota(jnp.int32, (block, block), 0)
                            column = lax.broadcasted_iota(jnp.int32, (block, block), 1)
                            scores = jnp.where(column <= row, scores, -1e30)
                        weights = jnp.exp2(scores * factor).astype(jnp.bfloat16)
                        total_ref[head] += dot_nn(weights, value_wide)

        logs = jnp.zeros((block, LANES), jnp.float32)
        for head in range(per_kv):
            summed = total_ref[head][:, LANES:]
            tree_out = total_ref[head][:, :LANES] / summed
            columns = slice(head * LANES, (head + 1) * LANES)
            attended_ref[span, columns] = tree_out
            gate = gate_ref[0, span, head : head + 1]
            mixed_ref[span, columns] = (gate * tree_out).astype(jnp.bfloat16)
            logs = jnp.where(lane == head, jnp.log(summed), logs)
        log_ref[0, span] = logs


def attend_forward(index, batches, tables, query_low, gates, blocks, per_kv):
    need, query_mask, key_mask = tables
    all_rows, wide = query_low.shape
    rows = all_rows // batches
    shards = len(blocks)
    groups = wide // (per_kv * LANES)
    own = per_kv * LANES
    block, _ = tiles_of(rows)
    tree_spec = pl.BlockSpec((rows, own), lambda g, need: (0, g))
    log_spec = pl.BlockSpec((1, rows, LANES), lambda g, need: (g, 0, 0))
    return pl.pallas_call(
        functools.partial(forward_kernel, shards, per_kv, LANES ** (-0.5) * LOG2_E),
        grid_spec=pltpu.PrefetchScalarGridSpec(
            num_scalar_prefetch=1,
            grid=(groups,),
            in_specs=[
                pl.BlockSpec((rows, own), lambda g, need: (index, g)),
                whole_block(query_mask.shape),
                pl.BlockSpec((1, rows, LANES), lambda g, need: (g, index, 0)),
                whole_block(key_mask.shape),
            ]
            + [pl.BlockSpec((rows, LANES), lambda g, need: (0, g))] * shards
            + [pl.BlockSpec((rows, LANES), lambda g, need: (0, groups + g))] * shards,
            out_specs=[tree_spec, tree_spec, log_spec],
            scratch_shapes=[pltpu.VMEM((per_kv, block, 2 * LANES), jnp.float32)],
        ),
        out_shape=[
            jax.ShapeDtypeStruct((rows, wide), jnp.bfloat16),
            jax.ShapeDtypeStruct((rows, wide), jnp.float32),
            jax.ShapeDtypeStruct((groups, rows, LANES), jnp.float32),
        ],
        compiler_params=params(),
        cost_estimate=cost(
            4 * rows * rows * shards * wide,
            8 * rows * wide + 2 * shards * rows * wide,
            0.19,
        ),
        name="attend_forward",
    )(need, query_low, query_mask, gates, key_mask, *blocks, *blocks)


def backward_kernel(
    shards,
    per_kv,
    need_ref,
    out_in_ref,
    w_out_ref,
    q_ref,
    qmask_ref,
    gate_ref,
    kmask_ref,
    log_ref,
    attended_ref,
    raw_ref,
    cos_ref,
    sin_ref,
    gain_ref,
    *refs,
):
    scale = LANES ** (-0.5)
    factor = scale * LOG2_E
    keys, values = refs[:shards], refs[shards : 2 * shards]
    query_in_ref, gain_grad_ref = refs[2 * shards : 2 * shards + 2]
    block_grads = refs[2 * shards + 2 : 3 * shards + 2]
    dq_ref, dk_ref, dv_ref, qwide_ref, dwide_ref = refs[3 * shards + 2 :]
    rows = q_ref.shape[0]
    block, tiles = tiles_of(rows)
    grad_mixed = split_dot_nt(out_in_ref[...], w_out_ref)
    lane = lax.broadcasted_iota(jnp.int32, (rows, LANES), 1)
    logits = jnp.zeros((rows, LANES), jnp.float32)
    for head in range(per_kv):
        columns = slice(head * LANES, (head + 1) * LANES)
        attended = attended_ref[:, columns]
        gate = gate_ref[0, :, head : head + 1]
        mixed_grad = grad_mixed[:, columns]
        logit = jnp.sum(mixed_grad * attended, axis=-1, keepdims=True) * gate * (1.0 - gate)
        logits = jnp.where(lane == head, logit, logits)
        attended_in = (mixed_grad * gate).astype(jnp.bfloat16)
        delta = jnp.sum(attended_in.astype(jnp.float32) * attended, axis=-1, keepdims=True)
        dwide_ref[head, :, :LANES] = attended_in
        dwide_ref[head, :, LANES:] = put_lanes(
            jnp.zeros((rows, LANES), jnp.bfloat16), three_parts(-delta)
        )
        qwide_ref[head, :, :LANES] = q_ref[:, columns]
        qwide_ref[head, :, LANES:] = put_lanes(
            qmask_ref[...], three_parts(log_ref[0, :, head : head + 1] * (-1.0 / scale))
        )
    query_in_ref[:, per_kv * LANES :] = logits.astype(jnp.bfloat16)
    dq_ref[...] = jnp.zeros_like(dq_ref)
    for shard in range(shards):
        for ci in range(tiles):
            part = slice(ci * block, (ci + 1) * block)
            at = shard * rows + ci * block
            dk_ref[...] = jnp.zeros_like(dk_ref)
            dv_ref[...] = jnp.zeros_like(dv_ref)
            for qi in range(tiles):
                if shard == 0 and ci > qi:
                    continue
                span = slice(qi * block, (qi + 1) * block)

                @pl.when(need_ref[(qi * shards + shard) * tiles + ci] > 0)
                def _(shard=shard, ci=ci, qi=qi, at=at, part=part, span=span):
                    key_low = keys[shard][part]
                    key_mask = kmask_ref[at : at + block]
                    key_wide = jnp.concatenate([key_low, key_mask], axis=1)
                    value_wide = jnp.concatenate([values[shard][part], key_mask], axis=1)
                    for head in range(per_kv):
                        scores = dot_nt(key_wide, qwide_ref[head, span])
                        if shard == 0 and ci == qi:
                            row = lax.broadcasted_iota(jnp.int32, (block, block), 0)
                            column = lax.broadcasted_iota(jnp.int32, (block, block), 1)
                            scores = jnp.where(row <= column, scores, -1e30)
                        weights = jnp.exp2(scores * factor)
                        change = dot_nt(value_wide, dwide_ref[head, span])
                        grad_scores = (weights * change).astype(jnp.bfloat16)
                        weights = weights.astype(jnp.bfloat16)
                        dv_ref[...] += dot_nn(weights, dwide_ref[head, span, :LANES])
                        dk_ref[...] += dot_nn(grad_scores, qwide_ref[head, span, :LANES])
                        dq_ref[head, span] += dot_tn(grad_scores, key_low)

            block_grads[shard][0, part] = (dk_ref[...] * scale).astype(jnp.bfloat16)
            block_grads[shard][1, part] = dv_ref[...].astype(jnp.bfloat16)
    gain_total = jnp.zeros((1, LANES), jnp.float32)
    for head in range(per_kv):
        columns = slice(head * LANES, (head + 1) * LANES)
        grads = rope_back(dq_ref[head] * scale, cos_ref[...], sin_ref[...])
        gain_part, query_grad = unit_back(raw_ref[:, columns], gain_ref[...], grads)
        gain_total += gain_part
        query_in_ref[:, columns] = query_grad.astype(jnp.bfloat16)

    @pl.when(pl.program_id(0) == 0)
    def _():
        gain_grad_ref[...] = jnp.zeros_like(gain_grad_ref)

    gain_grad_ref[0:1] += gain_total


def attend_backward(
    index,
    batches,
    tables,
    out_in,
    w_out,
    query_low,
    gates,
    logs,
    attended,
    query_raw,
    cos_rows,
    sin_rows,
    gain,
    blocks,
    per_kv,
):
    need, query_mask, key_mask = tables
    all_rows, wide = query_low.shape
    rows = all_rows // batches
    shards = len(blocks)
    groups = wide // (per_kv * LANES)
    own = per_kv * LANES
    block, _ = tiles_of(rows)
    merged_spec = pl.BlockSpec((rows, own), lambda g, need: (index, g))
    table_spec = pl.BlockSpec((rows, LANES), lambda g, need: (index, 0))
    return pl.pallas_call(
        functools.partial(backward_kernel, shards, per_kv),
        grid_spec=pltpu.PrefetchScalarGridSpec(
            num_scalar_prefetch=1,
            grid=(groups,),
            in_specs=[
                whole_block(out_in.shape),
                pl.BlockSpec((None,) + w_out.shape[1:], lambda g, need: (g, 0, 0, 0)),
                merged_spec,
                whole_block(query_mask.shape),
                pl.BlockSpec((1, rows, LANES), lambda g, need: (g, index, 0)),
                whole_block(key_mask.shape),
                pl.BlockSpec((1, rows, LANES), lambda g, need: (g, 0, 0)),
                pl.BlockSpec((rows, own), lambda g, need: (0, g)),
                merged_spec,
                table_spec,
                table_spec,
                whole_block((1, LANES)),
            ]
            + [pl.BlockSpec((rows, LANES), lambda g, need: (0, g))] * shards
            + [pl.BlockSpec((rows, LANES), lambda g, need: (0, groups + g))] * shards,
            out_specs=[
                pl.BlockSpec((rows, own + LANES), lambda g, need: (0, g)),
                sum_block((8, LANES)),
            ]
            + [pl.BlockSpec((2, rows, LANES), lambda g, need: (0, 0, g))] * shards,
            scratch_shapes=[
                pltpu.VMEM((per_kv, rows, LANES), jnp.float32),
                pltpu.VMEM((block, LANES), jnp.float32),
                pltpu.VMEM((block, LANES), jnp.float32),
                pltpu.VMEM((per_kv, rows, 2 * LANES), jnp.bfloat16),
                pltpu.VMEM((per_kv, rows, 2 * LANES), jnp.bfloat16),
            ],
        ),
        out_shape=[
            jax.ShapeDtypeStruct((rows, groups * (own + LANES)), jnp.bfloat16),
            jax.ShapeDtypeStruct((8, LANES), jnp.float32),
        ]
        + [jax.ShapeDtypeStruct((2, rows, groups * LANES), jnp.bfloat16)] * shards,
        compiler_params=params(),
        cost_estimate=cost(
            14 * rows * rows * shards * wide,
            20 * rows * wide + 4 * shards * rows * wide,
            0.21,
        ),
        name="attend_backward",
    )(
        need,
        out_in,
        w_out,
        query_low,
        query_mask,
        gates,
        key_mask,
        logs,
        attended,
        query_raw,
        cos_rows,
        sin_rows,
        gain,
        *blocks,
        *blocks,
    )


def key_back_kernel(groups, raw_ref, cos_ref, sin_ref, gain_ref, grads_ref, out_ref, gain_grad_ref):
    gain_total = jnp.zeros((1, LANES), jnp.float32)
    for k in range(groups):
        columns = slice(k * LANES, (k + 1) * LANES)
        grads = rope_back(grads_ref[0, :, columns].astype(jnp.float32), cos_ref[...], sin_ref[...])
        gain_part, key_grad = unit_back(raw_ref[:, columns], gain_ref[...], grads)
        gain_total += gain_part
        out_ref[:, 2 * k * LANES : (2 * k + 1) * LANES] = key_grad.astype(jnp.bfloat16)
        out_ref[:, (2 * k + 1) * LANES : (2 * k + 2) * LANES] = grads_ref[1, :, columns]
    gain_grad_ref[...] = jnp.broadcast_to(gain_total, gain_grad_ref.shape)


def key_back(index, key_raw, cos_rows, sin_rows, gain, key_grad):
    _, rows, wide = key_grad.shape
    table_spec = pl.BlockSpec((rows, LANES), lambda m: (index, 0))
    return pl.pallas_call(
        functools.partial(key_back_kernel, wide // LANES),
        grid=(1,),
        in_specs=[
            pl.BlockSpec((rows, wide), lambda m: (index, 0)),
            table_spec,
            table_spec,
            sum_block((1, LANES)),
            sum_block(key_grad.shape),
        ],
        out_specs=[sum_block((rows, 2 * wide)), sum_block((8, LANES))],
        out_shape=[
            jax.ShapeDtypeStruct((rows, 2 * wide), jnp.bfloat16),
            jax.ShapeDtypeStruct((8, LANES), jnp.float32),
        ],
        compiler_params=params(),
        cost_estimate=cost(30 * rows * wide, 12 * rows * wide),
        name="key_back",
    )(key_raw, cos_rows, sin_rows, gain, key_grad)


def sum_kernel(count, transposed, *refs):
    lefts, rights, out_ref = refs[:count], refs[count : 2 * count], refs[2 * count]
    dot = dot_nt if transposed else dot_nn
    total = dot(lefts[0][...], rights[0][...])
    for left, right in zip(lefts[1:], rights[1:]):
        total += dot(left[...], right[...])
    out_ref[...] = total.astype(jnp.bfloat16)


def sum_of_products(rows, lefts, rights, transposed):
    def left_spec(place):
        _, depth, row_block, column_block = place
        return pl.BlockSpec(
            (rows, depth), lambda n: (row_block, column_block), pipeline_mode=pl.Buffered(1)
        )

    depth_total = sum(place[1] for place in lefts)
    if transposed:
        columns = rights[0].shape[0]
        block = min(512, columns)
        right_specs = [pl.BlockSpec((block, right.shape[1]), lambda n: (n, 0)) for right in rights]
    else:
        shards, _, part = rights[0].shape
        columns = shards * part
        block = min(256, part)
        per = part // block
        right_specs = [
            pl.BlockSpec((None, right.shape[1], block), lambda n: (n // per, 0, n % per))
            for right in rights
        ]
    return pl.pallas_call(
        functools.partial(sum_kernel, len(lefts), transposed),
        grid=(columns // block,),
        in_specs=[left_spec(place) for place in lefts] + right_specs,
        out_specs=pl.BlockSpec((rows, block), lambda n: (0, n)),
        out_shape=jax.ShapeDtypeStruct((rows, columns), jnp.bfloat16),
        compiler_params=params(),
        cost_estimate=cost(
            2 * rows * depth_total * columns,
            2 * depth_total * (rows + columns) + 2 * rows * columns,
        ),
        name="sum_of_products",
    )(*[place[0] for place in lefts], *rights)


def gradient_kernel(counts, sizes, arrivals, *refs):
    lefts, at = [], 0
    for count in counts:
        lefts.append(refs[at : at + count])
        at += count
    outs = refs[len(refs) - len(arrivals) :]
    for arrived_count, out_ref in zip(arrivals, outs):
        totals = []
        for term in lefts:
            rights = refs[at : at + len(term)]
            at += len(term)
            total = dot_tn(term[0][...], rights[0][...])
            for left, right in zip(term[1:], rights[1:]):
                total += dot_tn(left[...], right[...])
            totals.append(total)
        arrived = refs[at : at + arrived_count]
        at += arrived_count
        column = 0
        for total, size in zip(totals, sizes):
            span = slice(column, column + size)
            for item in arrived:
                total += item[:, span].astype(jnp.float32)
            out_ref[:, span] = total.astype(jnp.bfloat16)
            column += size


def weight_gradients(rows, lefts, sizes, parts):
    def right_spec(size, row_block, column_block):
        return pl.BlockSpec(
            (rows, size), lambda m: (row_block, column_block), pipeline_mode=pl.Buffered(1)
        )

    def left_spec(row_block):
        return pl.BlockSpec((rows, block), lambda m: (row_block, m))

    width = lefts[0][0][0].shape[1]
    block = min(512, width)
    total = sum(sizes)
    out_spec = pl.BlockSpec((block, total), lambda m: (m, 0))
    specs = [left_spec(place[1]) for term in lefts for place in term]
    operands = [place[0] for term in lefts for place in term]
    for rights, arrived in parts:
        for size, term in zip(sizes, rights):
            specs += [right_spec(size, place[1], place[2]) for place in term]
            operands += [place[0] for place in term]
        specs += [out_spec] * len(arrived)
        operands += list(arrived)
    depth = rows * max(len(term) for term in lefts)
    return pl.pallas_call(
        functools.partial(
            gradient_kernel,
            [len(term) for term in lefts],
            sizes,
            [len(arrived) for _, arrived in parts],
        ),
        grid=(width // block,),
        in_specs=specs,
        out_specs=[out_spec] * len(parts),
        out_shape=[jax.ShapeDtypeStruct((width, total), jnp.bfloat16)] * len(parts),
        compiler_params=params(),
        cost_estimate=cost(
            2 * len(parts) * depth * width * total, 2 * depth * width + 4 * len(parts) * width * total
        ),
        name="weight_gradients",
    )(*operands)


def split_dot_nt(left, rights):
    part = rights.shape[2]
    total = dot_nt(left[:, :part], rights[0])
    for index in range(1, rights.shape[0]):
        total += dot_nt(left[:, index * part : (index + 1) * part], rights[index])
    return total


def mlp_kernel(batches, count, down_in_ref, *refs):
    inputs = refs[:batches]
    pair_ws = refs[batches : batches + count]
    down_ws = refs[batches + count : batches + 2 * count]
    hiddens = refs[batches + 2 * count : batches + 3 * count]
    pair_ins = refs[batches + 3 * count :]
    block = hiddens[0].shape[1]
    for index in range(batches):

        @pl.when(pl.program_id(0) == index)
        def _(index=index):
            for k in range(count):
                gate_pre = dot_nn(inputs[index][...], pair_ws[k][:, :block])
                up_pre = dot_nn(inputs[index][...], pair_ws[k][:, block:])
                grad_hidden = split_dot_nt(down_in_ref[...], down_ws[k])
                sigmoid_gate = jax.nn.sigmoid(gate_pre)
                silu_gate = gate_pre * sigmoid_gate
                hiddens[k][...] = (silu_gate * up_pre).astype(jnp.bfloat16)
                pair_ins[k][:, block:] = (grad_hidden * silu_gate).astype(jnp.bfloat16)
                pair_ins[k][:, :block] = (
                    grad_hidden * up_pre * sigmoid_gate * (1.0 + gate_pre * (1.0 - sigmoid_gate))
                ).astype(jnp.bfloat16)


def mlp_units(inputs, down_in, pair_ws, down_ws):
    all_rows, width = down_in.shape
    batches, count = len(inputs), len(pair_ws)
    rows, units = all_rows // batches, pair_ws[0].shape[1] // 2
    return pl.pallas_call(
        functools.partial(mlp_kernel, batches, count),
        grid=(batches,),
        in_specs=[pl.BlockSpec((rows, width), lambda m: (m, 0))]
        + [whole_block(item.shape) for item in list(inputs) + pair_ws + down_ws],
        out_specs=[pl.BlockSpec((rows, units), lambda m: (m, 0))] * count
        + [pl.BlockSpec((rows, 2 * units), lambda m: (m, 0))] * count,
        out_shape=[jax.ShapeDtypeStruct((all_rows, units), jnp.bfloat16)] * count
        + [jax.ShapeDtypeStruct((all_rows, 2 * units), jnp.bfloat16)] * count,
        compiler_params=params(),
        cost_estimate=cost(
            6 * count * all_rows * width * units, 4 * all_rows * width + 6 * count * width * units
        ),
        name="mlp_units",
    )(down_in, *inputs, *pair_ws, *down_ws)


def add_norm_kernel(stream_ref, low_ref, other_ref, gain_ref, middle_ref, normed_ref):
    middle = (
        stream_ref[...].astype(jnp.float32)
        + (low_ref[...].astype(jnp.float32) + other_ref[...].astype(jnp.float32))
    )
    unit, _ = unit_of(middle)
    middle_ref[...] = middle
    normed_ref[...] = (unit * gain_ref[...]).astype(jnp.bfloat16)


def add_norm(index, stream, low_part, other_part, gain):
    rows, width = low_part.shape
    block = min(128, rows)
    first = index * (rows // block)
    spec = pl.BlockSpec((block, width), lambda m: (m, 0))
    return pl.pallas_call(
        add_norm_kernel,
        grid=(rows // block,),
        in_specs=[
            pl.BlockSpec((block, width), lambda m: (first + m, 0)),
            spec,
            spec,
            whole_block((1, width)),
        ],
        out_specs=[spec, spec],
        out_shape=[
            jax.ShapeDtypeStruct((rows, width), jnp.float32),
            jax.ShapeDtypeStruct((rows, width), jnp.bfloat16),
        ],
        compiler_params=params(),
        cost_estimate=cost(8 * rows * width, 12 * rows * width),
        name="add_norm",
    )(stream, low_part, other_part, gain)


def norm_back_kernel(values_ref, low_ref, other_ref, gain_ref, up_ref, *outs):
    grads = low_ref[...].astype(jnp.float32) + other_ref[...].astype(jnp.float32)
    gain_part, back = unit_back(values_ref[...].astype(jnp.float32), gain_ref[...], grads)
    total = up_ref[...].astype(jnp.float32) + back
    outs[0][...] = total.astype(jnp.bfloat16)
    for out_ref in outs[2:]:
        out_ref[...] = total

    @pl.when(pl.program_id(0) == 0)
    def _():
        outs[1][...] = jnp.zeros_like(outs[1])

    outs[1][0:1] += gain_part


def norm_back(values, values_at, low_part, other_part, gain, upstream, up_at, keep):
    rows, width = low_part.shape
    block = min(128, rows)
    steps = rows // block
    spec = pl.BlockSpec((block, width), lambda m: (m, 0))
    return pl.pallas_call(
        norm_back_kernel,
        grid=(steps,),
        in_specs=[
            pl.BlockSpec((block, width), lambda m: (values_at * steps + m, 0)),
            spec,
            spec,
            whole_block((1, width)),
            pl.BlockSpec((block, width), lambda m: (up_at * steps + m, 0)),
        ],
        out_specs=[spec, sum_block((8, width))] + [spec] * keep,
        out_shape=[
            jax.ShapeDtypeStruct((rows, width), jnp.bfloat16),
            jax.ShapeDtypeStruct((8, width), jnp.float32),
        ]
        + [jax.ShapeDtypeStruct((rows, width), jnp.float32)] * keep,
        compiler_params=params(),
        cost_estimate=cost(16 * rows * width, 16 * rows * width),
        name="norm_back",
    )(values, low_part, other_part, gain, upstream)


def order_kernel(per_quarter, turned, own_ref, *refs):
    pieces, out_ref = refs[:-1], refs[-1]
    step = pl.program_id(0)
    places = len(pieces) // per_quarter
    for index, piece in enumerate(pieces):

        @pl.when(step == index % places * per_quarter + index // places)
        def _(piece=piece):
            value = piece[...].astype(jnp.float32)
            out_ref[...] = value.T if turned else value


def in_order(chunks, block, column, turned=False):
    rows = chunks[0][0].shape[0]
    places, per_quarter = len(chunks[0]), len(chunks)
    own = lax.axis_index("replica").astype(jnp.int32).reshape(1)

    def out_of(step, own):
        place = step // per_quarter
        flip = jnp.where(place == 1, 2, jnp.where(place == 2, 1, place))
        at = jnp.bitwise_xor(own[0], flip) * per_quarter + step % per_quarter
        return (at, 0) if turned else (0, at)

    total = places * per_quarter * block
    pieces = [piece for chunk in chunks for piece in chunk]
    return pl.pallas_call(
        functools.partial(order_kernel, per_quarter, turned),
        grid_spec=pltpu.PrefetchScalarGridSpec(
            num_scalar_prefetch=1,
            grid=(places * per_quarter,),
            in_specs=[pl.BlockSpec((rows, block), lambda step, own: (0, column))] * len(pieces),
            out_specs=pl.BlockSpec((block, rows) if turned else (rows, block), out_of),
        ),
        out_shape=jax.ShapeDtypeStruct((total, rows) if turned else (rows, total), jnp.float32),
        compiler_params=params(),
        cost_estimate=cost(rows * total, 6 * rows * total),
        name="in_order",
    )(own, *pieces)


class Fold:
    def __init__(self, make_parts, far, far_end, direct):
        self.make_parts, self.far, self.far_end, self.direct = make_parts, far, far_end, direct

    def steps32(self):
        third, second = self.make_parts((3,), (2,))
        self.from_third, self.from_near = across(third, 1), across(second, 1)

    def step1(self):
        (part,) = self.make_parts((1, self.from_third))
        self.from_far = self.far.run(to_far, part)

    def step0(self):
        (part,) = self.make_parts((0, self.from_near, self.from_far))
        self.shard = scatter_rows(part)

    def steps10(self):
        first, own = self.make_parts((1, self.from_third), (0, self.from_near))
        self.far_shard, self.shard = scatter_rows(first), scatter_rows(own)

    def end(self):
        if self.direct:
            arrived = self.far_end.run(to_far, self.far_shard)
            total = self.shard.astype(jnp.float32) + arrived.astype(jnp.float32)
            self.shard = total.astype(jnp.bfloat16)
        return spread(self.shard, self.far_end)


class RelayBack:
    def __init__(self, parts):
        self.parts, self.steps = parts, []

    def advance(self, *earlier):
        at = len(self.parts) - 1 - len(self.steps)
        if at > 0:
            carry = self.steps[-1] if self.steps else self.parts[at]
            carry = after(carry, *earlier) if earlier else carry
            pairs = [(index, index - 1) for index in range(1, len(self.parts))]
            arrived = lax.ppermute(carry, "fsdp", pairs).astype(jnp.float32)
            total = self.parts[at - 1].astype(jnp.float32) + arrived
            self.steps.append(total.astype(jnp.bfloat16))
        return self.steps[-1]

    def finish(self):
        while len(self.steps) < len(self.parts) - 1:
            self.advance()
        return self.steps[-1]


def local(
    tokens,
    cotangent,
    lengths,
    parents,
    attn_gain,
    qk_gain,
    w_query,
    key_weight_matrix,
    value_weight_matrix,
    w_headgate,
    w_out,
    mlp_gain,
    w_gate,
    w_up,
    w_down,
):
    batches, rows, width = tokens.shape
    shards = lax.axis_size("fsdp")
    shard = lax.axis_index("fsdp")
    query_gain, key_gain = qk_gain[0, 0:1], qk_gain[0, 1:2]
    low = jnp.bfloat16

    query_piece = own_quarter(w_query[0], 1)
    head_piece = own_quarter(w_headgate[0], 1)
    per_kv = query_piece.shape[1] // LANES
    own = per_kv * LANES
    pad = jnp.zeros((query_piece.shape[0], LANES - head_piece.shape[1]), low)
    gate_piece, up_piece = own_quarter(w_gate[0], 1), own_quarter(w_up[0], 1)
    down_piece = own_quarter(w_down[0], 0)
    unit_block = min(256, gate_piece.shape[1])
    unit_blocks = gate_piece.shape[1] // unit_block
    def unit_span(value, block, axis):
        return lax.slice_in_dim(value, block * unit_block, (block + 1) * unit_block, axis=axis)

    far_in, far_out, far_end = Line(2), Line(2), Line(2)
    key_value_w = spread(
        gather_shards(
            jnp.concatenate(
                [own_quarter(key_weight_matrix[0], 1), own_quarter(value_weight_matrix[0], 1)],
                axis=1,
            ),
        ),
        far_in,
    )
    query_part = gather_shards(jnp.concatenate([query_piece, head_piece, pad], axis=1))
    out_part = gather_stacked(own_quarter(w_out[0], 0))
    groups = len(key_value_w)
    chunk_of = range(unit_blocks)

    tables, positions = [], []
    for index in range(batches):
        need, query_mask, key_mask, position = tree_need(
            lengths[index, 0], parents[index, 0], shard, rows, shards
        )
        tables.append((need, query_mask, key_mask))
        positions.append(position)
    half = LANES // 2
    frequency = THETA ** (-(jnp.arange(half, dtype=jnp.float32) * 2.0 / LANES))
    angle = jnp.concatenate(positions).astype(jnp.float32)[:, None] * frequency[None, :]
    cosine, sine = jnp.cos(angle), jnp.sin(angle)
    cos_rows = jnp.concatenate([cosine, cosine], axis=1)
    sin_rows = jnp.concatenate([-sine, sine], axis=1)

    core = Line(1)
    stream = tokens.reshape(batches * rows, width)
    down_in = cotangent.reshape(batches * rows, width)
    normed_low = (unit_of(stream.astype(jnp.float32))[0] * attn_gain).astype(low)
    key_value, key_raw = core.run(
        key_value_heads, normed_low, key_value_w, cos_rows, sin_rows, key_gain
    )
    query_w = spread(after(query_part, key_value), far_in)
    relays = [Relay(key_value[index * rows : (index + 1) * rows], shards) for index in range(batches)]
    for index, relay in enumerate(relays):
        if index > 0:
            relay.hold(relays[index - 1].latest)
        relay.advance()
    core.hold(*[relay.latest for relay in relays[1:]])
    query_low, query_raw, gates = core.run(
        query_heads, normed_low, query_w, cos_rows, sin_rows, query_gain, per_kv
    )
    out_w = jnp.stack(spread(after(out_part, key_value), far_in))
    for _ in range(2, shards):
        relays[0].advance()
    for index in range(1, batches):
        for step in range(2, shards - 1):
            relays[index].hold(query_low)
            relays[index].advance()
    blocks = [relay.blocks for relay in relays]
    tie = blocks[0][-1]
    pair_w, down_w, pair_parts = [], [], []
    for chunk in chunk_of:
        piece = jnp.concatenate(
            [unit_span(gate_piece, chunk, 1), unit_span(up_piece, chunk, 1)], axis=1
        )
        pair_parts.append(gather_shards(after(piece, tie, query_low, out_part)))
    down_part = gather_stacked(after(down_piece, tie, query_low, out_part))
    pair_parts[0] = after(pair_parts[0], blocks[0][-1])
    pair_w.append(spread(pair_parts[0], far_in))
    mixed, attended, logs, middle, mlp_low, parts = [], [], [], [], [], []
    for index in range(batches):
        tree_mixed, tree_out, tree_log = core.run(
            lambda query: attend_forward(
                index, batches, tables[index], query, gates, blocks[index], per_kv
            ),
            query_low,
        )
        for relay in relays:
            relay.hold(tree_mixed)
            relay.advance()
        mixed.append(tree_mixed)
        attended.append(tree_out)
        logs.append(tree_log)
        part = core.run(
            lambda left: sum_of_products(
                rows,
                [(left, own, 0, k) for k in range(groups)],
                [out_w[k] for k in range(groups)],
                False,
            ),
            tree_mixed,
        )
        parts.append((part, tensor_other(part)))
    down_part = after(down_part, part)
    for chunk in chunk_of:
        down_w.append(spread(unit_span(down_part, chunk, 1), far_in))
    for item in pair_parts[1:]:
        pair_w.append(spread(after(item, part), far_in))
    for index in range(batches):
        core.hold(pair_w[0][1], down_w[min(index, unit_blocks - 1)][1])
        tree_middle, tree_normed = core.run(
            lambda part: add_norm(index, stream, part, parts[index][1], mlp_gain), parts[index][0]
        )
        middle.append(tree_middle)
        mlp_low.append(tree_normed)

    hidden = [[None] * groups for _ in chunk_of]
    pair_in = [[None] * groups for _ in chunk_of]

    def do_units(chunk, members):
        made = core.run(
            lambda upstream: mlp_units(
                mlp_low,
                upstream,
                [pair_w[chunk][k] for k in members],
                [down_w[chunk][k] for k in members],
            ),
            down_in,
        )
        for place, k in enumerate(members):
            hidden[chunk][k], pair_in[chunk][k] = made[place], made[len(members) + place]

    def fold(lefts, sizes, rights_of, direct=False):
        def make_parts(*wanted):
            def work(first):
                own_lefts = [[(first,) + lefts[0][0][1:]] + lefts[0][1:]] + lefts[1:]
                parts = [(rights_of(k), arrived) for k, *arrived in wanted]
                return weight_gradients(rows, own_lefts, sizes, parts)

            return core.run(work, lefts[0][0][0])

        return Fold(make_parts, far_out, far_end, direct)

    def both(value, column=0):
        return [(value, index, column) for index in range(batches)]

    def apart(values, column=0):
        return [(value, 0, column) for value in values]

    unit_folds = [
        fold(
            [apart(mlp_low), both(down_in)],
            [2 * unit_block, unit_block],
            lambda k, c=c: [both(pair_in[c][k]), both(hidden[c][k])],
            direct=c == 0,
        )
        for c in chunk_of
    ]

    middle_parts = []

    def do_middle_part(index):
        part = core.run(
            lambda left: sum_of_products(
                rows,
                [
                    (left if (c, k) == (0, 0) else pair_in[c][k], 2 * unit_block, index, 0)
                    for c in chunk_of
                    for k in range(groups)
                ],
                [pair_w[c][k] for c in chunk_of for k in range(groups)],
                True,
            ),
            pair_in[0][0],
        )
        middle_parts.append((part, tensor_other(part)))

    mlp_gain_grad, grad_middle, out_in = [], [], []
    query_in, query_gain_grad, relays_back = [], [], []

    def do_norm_back(index):
        low_out, gain_part, full = core.run(
            lambda part: norm_back(
                middle[index], 0, part, middle_parts[index][1], mlp_gain, down_in, index, 1
            ),
            middle_parts[index][0],
        )
        out_in.append(low_out)
        mlp_gain_grad.append(gain_part)
        grad_middle.append(full)

    def do_attention_back(index):
        tree_in, gain_part, *grads = core.run(
            lambda upstream: attend_backward(
                index,
                batches,
                tables[index],
                upstream,
                out_w,
                query_low,
                gates,
                logs[index],
                attended[index],
                query_raw,
                cos_rows,
                sin_rows,
                query_gain,
                blocks[index],
                per_kv,
            ),
            out_in[index],
        )
        query_in.append(tree_in)
        query_gain_grad.append(gain_part)
        relays_back.append(RelayBack(grads))
        relays_back[-1].advance()

    result_parts = []

    def do_result_part(index):
        part = core.run(
            lambda left: sum_of_products(
                rows,
                [
                    (left if (c, k) == (0, 0) else hidden[c][k], unit_block, index, 0)
                    for c in chunk_of
                    for k in range(groups)
                ],
                [down_w[c][k] for c in chunk_of for k in range(groups)],
                False,
            ),
            hidden[0][0],
        )
        result_parts.append((part, tensor_other(part)))

    final = unit_blocks - 1
    for chunk in chunk_of:
        if chunk > 0:
            core.hold(pair_w[chunk][1])
        do_units(chunk, (0, 2))
        if chunk > 0:
            previous = unit_folds[chunk - 1]
            previous.steps10() if previous.direct else previous.step1()
            core.hold(pair_parts[-1])
        else:
            core.hold(down_w[-1][1])
        do_units(chunk, (1, 3))
        unit_folds[chunk].steps32()
    do_middle_part(0)
    if unit_folds[final].direct:
        unit_folds[final].steps10()
    else:
        unit_folds[final].step1()
    for index in range(1, batches):
        do_middle_part(index)
    waiting = [item for item in unit_folds if not item.direct]
    do_norm_back(0)
    for item in waiting[:-1]:
        item.step0()
    do_attention_back(0)
    core.hold(*[item.from_far for item in waiting[-1:]])
    for index in range(1, batches):
        do_norm_back(index)
    do_result_part(0)
    core.hold(relays_back[0].steps[0])
    for item in waiting[-1:]:
        item.step0()
    unit_ends = [unit_folds[0].end()]
    for index in range(1, batches):
        do_result_part(index)
    core.hold(relays_back[0].advance(), result_parts[0][1])
    for index in range(1, batches):
        do_attention_back(index)
    query_block = own + LANES
    wide_fold = fold(
        [apart(out_in), both(normed_low)],
        [own, query_block],
        lambda k: [apart(mixed, k), apart(query_in, k)],
    )
    wide_fold.steps32()
    wide_fold.step1()
    for relay in relays_back[1:]:
        relay.advance(core.sent[-1])
    key_block = 2 * LANES
    key_in, key_gain_grad, stream_parts = [], [], []

    def do_key_back(index):
        tree_in, gain_part = core.run(
            lambda raw: key_back(
                index, raw, cos_rows, sin_rows, key_gain, relays_back[index].finish()
            ),
            key_raw,
        )
        key_in.append(tree_in)
        key_gain_grad.append(gain_part)

    def do_stream_part(index):
        part = core.run(
            lambda left: sum_of_products(
                rows,
                [(query_in[index], query_block, 0, k) for k in range(groups)]
                + [(left, key_block, 0, k) for k in range(groups)],
                query_w + key_value_w,
                True,
            ),
            key_in[index],
        )
        stream_parts.append((part, tensor_other(part)))

    attn_gain_grad, input_grad = [], []

    def do_stream_back(index):
        part, other = stream_parts[index]
        low_out, gain_part = core.run(
            lambda part: norm_back(
                stream, index, part, other, attn_gain, grad_middle[index], 0, 0
            ),
            part,
        )
        input_grad.append(low_out)
        attn_gain_grad.append(gain_part)

    do_key_back(0)
    unit_ends += [item.end() for item in unit_folds[1:]]
    for pieces in unit_ends:
        core.hold(pieces[1], pieces[3])
    do_stream_part(0)
    core.hold(*[part[1] for part in result_parts])

    def do_order(column):
        return core.run(
            lambda first: in_order(
                [[first] + unit_ends[0][1:]] + unit_ends[1:], unit_block, column, column == 2
            ),
            unit_ends[0][0],
        )

    gate_order = do_order(0)
    for index in range(1, batches):
        do_key_back(index)
    key_fold = fold([both(normed_low)], [key_block], lambda k: [apart(key_in, k)])
    key_fold.steps32()
    core.hold(wide_fold.from_far)
    for index in range(1, batches):
        do_stream_part(index)
    key_fold.step1()
    core.hold(stream_parts[0][1])
    wide_fold.step0()
    up_order = do_order(1)
    do_stream_back(0)
    core.hold(stream_parts[-1][1])
    key_fold.step0()
    down_order = do_order(2)
    for index in range(1, batches):
        do_stream_back(index)
    results = [
        (
            middle[index]
            + (part.astype(jnp.float32) + other.astype(jnp.float32))
        ).astype(low)
        for index, (part, other) in enumerate(result_parts)
    ]
    wide_shards = wide_fold.end()
    key_shards = key_fold.end()
    query_sum, key_sum = [
        jnp.sum(jnp.stack(items), axis=0)[0] for items in (query_gain_grad, key_gain_grad)
    ]
    wide_sums = [
        jnp.sum(jnp.stack(items), axis=0)[0] for items in (attn_gain_grad, mlp_gain_grad)
    ]
    gain_sum = axis_sum(
        axis_sum(jnp.concatenate(wide_sums + [query_sum, key_sum]), "replica"), "fsdp"
    )
    head_sum = axis_sum(gain_sum[2 * width :], "tensor")

    def own_slice(value, axis):
        size = value.shape[axis] // shards
        return lax.dynamic_slice_in_dim(value, shard * size, size, axis)[None]

    gate_count = head_piece.shape[1]
    gate_grad = in_order([wide_shards], LANES, 2 * per_kv)
    gate_grad = gate_grad.reshape(gate_grad.shape[0], groups, LANES)[:, :, :gate_count]
    return (
        jnp.stack(results),
        jnp.stack(input_grad),
        own_slice(gain_sum[:width], 0),
        own_slice(head_sum.reshape(2, LANES), 1),
        in_order([wide_shards], own, 1)[None],
        in_order([key_shards], LANES, 0)[None],
        in_order([key_shards], LANES, 1)[None],
        gate_grad.reshape(1, gate_grad.shape[0], groups * gate_count),
        in_order([wide_shards], own, 0, turned=True)[None],
        own_slice(gain_sum[width : 2 * width], 0),
        gate_order[None],
        up_order[None],
        down_order[None],
    )


def solution(mesh):
    placed = (
        P(None, ("replica", "fsdp"), None),
        P(None, ("replica", "fsdp"), None),
        P(None, "replica", None),
        P(None, "replica", None),
        P(),
        P(),
        P(None, "fsdp", "tensor"),
        P(None, "fsdp", "tensor"),
        P(None, "fsdp", "tensor"),
        P(None, "fsdp", "tensor"),
        P(None, "tensor", "fsdp"),
        P(),
        P(None, "fsdp", "tensor"),
        P(None, "fsdp", "tensor"),
        P(None, "tensor", "fsdp"),
    )
    return jax.shard_map(
        local,
        mesh=mesh,
        in_specs=placed,
        out_specs=(
            P(None, ("replica", "fsdp"), None),
            P(None, ("replica", "fsdp"), None),
            P(None, "fsdp"),
            P(None, None, "fsdp"),
            P(None, "fsdp", "tensor"),
            P(None, "fsdp", "tensor"),
            P(None, "fsdp", "tensor"),
            P(None, "fsdp", "tensor"),
            P(None, "tensor", "fsdp"),
            P(None, "fsdp"),
            P(None, "fsdp", "tensor"),
            P(None, "fsdp", "tensor"),
            P(None, "tensor", "fsdp"),
        ),
        check_vma=False,
    )
```

```python
import functools

import jax
import jax.numpy as jnp
from jax import lax
from jax.experimental import pallas as pl
from jax.experimental.pallas import tpu as pltpu
from jax.sharding import PartitionSpec as P

EPSILON = 1e-06
THETA = 1000000.0
LOG2_E = 1.4426950408889634
LANES = 128
EXTRA_AT = 16
VMEM_BYTES = 58 * 1024 * 1024
COST_SHARE = 0.22


def segment_table(lengths, parents):
    count = lengths.shape[0]
    starts = jnp.cumsum(lengths) - lengths
    labels = jnp.arange(count, dtype=jnp.int32)
    parent_hot = (parents[:, None] == labels[None, :]).astype(jnp.int32)
    grand_hot = jnp.dot(parent_hot, parent_hot)
    eye_hot = (labels[:, None] == labels[None, :]).astype(jnp.int32)
    ancestor = (eye_hot + parent_hot + grand_hot > 0).astype(jnp.int32)
    before = jnp.sum(ancestor * (1 - eye_hot) * lengths[None, :], axis=1)
    return (starts, before - starts, ancestor)


def row_segments(indices, starts, count):
    labels = jnp.arange(count, dtype=jnp.int32)
    member = jnp.sum((indices[:, None] >= starts[None, :]).astype(jnp.int32), axis=1) - 1
    return (member[:, None] == labels[None, :]).astype(jnp.int32)


def swaps(bit, count):
    return [(index, index ^ bit) for index in range(count)]


def across(value, bit):
    return lax.ppermute(value, "replica", swaps(bit, lax.axis_size("replica")))


def own_quarter(shard, axis):
    size = shard.shape[axis] // lax.axis_size("replica")
    return lax.dynamic_slice_in_dim(shard, lax.axis_index("replica") * size, size, axis)


def spread(block):
    other = across(block, 2)
    return [block, other, across(block, 1), across(other, 1)]


def after(value, *earlier):
    return lax.optimization_barrier((value, *earlier))[0] if earlier else value


class Line:
    def __init__(self, depth):
        self.depth = depth
        self.sent = []
        self.held = []

    def before(self):
        last = [self.sent[-self.depth]] if len(self.sent) >= self.depth else []
        held, self.held = self.held, []
        return last + held

    def hold(self, *values):
        self.held += values

    def run(self, function, value, *rest):
        result = function(after(value, *self.before()), *rest)
        self.sent.append(result[0] if isinstance(result, (list, tuple)) else result)
        return result


def gather_shards(value):
    return lax.all_gather(value, "fsdp", axis=0, tiled=True)


def gather_stacked(value):
    return lax.all_gather(value, "fsdp", axis=0, tiled=False)


def scatter_rows(value):
    return lax.psum_scatter(value, "fsdp", scatter_dimension=0, tiled=True)


def to_far(value):
    return across(value, 2)


def spread(block, far_line):
    other = far_line.run(to_far, block)
    return [block, other, across(block, 1), across(other, 1)]


def axis_sum(value, axis):
    size, bit = lax.axis_size(axis), 1
    while bit < size:
        if bit * 4 <= size:
            near, far, both = [
                lax.ppermute(value, axis, swaps(bit * flip, size)) for flip in (1, 2, 3)
            ]
            value, bit = (value + near) + (far + both), bit * 4
        else:
            value, bit = value + lax.ppermute(value, axis, swaps(bit, size)), bit * 2
    return value


def tensor_other(low_part):
    return lax.ppermute(low_part, "tensor", swaps(1, lax.axis_size("tensor")))


class Relay:
    def __init__(self, block, count):
        self.blocks, self.count, self.held = [block], count, []
        self.latest = block

    def hold(self, *values):
        self.held += values

    def advance(self):
        if len(self.blocks) < self.count:
            value = after(self.blocks[-1], *self.held) if self.held else self.blocks[-1]
            self.held = []
            pairs = [(index, index + 1) for index in range(self.count - 1)]
            self.blocks.append(lax.ppermute(value, "fsdp", pairs))
            self.latest = self.blocks[-1]


def params():
    return pltpu.CompilerParams(vmem_limit_bytes=VMEM_BYTES)


def cost(flops, moved, rate=0.56):
    return pl.CostEstimate(
        flops=int(flops * COST_SHARE / rate),
        bytes_accessed=int(moved * COST_SHARE / 0.6),
        transcendentals=0,
    )


def whole_block(shape):
    return pl.BlockSpec(shape, lambda *index: (0,) * len(shape), pipeline_mode=pl.Buffered(1))


def sum_block(shape):
    return pl.BlockSpec(shape, lambda *index: (0,) * len(shape))


def dot_nn(left, right):
    return jnp.dot(left, right, preferred_element_type=jnp.float32)


def dot_nt(left, right):
    return lax.dot_general(
        left, right, (((1,), (1,)), ((), ())), preferred_element_type=jnp.float32
    )


def dot_tn(left, right):
    return lax.dot_general(
        left, right, (((0,), (0,)), ((), ())), preferred_element_type=jnp.float32
    )


def three_parts(value):
    first = value.astype(jnp.bfloat16)
    rest = value - first.astype(jnp.float32)
    second = rest.astype(jnp.bfloat16)
    third = (rest - second.astype(jnp.float32)).astype(jnp.bfloat16)
    return (first, second, third)


def put_lanes(base, parts):
    lane = lax.broadcasted_iota(jnp.int32, base.shape, 1)
    value = base.astype(jnp.float32)
    for offset, part in enumerate(parts):
        value = jnp.where(lane == EXTRA_AT + offset, part.astype(jnp.float32), value)
    return value.astype(jnp.bfloat16)


def rope(values, cos_rows, sin_rows):
    return values * cos_rows + pltpu.roll(values, LANES // 2, 1) * sin_rows


def rope_back(grads, cos_rows, sin_rows):
    return grads * cos_rows - pltpu.roll(grads, LANES // 2, 1) * sin_rows


def unit_of(raw):
    inverse = lax.rsqrt(jnp.mean(raw * raw, axis=-1, keepdims=True) + EPSILON)
    return (raw * inverse, inverse)


def unit_back(raw, gain, grads):
    unit, inverse = unit_of(raw)
    scaled = grads * gain
    gain_part = jnp.sum(grads * unit, axis=0, keepdims=True)
    return (
        gain_part,
        inverse * (scaled - unit * jnp.mean(scaled * unit, axis=-1, keepdims=True)),
    )


def key_value_kernel(groups, x_ref, cos_ref, sin_ref, gain_ref, *refs):
    weights, (kv_ref, raw_ref) = refs[:groups], refs[groups:]
    for k in range(groups):
        part = dot_nn(x_ref[...], weights[k][...])
        raw = part[:, :LANES]
        unit, _ = unit_of(raw)
        raw_ref[:, k * LANES : (k + 1) * LANES] = raw
        kv_ref[:, k * LANES : (k + 1) * LANES] = rope(
            unit * gain_ref[...], cos_ref[...], sin_ref[...]
        ).astype(jnp.bfloat16)
        at = (groups + k) * LANES
        kv_ref[:, at : at + LANES] = part[:, LANES:].astype(jnp.bfloat16)


def key_value_heads(normed_low, weights, cos_rows, sin_rows, gain):
    rows, width = normed_low.shape
    groups, block = len(weights), min(256, rows)
    return pl.pallas_call(
        functools.partial(key_value_kernel, groups),
        grid=(rows // block,),
        in_specs=[
            pl.BlockSpec((block, width), lambda m: (m, 0)),
            pl.BlockSpec((block, LANES), lambda m: (m, 0)),
            pl.BlockSpec((block, LANES), lambda m: (m, 0)),
            whole_block((1, LANES)),
        ]
        + [whole_block(weight.shape) for weight in weights],
        out_specs=[
            pl.BlockSpec((block, 2 * groups * LANES), lambda m: (m, 0)),
            pl.BlockSpec((block, groups * LANES), lambda m: (m, 0)),
        ],
        out_shape=[
            jax.ShapeDtypeStruct((rows, 2 * groups * LANES), jnp.bfloat16),
            jax.ShapeDtypeStruct((rows, groups * LANES), jnp.float32),
        ],
        compiler_params=params(),
        cost_estimate=cost(4 * rows * width * groups * LANES, 4 * rows * width),
        name="key_value_heads",
    )(normed_low, cos_rows, sin_rows, gain, *weights)


def query_kernel(groups, per_kv, x_ref, cos_ref, sin_ref, gain_ref, *refs):
    weights, (low_ref, raw_ref, gate_ref) = refs[:groups], refs[groups:]
    for k in range(groups):
        part = dot_nn(x_ref[...], weights[k][...])
        for head in range(per_kv):
            raw = part[:, head * LANES : (head + 1) * LANES]
            unit, _ = unit_of(raw)
            at = (k * per_kv + head) * LANES
            raw_ref[:, at : at + LANES] = raw
            low_ref[:, at : at + LANES] = rope(
                unit * gain_ref[...], cos_ref[...], sin_ref[...]
            ).astype(jnp.bfloat16)
        gate_ref[k] = jax.nn.sigmoid(part[:, per_kv * LANES :])


def query_heads(normed_low, weights, cos_rows, sin_rows, gain, per_kv):
    rows, width = normed_low.shape
    groups, block = len(weights), min(256, rows)
    wide = groups * per_kv * LANES
    return pl.pallas_call(
        functools.partial(query_kernel, groups, per_kv),
        grid=(rows // block,),
        in_specs=[
            pl.BlockSpec((block, width), lambda m: (m, 0)),
            pl.BlockSpec((block, LANES), lambda m: (m, 0)),
            pl.BlockSpec((block, LANES), lambda m: (m, 0)),
            whole_block((1, LANES)),
        ]
        + [whole_block(weight.shape) for weight in weights],
        out_specs=[
            pl.BlockSpec((block, wide), lambda m: (m, 0)),
            pl.BlockSpec((block, wide), lambda m: (m, 0)),
            pl.BlockSpec((groups, block, LANES), lambda m: (0, m, 0)),
        ],
        out_shape=[
            jax.ShapeDtypeStruct((rows, wide), jnp.bfloat16),
            jax.ShapeDtypeStruct((rows, wide), jnp.float32),
            jax.ShapeDtypeStruct((groups, rows, LANES), jnp.float32),
        ],
        compiler_params=params(),
        cost_estimate=cost(2 * rows * width * groups * (per_kv + 1) * LANES, 4 * rows * width),
        name="query_heads",
    )(normed_low, cos_rows, sin_rows, gain, *weights)


def tiles_of(row_count):
    block = min(256, row_count)
    return (block, row_count // block)


def tree_need(lengths, parents, shard, row_count, shards):
    count = lengths.shape[0]
    starts, offsets, ancestor = segment_table(lengths, parents)
    block, tiles = tiles_of(row_count)
    query_index = shard * row_count + jnp.arange(row_count, dtype=jnp.int32)
    query_hot = row_segments(query_index, starts, count)
    reach = jnp.sum(query_hot[:, :, None] * ancestor[None, :, :], axis=1)
    position = query_index + jnp.sum(query_hot * offsets[None, :], axis=1)
    back = jnp.arange(shards, dtype=jnp.int32)[:, None]
    key_index = (shard - back) * row_count + jnp.arange(row_count, dtype=jnp.int32)[None, :]
    key_hot = row_segments(key_index.reshape(-1), starts, count)
    query_has = jnp.max(reach.reshape(tiles, block, count), axis=1)
    key_has = jnp.max(key_hot.reshape(shards, tiles, block, count), axis=2)
    need = jnp.sum(query_has[:, None, None, :] * key_has[None], axis=-1) > 0
    wall = jnp.where(reach > 0, 0.0, -1e30)
    query_mask = jnp.pad(wall, ((0, 0), (0, LANES - count))).astype(jnp.bfloat16)
    lane = jnp.arange(LANES)[None, :]
    ones = ((lane >= EXTRA_AT) & (lane < EXTRA_AT + 3)).astype(jnp.float32)
    key_mask = jnp.pad(key_hot.astype(jnp.float32), ((0, 0), (0, LANES - count))) + ones
    return (need.astype(jnp.int32).reshape(-1), query_mask, key_mask.astype(jnp.bfloat16), position)


def forward_kernel(
    shards, per_kv, factor, need_ref, q_ref, qmask_ref, gate_ref, kmask_ref, *refs
):
    keys, values = refs[:shards], refs[shards : 2 * shards]
    mixed_ref, attended_ref, log_ref, total_ref = refs[-4:]
    rows = q_ref.shape[0]
    block, tiles = tiles_of(rows)
    lane = lax.broadcasted_iota(jnp.int32, (block, LANES), 1)
    for qi in range(tiles):
        span = slice(qi * block, (qi + 1) * block)
        total_ref[...] = jnp.zeros_like(total_ref)
        for shard in range(shards):
            for ci in range(tiles):
                if shard == 0 and ci > qi:
                    continue
                part = slice(ci * block, (ci + 1) * block)

                @pl.when(need_ref[(qi * shards + shard) * tiles + ci] > 0)
                def _(shard=shard, ci=ci, part=part):
                    at = shard * rows + ci * block
                    key_mask = kmask_ref[at : at + block]
                    key_wide = jnp.concatenate([keys[shard][part], key_mask], axis=1)
                    value_wide = jnp.concatenate(
                        [values[shard][part], jnp.ones((block, LANES), jnp.bfloat16)], axis=1
                    )
                    for head in range(per_kv):
                        query_wide = jnp.concatenate(
                            [q_ref[span, head * LANES : (head + 1) * LANES], qmask_ref[span]],
                            axis=1,
                        )
                        scores = dot_nt(query_wide, key_wide)
                        if shard == 0 and ci == qi:
                            row = lax.broadcasted_iota(jnp.int32, (block, block), 0)
                            column = lax.broadcasted_iota(jnp.int32, (block, block), 1)
                            scores = jnp.where(column <= row, scores, -1e30)
                        weights = jnp.exp2(scores * factor).astype(jnp.bfloat16)
                        total_ref[head] += dot_nn(weights, value_wide)

        logs = jnp.zeros((block, LANES), jnp.float32)
        for head in range(per_kv):
            summed = total_ref[head][:, LANES:]
            tree_out = total_ref[head][:, :LANES] / summed
            columns = slice(head * LANES, (head + 1) * LANES)
            attended_ref[span, columns] = tree_out
            gate = gate_ref[0, span, head : head + 1]
            mixed_ref[span, columns] = (gate * tree_out).astype(jnp.bfloat16)
            logs = jnp.where(lane == head, jnp.log(summed), logs)
        log_ref[0, span] = logs


def attend_forward(index, batches, tables, query_low, gates, blocks, per_kv):
    need, query_mask, key_mask = tables
    all_rows, wide = query_low.shape
    rows = all_rows // batches
    shards = len(blocks)
    groups = wide // (per_kv * LANES)
    own = per_kv * LANES
    block, _ = tiles_of(rows)
    tree_spec = pl.BlockSpec((rows, own), lambda g, need: (0, g))
    log_spec = pl.BlockSpec((1, rows, LANES), lambda g, need: (g, 0, 0))
    return pl.pallas_call(
        functools.partial(forward_kernel, shards, per_kv, LANES ** (-0.5) * LOG2_E),
        grid_spec=pltpu.PrefetchScalarGridSpec(
            num_scalar_prefetch=1,
            grid=(groups,),
            in_specs=[
                pl.BlockSpec((rows, own), lambda g, need: (index, g)),
                whole_block(query_mask.shape),
                pl.BlockSpec((1, rows, LANES), lambda g, need: (g, index, 0)),
                whole_block(key_mask.shape),
            ]
            + [pl.BlockSpec((rows, LANES), lambda g, need: (0, g))] * shards
            + [pl.BlockSpec((rows, LANES), lambda g, need: (0, groups + g))] * shards,
            out_specs=[tree_spec, tree_spec, log_spec],
            scratch_shapes=[pltpu.VMEM((per_kv, block, 2 * LANES), jnp.float32)],
        ),
        out_shape=[
            jax.ShapeDtypeStruct((rows, wide), jnp.bfloat16),
            jax.ShapeDtypeStruct((rows, wide), jnp.float32),
            jax.ShapeDtypeStruct((groups, rows, LANES), jnp.float32),
        ],
        compiler_params=params(),
        cost_estimate=cost(
            4 * rows * rows * shards * wide,
            8 * rows * wide + 2 * shards * rows * wide,
            0.19,
        ),
        name="attend_forward",
    )(need, query_low, query_mask, gates, key_mask, *blocks, *blocks)


def backward_kernel(
    shards,
    per_kv,
    need_ref,
    out_in_ref,
    w_out_ref,
    q_ref,
    qmask_ref,
    gate_ref,
    kmask_ref,
    log_ref,
    attended_ref,
    raw_ref,
    cos_ref,
    sin_ref,
    gain_ref,
    *refs,
):
    scale = LANES ** (-0.5)
    factor = scale * LOG2_E
    keys, values = refs[:shards], refs[shards : 2 * shards]
    query_in_ref, gain_grad_ref = refs[2 * shards : 2 * shards + 2]
    block_grads = refs[2 * shards + 2 : 3 * shards + 2]
    dq_ref, dk_ref, dv_ref, qwide_ref, dwide_ref = refs[3 * shards + 2 :]
    rows = q_ref.shape[0]
    block, tiles = tiles_of(rows)
    grad_mixed = split_dot_nt(out_in_ref[...], w_out_ref)
    lane = lax.broadcasted_iota(jnp.int32, (rows, LANES), 1)
    logits = jnp.zeros((rows, LANES), jnp.float32)
    for head in range(per_kv):
        columns = slice(head * LANES, (head + 1) * LANES)
        attended = attended_ref[:, columns]
        gate = gate_ref[0, :, head : head + 1]
        mixed_grad = grad_mixed[:, columns]
        logit = jnp.sum(mixed_grad * attended, axis=-1, keepdims=True) * gate * (1.0 - gate)
        logits = jnp.where(lane == head, logit, logits)
        attended_in = (mixed_grad * gate).astype(jnp.bfloat16)
        delta = jnp.sum(attended_in.astype(jnp.float32) * attended, axis=-1, keepdims=True)
        dwide_ref[head, :, :LANES] = attended_in
        dwide_ref[head, :, LANES:] = put_lanes(
            jnp.zeros((rows, LANES), jnp.bfloat16), three_parts(-delta)
        )
        qwide_ref[head, :, :LANES] = q_ref[:, columns]
        qwide_ref[head, :, LANES:] = put_lanes(
            qmask_ref[...], three_parts(log_ref[0, :, head : head + 1] * (-1.0 / scale))
        )
    query_in_ref[:, per_kv * LANES :] = logits.astype(jnp.bfloat16)
    dq_ref[...] = jnp.zeros_like(dq_ref)
    for shard in range(shards):
        for ci in range(tiles):
            part = slice(ci * block, (ci + 1) * block)
            at = shard * rows + ci * block
            dk_ref[...] = jnp.zeros_like(dk_ref)
            dv_ref[...] = jnp.zeros_like(dv_ref)
            for qi in range(tiles):
                if shard == 0 and ci > qi:
                    continue
                span = slice(qi * block, (qi + 1) * block)

                @pl.when(need_ref[(qi * shards + shard) * tiles + ci] > 0)
                def _(shard=shard, ci=ci, qi=qi, at=at, part=part, span=span):
                    key_low = keys[shard][part]
                    key_mask = kmask_ref[at : at + block]
                    key_wide = jnp.concatenate([key_low, key_mask], axis=1)
                    value_wide = jnp.concatenate([values[shard][part], key_mask], axis=1)
                    for head in range(per_kv):
                        scores = dot_nt(key_wide, qwide_ref[head, span])
                        if shard == 0 and ci == qi:
                            row = lax.broadcasted_iota(jnp.int32, (block, block), 0)
                            column = lax.broadcasted_iota(jnp.int32, (block, block), 1)
                            scores = jnp.where(row <= column, scores, -1e30)
                        weights = jnp.exp2(scores * factor)
                        change = dot_nt(value_wide, dwide_ref[head, span])
                        grad_scores = (weights * change).astype(jnp.bfloat16)
                        weights = weights.astype(jnp.bfloat16)
                        dv_ref[...] += dot_nn(weights, dwide_ref[head, span, :LANES])
                        dk_ref[...] += dot_nn(grad_scores, qwide_ref[head, span, :LANES])
                        dq_ref[head, span] += dot_tn(grad_scores, key_low)

            block_grads[shard][0, part] = (dk_ref[...] * scale).astype(jnp.bfloat16)
            block_grads[shard][1, part] = dv_ref[...].astype(jnp.bfloat16)
    gain_total = jnp.zeros((1, LANES), jnp.float32)
    for head in range(per_kv):
        columns = slice(head * LANES, (head + 1) * LANES)
        grads = rope_back(dq_ref[head] * scale, cos_ref[...], sin_ref[...])
        gain_part, query_grad = unit_back(raw_ref[:, columns], gain_ref[...], grads)
        gain_total += gain_part
        query_in_ref[:, columns] = query_grad.astype(jnp.bfloat16)

    @pl.when(pl.program_id(0) == 0)
    def _():
        gain_grad_ref[...] = jnp.zeros_like(gain_grad_ref)

    gain_grad_ref[0:1] += gain_total


def attend_backward(
    index,
    batches,
    tables,
    out_in,
    w_out,
    query_low,
    gates,
    logs,
    attended,
    query_raw,
    cos_rows,
    sin_rows,
    gain,
    blocks,
    per_kv,
):
    need, query_mask, key_mask = tables
    all_rows, wide = query_low.shape
    rows = all_rows // batches
    shards = len(blocks)
    groups = wide // (per_kv * LANES)
    own = per_kv * LANES
    block, _ = tiles_of(rows)
    merged_spec = pl.BlockSpec((rows, own), lambda g, need: (index, g))
    table_spec = pl.BlockSpec((rows, LANES), lambda g, need: (index, 0))
    return pl.pallas_call(
        functools.partial(backward_kernel, shards, per_kv),
        grid_spec=pltpu.PrefetchScalarGridSpec(
            num_scalar_prefetch=1,
            grid=(groups,),
            in_specs=[
                whole_block(out_in.shape),
                pl.BlockSpec((None,) + w_out.shape[1:], lambda g, need: (g, 0, 0, 0)),
                merged_spec,
                whole_block(query_mask.shape),
                pl.BlockSpec((1, rows, LANES), lambda g, need: (g, index, 0)),
                whole_block(key_mask.shape),
                pl.BlockSpec((1, rows, LANES), lambda g, need: (g, 0, 0)),
                pl.BlockSpec((rows, own), lambda g, need: (0, g)),
                merged_spec,
                table_spec,
                table_spec,
                whole_block((1, LANES)),
            ]
            + [pl.BlockSpec((rows, LANES), lambda g, need: (0, g))] * shards
            + [pl.BlockSpec((rows, LANES), lambda g, need: (0, groups + g))] * shards,
            out_specs=[
                pl.BlockSpec((rows, own + LANES), lambda g, need: (0, g)),
                sum_block((8, LANES)),
            ]
            + [pl.BlockSpec((2, rows, LANES), lambda g, need: (0, 0, g))] * shards,
            scratch_shapes=[
                pltpu.VMEM((per_kv, rows, LANES), jnp.float32),
                pltpu.VMEM((block, LANES), jnp.float32),
                pltpu.VMEM((block, LANES), jnp.float32),
                pltpu.VMEM((per_kv, rows, 2 * LANES), jnp.bfloat16),
                pltpu.VMEM((per_kv, rows, 2 * LANES), jnp.bfloat16),
            ],
        ),
        out_shape=[
            jax.ShapeDtypeStruct((rows, groups * (own + LANES)), jnp.bfloat16),
            jax.ShapeDtypeStruct((8, LANES), jnp.float32),
        ]
        + [jax.ShapeDtypeStruct((2, rows, groups * LANES), jnp.bfloat16)] * shards,
        compiler_params=params(),
        cost_estimate=cost(
            14 * rows * rows * shards * wide,
            20 * rows * wide + 4 * shards * rows * wide,
            0.21,
        ),
        name="attend_backward",
    )(
        need,
        out_in,
        w_out,
        query_low,
        query_mask,
        gates,
        key_mask,
        logs,
        attended,
        query_raw,
        cos_rows,
        sin_rows,
        gain,
        *blocks,
        *blocks,
    )


def key_back_kernel(groups, raw_ref, cos_ref, sin_ref, gain_ref, grads_ref, out_ref, gain_grad_ref):
    gain_total = jnp.zeros((1, LANES), jnp.float32)
    for k in range(groups):
        columns = slice(k * LANES, (k + 1) * LANES)
        grads = rope_back(grads_ref[0, :, columns].astype(jnp.float32), cos_ref[...], sin_ref[...])
        gain_part, key_grad = unit_back(raw_ref[:, columns], gain_ref[...], grads)
        gain_total += gain_part
        out_ref[:, 2 * k * LANES : (2 * k + 1) * LANES] = key_grad.astype(jnp.bfloat16)
        out_ref[:, (2 * k + 1) * LANES : (2 * k + 2) * LANES] = grads_ref[1, :, columns]
    gain_grad_ref[...] = jnp.broadcast_to(gain_total, gain_grad_ref.shape)


def key_back(index, key_raw, cos_rows, sin_rows, gain, key_grad):
    _, rows, wide = key_grad.shape
    table_spec = pl.BlockSpec((rows, LANES), lambda m: (index, 0))
    return pl.pallas_call(
        functools.partial(key_back_kernel, wide // LANES),
        grid=(1,),
        in_specs=[
            pl.BlockSpec((rows, wide), lambda m: (index, 0)),
            table_spec,
            table_spec,
            sum_block((1, LANES)),
            sum_block(key_grad.shape),
        ],
        out_specs=[sum_block((rows, 2 * wide)), sum_block((8, LANES))],
        out_shape=[
            jax.ShapeDtypeStruct((rows, 2 * wide), jnp.bfloat16),
            jax.ShapeDtypeStruct((8, LANES), jnp.float32),
        ],
        compiler_params=params(),
        cost_estimate=cost(30 * rows * wide, 12 * rows * wide),
        name="key_back",
    )(key_raw, cos_rows, sin_rows, gain, key_grad)


def sum_kernel(count, transposed, *refs):
    lefts, rights, out_ref = refs[:count], refs[count : 2 * count], refs[2 * count]
    dot = dot_nt if transposed else dot_nn
    total = dot(lefts[0][...], rights[0][...])
    for left, right in zip(lefts[1:], rights[1:]):
        total += dot(left[...], right[...])
    out_ref[...] = total.astype(jnp.bfloat16)


def sum_of_products(rows, lefts, rights, transposed):
    def left_spec(place):
        _, depth, row_block, column_block = place
        return pl.BlockSpec(
            (rows, depth), lambda n: (row_block, column_block), pipeline_mode=pl.Buffered(1)
        )

    depth_total = sum(place[1] for place in lefts)
    if transposed:
        columns = rights[0].shape[0]
        block = min(512, columns)
        right_specs = [pl.BlockSpec((block, right.shape[1]), lambda n: (n, 0)) for right in rights]
    else:
        shards, _, part = rights[0].shape
        columns = shards * part
        block = min(256, part)
        per = part // block
        right_specs = [
            pl.BlockSpec((None, right.shape[1], block), lambda n: (n // per, 0, n % per))
            for right in rights
        ]
    return pl.pallas_call(
        functools.partial(sum_kernel, len(lefts), transposed),
        grid=(columns // block,),
        in_specs=[left_spec(place) for place in lefts] + right_specs,
        out_specs=pl.BlockSpec((rows, block), lambda n: (0, n)),
        out_shape=jax.ShapeDtypeStruct((rows, columns), jnp.bfloat16),
        compiler_params=params(),
        cost_estimate=cost(
            2 * rows * depth_total * columns,
            2 * depth_total * (rows + columns) + 2 * rows * columns,
        ),
        name="sum_of_products",
    )(*[place[0] for place in lefts], *rights)


def gradient_kernel(counts, sizes, arrivals, *refs):
    lefts, at = [], 0
    for count in counts:
        lefts.append(refs[at : at + count])
        at += count
    outs = refs[len(refs) - len(arrivals) :]
    for arrived_count, out_ref in zip(arrivals, outs):
        totals = []
        for term in lefts:
            rights = refs[at : at + len(term)]
            at += len(term)
            total = dot_tn(term[0][...], rights[0][...])
            for left, right in zip(term[1:], rights[1:]):
                total += dot_tn(left[...], right[...])
            totals.append(total)
        arrived = refs[at : at + arrived_count]
        at += arrived_count
        column = 0
        for total, size in zip(totals, sizes):
            span = slice(column, column + size)
            for item in arrived:
                total += item[:, span].astype(jnp.float32)
            out_ref[:, span] = total.astype(jnp.bfloat16)
            column += size


def weight_gradients(rows, lefts, sizes, parts):
    def right_spec(size, row_block, column_block):
        return pl.BlockSpec(
            (rows, size), lambda m: (row_block, column_block), pipeline_mode=pl.Buffered(1)
        )

    def left_spec(row_block):
        return pl.BlockSpec((rows, block), lambda m: (row_block, m))

    width = lefts[0][0][0].shape[1]
    block = min(512, width)
    total = sum(sizes)
    out_spec = pl.BlockSpec((block, total), lambda m: (m, 0))
    specs = [left_spec(place[1]) for term in lefts for place in term]
    operands = [place[0] for term in lefts for place in term]
    for rights, arrived in parts:
        for size, term in zip(sizes, rights):
            specs += [right_spec(size, place[1], place[2]) for place in term]
            operands += [place[0] for place in term]
        specs += [out_spec] * len(arrived)
        operands += list(arrived)
    depth = rows * max(len(term) for term in lefts)
    return pl.pallas_call(
        functools.partial(
            gradient_kernel,
            [len(term) for term in lefts],
            sizes,
            [len(arrived) for _, arrived in parts],
        ),
        grid=(width // block,),
        in_specs=specs,
        out_specs=[out_spec] * len(parts),
        out_shape=[jax.ShapeDtypeStruct((width, total), jnp.bfloat16)] * len(parts),
        compiler_params=params(),
        cost_estimate=cost(
            2 * len(parts) * depth * width * total, 2 * depth * width + 4 * len(parts) * width * total
        ),
        name="weight_gradients",
    )(*operands)


def split_dot_nt(left, rights):
    part = rights.shape[2]
    total = dot_nt(left[:, :part], rights[0])
    for index in range(1, rights.shape[0]):
        total += dot_nt(left[:, index * part : (index + 1) * part], rights[index])
    return total


def mlp_kernel(batches, count, down_in_ref, *refs):
    inputs = refs[:batches]
    pair_ws = refs[batches : batches + count]
    down_ws = refs[batches + count : batches + 2 * count]
    hiddens = refs[batches + 2 * count : batches + 3 * count]
    pair_ins = refs[batches + 3 * count :]
    block = hiddens[0].shape[1]
    for index in range(batches):

        @pl.when(pl.program_id(0) == index)
        def _(index=index):
            for k in range(count):
                gate_pre = dot_nn(inputs[index][...], pair_ws[k][:, :block])
                up_pre = dot_nn(inputs[index][...], pair_ws[k][:, block:])
                grad_hidden = split_dot_nt(down_in_ref[...], down_ws[k])
                sigmoid_gate = jax.nn.sigmoid(gate_pre)
                silu_gate = gate_pre * sigmoid_gate
                hiddens[k][...] = (silu_gate * up_pre).astype(jnp.bfloat16)
                pair_ins[k][:, block:] = (grad_hidden * silu_gate).astype(jnp.bfloat16)
                pair_ins[k][:, :block] = (
                    grad_hidden * up_pre * sigmoid_gate * (1.0 + gate_pre * (1.0 - sigmoid_gate))
                ).astype(jnp.bfloat16)


def mlp_units(inputs, down_in, pair_ws, down_ws):
    all_rows, width = down_in.shape
    batches, count = len(inputs), len(pair_ws)
    rows, units = all_rows // batches, pair_ws[0].shape[1] // 2
    return pl.pallas_call(
        functools.partial(mlp_kernel, batches, count),
        grid=(batches,),
        in_specs=[pl.BlockSpec((rows, width), lambda m: (m, 0))]
        + [whole_block(item.shape) for item in list(inputs) + pair_ws + down_ws],
        out_specs=[pl.BlockSpec((rows, units), lambda m: (m, 0))] * count
        + [pl.BlockSpec((rows, 2 * units), lambda m: (m, 0))] * count,
        out_shape=[jax.ShapeDtypeStruct((all_rows, units), jnp.bfloat16)] * count
        + [jax.ShapeDtypeStruct((all_rows, 2 * units), jnp.bfloat16)] * count,
        compiler_params=params(),
        cost_estimate=cost(
            6 * count * all_rows * width * units, 4 * all_rows * width + 6 * count * width * units
        ),
        name="mlp_units",
    )(down_in, *inputs, *pair_ws, *down_ws)


def add_norm_kernel(stream_ref, low_ref, other_ref, gain_ref, middle_ref, normed_ref):
    middle = (
        stream_ref[...].astype(jnp.float32)
        + (low_ref[...].astype(jnp.float32) + other_ref[...].astype(jnp.float32))
    )
    unit, _ = unit_of(middle)
    middle_ref[...] = middle
    normed_ref[...] = (unit * gain_ref[...]).astype(jnp.bfloat16)


def add_norm(index, stream, low_part, other_part, gain):
    rows, width = low_part.shape
    block = min(128, rows)
    first = index * (rows // block)
    spec = pl.BlockSpec((block, width), lambda m: (m, 0))
    return pl.pallas_call(
        add_norm_kernel,
        grid=(rows // block,),
        in_specs=[
            pl.BlockSpec((block, width), lambda m: (first + m, 0)),
            spec,
            spec,
            whole_block((1, width)),
        ],
        out_specs=[spec, spec],
        out_shape=[
            jax.ShapeDtypeStruct((rows, width), jnp.float32),
            jax.ShapeDtypeStruct((rows, width), jnp.bfloat16),
        ],
        compiler_params=params(),
        cost_estimate=cost(8 * rows * width, 12 * rows * width),
        name="add_norm",
    )(stream, low_part, other_part, gain)


def norm_back_kernel(values_ref, low_ref, other_ref, gain_ref, up_ref, *outs):
    grads = low_ref[...].astype(jnp.float32) + other_ref[...].astype(jnp.float32)
    gain_part, back = unit_back(values_ref[...].astype(jnp.float32), gain_ref[...], grads)
    total = up_ref[...].astype(jnp.float32) + back
    outs[0][...] = total.astype(jnp.bfloat16)
    for out_ref in outs[2:]:
        out_ref[...] = total

    @pl.when(pl.program_id(0) == 0)
    def _():
        outs[1][...] = jnp.zeros_like(outs[1])

    outs[1][0:1] += gain_part


def norm_back(values, values_at, low_part, other_part, gain, upstream, up_at, keep):
    rows, width = low_part.shape
    block = min(128, rows)
    steps = rows // block
    spec = pl.BlockSpec((block, width), lambda m: (m, 0))
    return pl.pallas_call(
        norm_back_kernel,
        grid=(steps,),
        in_specs=[
            pl.BlockSpec((block, width), lambda m: (values_at * steps + m, 0)),
            spec,
            spec,
            whole_block((1, width)),
            pl.BlockSpec((block, width), lambda m: (up_at * steps + m, 0)),
        ],
        out_specs=[spec, sum_block((8, width))] + [spec] * keep,
        out_shape=[
            jax.ShapeDtypeStruct((rows, width), jnp.bfloat16),
            jax.ShapeDtypeStruct((8, width), jnp.float32),
        ]
        + [jax.ShapeDtypeStruct((rows, width), jnp.float32)] * keep,
        compiler_params=params(),
        cost_estimate=cost(16 * rows * width, 16 * rows * width),
        name="norm_back",
    )(values, low_part, other_part, gain, upstream)


def order_kernel(per_quarter, turned, own_ref, *refs):
    pieces, out_ref = refs[:-1], refs[-1]
    step = pl.program_id(0)
    places = len(pieces) // per_quarter
    for index, piece in enumerate(pieces):

        @pl.when(step == index % places * per_quarter + index // places)
        def _(piece=piece):
            value = piece[...].astype(jnp.float32)
            out_ref[...] = value.T if turned else value


def in_order(chunks, block, column, turned=False):
    rows = chunks[0][0].shape[0]
    places, per_quarter = len(chunks[0]), len(chunks)
    own = lax.axis_index("replica").astype(jnp.int32).reshape(1)

    def out_of(step, own):
        place = step // per_quarter
        flip = jnp.where(place == 1, 2, jnp.where(place == 2, 1, place))
        at = jnp.bitwise_xor(own[0], flip) * per_quarter + step % per_quarter
        return (at, 0) if turned else (0, at)

    total = places * per_quarter * block
    pieces = [piece for chunk in chunks for piece in chunk]
    return pl.pallas_call(
        functools.partial(order_kernel, per_quarter, turned),
        grid_spec=pltpu.PrefetchScalarGridSpec(
            num_scalar_prefetch=1,
            grid=(places * per_quarter,),
            in_specs=[pl.BlockSpec((rows, block), lambda step, own: (0, column))] * len(pieces),
            out_specs=pl.BlockSpec((block, rows) if turned else (rows, block), out_of),
        ),
        out_shape=jax.ShapeDtypeStruct((total, rows) if turned else (rows, total), jnp.float32),
        compiler_params=params(),
        cost_estimate=cost(rows * total, 6 * rows * total),
        name="in_order",
    )(own, *pieces)


class Fold:
    def __init__(self, make_parts, far, far_end, direct):
        self.make_parts, self.far, self.far_end, self.direct = make_parts, far, far_end, direct

    def steps32(self):
        third, second = self.make_parts((3,), (2,))
        self.from_third, self.from_near = across(third, 1), across(second, 1)

    def step1(self):
        (part,) = self.make_parts((1, self.from_third))
        self.from_far = self.far.run(to_far, part)

    def step0(self):
        (part,) = self.make_parts((0, self.from_near, self.from_far))
        self.shard = scatter_rows(part)

    def steps10(self):
        first, own = self.make_parts((1, self.from_third), (0, self.from_near))
        self.far_shard, self.shard = scatter_rows(first), scatter_rows(own)

    def end(self):
        if self.direct:
            arrived = self.far_end.run(to_far, self.far_shard)
            total = self.shard.astype(jnp.float32) + arrived.astype(jnp.float32)
            self.shard = total.astype(jnp.bfloat16)
        return spread(self.shard, self.far_end)


class RelayBack:
    def __init__(self, parts):
        self.parts, self.steps = parts, []

    def advance(self, *earlier):
        at = len(self.parts) - 1 - len(self.steps)
        if at > 0:
            carry = self.steps[-1] if self.steps else self.parts[at]
            carry = after(carry, *earlier) if earlier else carry
            pairs = [(index, index - 1) for index in range(1, len(self.parts))]
            arrived = lax.ppermute(carry, "fsdp", pairs).astype(jnp.float32)
            total = self.parts[at - 1].astype(jnp.float32) + arrived
            self.steps.append(total.astype(jnp.bfloat16))
        return self.steps[-1]

    def finish(self):
        while len(self.steps) < len(self.parts) - 1:
            self.advance()
        return self.steps[-1]


def local(
    tokens,
    cotangent,
    lengths,
    parents,
    attn_gain,
    qk_gain,
    w_query,
    key_weight_matrix,
    value_weight_matrix,
    w_headgate,
    w_out,
    mlp_gain,
    w_gate,
    w_up,
    w_down,
):
    batches, rows, width = tokens.shape
    shards = lax.axis_size("fsdp")
    shard = lax.axis_index("fsdp")
    query_gain, key_gain = qk_gain[0, 0:1], qk_gain[0, 1:2]
    low = jnp.bfloat16

    query_piece = own_quarter(w_query[0], 1)
    head_piece = own_quarter(w_headgate[0], 1)
    per_kv = query_piece.shape[1] // LANES
    own = per_kv * LANES
    pad = jnp.zeros((query_piece.shape[0], LANES - head_piece.shape[1]), low)
    gate_piece, up_piece = own_quarter(w_gate[0], 1), own_quarter(w_up[0], 1)
    down_piece = own_quarter(w_down[0], 0)
    unit_block = min(256, gate_piece.shape[1])
    unit_blocks = gate_piece.shape[1] // unit_block
    def unit_span(value, block, axis):
        return lax.slice_in_dim(value, block * unit_block, (block + 1) * unit_block, axis=axis)

    far_in, far_out, far_end = Line(2), Line(2), Line(2)
    key_value_w = spread(
        gather_shards(
            jnp.concatenate(
                [own_quarter(key_weight_matrix[0], 1), own_quarter(value_weight_matrix[0], 1)],
                axis=1,
            ),
        ),
        far_in,
    )
    query_part = gather_shards(jnp.concatenate([query_piece, head_piece, pad], axis=1))
    out_part = gather_stacked(own_quarter(w_out[0], 0))
    groups = len(key_value_w)
    chunk_of = range(unit_blocks)

    tables, positions = [], []
    for index in range(batches):
        need, query_mask, key_mask, position = tree_need(
            lengths[index, 0], parents[index, 0], shard, rows, shards
        )
        tables.append((need, query_mask, key_mask))
        positions.append(position)
    half = LANES // 2
    frequency = THETA ** (-(jnp.arange(half, dtype=jnp.float32) * 2.0 / LANES))
    angle = jnp.concatenate(positions).astype(jnp.float32)[:, None] * frequency[None, :]
    cosine, sine = jnp.cos(angle), jnp.sin(angle)
    cos_rows = jnp.concatenate([cosine, cosine], axis=1)
    sin_rows = jnp.concatenate([-sine, sine], axis=1)

    core = Line(1)
    stream = tokens.reshape(batches * rows, width)
    down_in = cotangent.reshape(batches * rows, width)
    normed_low = (unit_of(stream.astype(jnp.float32))[0] * attn_gain).astype(low)
    key_value, key_raw = core.run(
        key_value_heads, normed_low, key_value_w, cos_rows, sin_rows, key_gain
    )
    query_w = spread(after(query_part, key_value), far_in)
    relays = [Relay(key_value[index * rows : (index + 1) * rows], shards) for index in range(batches)]
    for index, relay in enumerate(relays):
        if index > 0:
            relay.hold(relays[index - 1].latest)
        relay.advance()
    core.hold(*[relay.latest for relay in relays[1:]])
    query_low, query_raw, gates = core.run(
        query_heads, normed_low, query_w, cos_rows, sin_rows, query_gain, per_kv
    )
    out_w = jnp.stack(spread(after(out_part, key_value), far_in))
    for _ in range(2, shards):
        relays[0].advance()
    for index in range(1, batches):
        for step in range(2, shards - 1):
            relays[index].hold(query_low)
            relays[index].advance()
    blocks = [relay.blocks for relay in relays]
    tie = blocks[0][-1]
    pair_w, down_w, pair_parts = [], [], []
    for chunk in chunk_of:
        piece = jnp.concatenate(
            [unit_span(gate_piece, chunk, 1), unit_span(up_piece, chunk, 1)], axis=1
        )
        pair_parts.append(gather_shards(after(piece, tie, query_low, out_part)))
    down_part = gather_stacked(after(down_piece, tie, query_low, out_part))
    pair_parts[0] = after(pair_parts[0], blocks[0][-1])
    pair_w.append(spread(pair_parts[0], far_in))
    mixed, attended, logs, middle, mlp_low, parts = [], [], [], [], [], []
    for index in range(batches):
        tree_mixed, tree_out, tree_log = core.run(
            lambda query: attend_forward(
                index, batches, tables[index], query, gates, blocks[index], per_kv
            ),
            query_low,
        )
        for relay in relays:
            relay.hold(tree_mixed)
            relay.advance()
        mixed.append(tree_mixed)
        attended.append(tree_out)
        logs.append(tree_log)
        part = core.run(
            lambda left: sum_of_products(
                rows,
                [(left, own, 0, k) for k in range(groups)],
                [out_w[k] for k in range(groups)],
                False,
            ),
            tree_mixed,
        )
        parts.append((part, tensor_other(part)))
    down_part = after(down_part, part)
    for chunk in chunk_of:
        down_w.append(spread(unit_span(down_part, chunk, 1), far_in))
    for item in pair_parts[1:]:
        pair_w.append(spread(after(item, part), far_in))
    for index in range(batches):
        core.hold(pair_w[0][1], down_w[min(index, unit_blocks - 1)][1])
        tree_middle, tree_normed = core.run(
            lambda part: add_norm(index, stream, part, parts[index][1], mlp_gain), parts[index][0]
        )
        middle.append(tree_middle)
        mlp_low.append(tree_normed)

    hidden = [[None] * groups for _ in chunk_of]
    pair_in = [[None] * groups for _ in chunk_of]

    def do_units(chunk, members):
        made = core.run(
            lambda upstream: mlp_units(
                mlp_low,
                upstream,
                [pair_w[chunk][k] for k in members],
                [down_w[chunk][k] for k in members],
            ),
            down_in,
        )
        for place, k in enumerate(members):
            hidden[chunk][k], pair_in[chunk][k] = made[place], made[len(members) + place]

    def fold(lefts, sizes, rights_of, direct=False):
        def make_parts(*wanted):
            def work(first):
                own_lefts = [[(first,) + lefts[0][0][1:]] + lefts[0][1:]] + lefts[1:]
                parts = [(rights_of(k), arrived) for k, *arrived in wanted]
                return weight_gradients(rows, own_lefts, sizes, parts)

            return core.run(work, lefts[0][0][0])

        return Fold(make_parts, far_out, far_end, direct)

    def both(value, column=0):
        return [(value, index, column) for index in range(batches)]

    def apart(values, column=0):
        return [(value, 0, column) for value in values]

    unit_folds = [
        fold(
            [apart(mlp_low), both(down_in)],
            [2 * unit_block, unit_block],
            lambda k, c=c: [both(pair_in[c][k]), both(hidden[c][k])],
            direct=c == 0,
        )
        for c in chunk_of
    ]

    middle_parts = []

    def do_middle_part(index):
        part = core.run(
            lambda left: sum_of_products(
                rows,
                [
                    (left if (c, k) == (0, 0) else pair_in[c][k], 2 * unit_block, index, 0)
                    for c in chunk_of
                    for k in range(groups)
                ],
                [pair_w[c][k] for c in chunk_of for k in range(groups)],
                True,
            ),
            pair_in[0][0],
        )
        middle_parts.append((part, tensor_other(part)))

    mlp_gain_grad, grad_middle, out_in = [], [], []
    query_in, query_gain_grad, relays_back = [], [], []

    def do_norm_back(index):
        low_out, gain_part, full = core.run(
            lambda part: norm_back(
                middle[index], 0, part, middle_parts[index][1], mlp_gain, down_in, index, 1
            ),
            middle_parts[index][0],
        )
        out_in.append(low_out)
        mlp_gain_grad.append(gain_part)
        grad_middle.append(full)

    def do_attention_back(index):
        tree_in, gain_part, *grads = core.run(
            lambda upstream: attend_backward(
                index,
                batches,
                tables[index],
                upstream,
                out_w,
                query_low,
                gates,
                logs[index],
                attended[index],
                query_raw,
                cos_rows,
                sin_rows,
                query_gain,
                blocks[index],
                per_kv,
            ),
            out_in[index],
        )
        query_in.append(tree_in)
        query_gain_grad.append(gain_part)
        relays_back.append(RelayBack(grads))
        relays_back[-1].advance()

    result_parts = []

    def do_result_part(index):
        part = core.run(
            lambda left: sum_of_products(
                rows,
                [
                    (left if (c, k) == (0, 0) else hidden[c][k], unit_block, index, 0)
                    for c in chunk_of
                    for k in range(groups)
                ],
                [down_w[c][k] for c in chunk_of for k in range(groups)],
                False,
            ),
            hidden[0][0],
        )
        result_parts.append((part, tensor_other(part)))

    final = unit_blocks - 1
    for chunk in chunk_of:
        if chunk > 0:
            core.hold(pair_w[chunk][1])
        do_units(chunk, (0, 2))
        if chunk > 0:
            previous = unit_folds[chunk - 1]
            previous.steps10() if previous.direct else previous.step1()
            core.hold(pair_parts[-1])
        else:
            core.hold(down_w[-1][1])
        do_units(chunk, (1, 3))
        unit_folds[chunk].steps32()
    do_middle_part(0)
    if unit_folds[final].direct:
        unit_folds[final].steps10()
    else:
        unit_folds[final].step1()
    for index in range(1, batches):
        do_middle_part(index)
    waiting = [item for item in unit_folds if not item.direct]
    do_norm_back(0)
    for item in waiting[:-1]:
        item.step0()
    do_attention_back(0)
    core.hold(*[item.from_far for item in waiting[-1:]])
    for index in range(1, batches):
        do_norm_back(index)
    do_result_part(0)
    core.hold(relays_back[0].steps[0])
    for item in waiting[-1:]:
        item.step0()
    unit_ends = [unit_folds[0].end()]
    for index in range(1, batches):
        do_result_part(index)
    core.hold(relays_back[0].advance(), result_parts[0][1])
    for index in range(1, batches):
        do_attention_back(index)
    query_block = own + LANES
    wide_fold = fold(
        [apart(out_in), both(normed_low)],
        [own, query_block],
        lambda k: [apart(mixed, k), apart(query_in, k)],
    )
    wide_fold.steps32()
    wide_fold.step1()
    for relay in relays_back[1:]:
        relay.advance(core.sent[-1])
    key_block = 2 * LANES
    key_in, key_gain_grad, stream_parts = [], [], []

    def do_key_back(index):
        tree_in, gain_part = core.run(
            lambda raw: key_back(
                index, raw, cos_rows, sin_rows, key_gain, relays_back[index].finish()
            ),
            key_raw,
        )
        key_in.append(tree_in)
        key_gain_grad.append(gain_part)

    def do_stream_part(index):
        part = core.run(
            lambda left: sum_of_products(
                rows,
                [(query_in[index], query_block, 0, k) for k in range(groups)]
                + [(left, key_block, 0, k) for k in range(groups)],
                query_w + key_value_w,
                True,
            ),
            key_in[index],
        )
        stream_parts.append((part, tensor_other(part)))

    attn_gain_grad, input_grad = [], []

    def do_stream_back(index):
        part, other = stream_parts[index]
        low_out, gain_part = core.run(
            lambda part: norm_back(
                stream, index, part, other, attn_gain, grad_middle[index], 0, 0
            ),
            part,
        )
        input_grad.append(low_out)
        attn_gain_grad.append(gain_part)

    do_key_back(0)
    unit_ends += [item.end() for item in unit_folds[1:]]
    for pieces in unit_ends:
        core.hold(pieces[1], pieces[3])
    do_stream_part(0)
    core.hold(*[part[1] for part in result_parts])

    def do_order(column):
        return core.run(
            lambda first: in_order(
                [[first] + unit_ends[0][1:]] + unit_ends[1:], unit_block, column, column == 2
            ),
            unit_ends[0][0],
        )

    gate_order = do_order(0)
    for index in range(1, batches):
        do_key_back(index)
    key_fold = fold([both(normed_low)], [key_block], lambda k: [apart(key_in, k)])
    key_fold.steps32()
    wide_fold.step0()
    for index in range(1, batches):
        do_stream_part(index)
    key_fold.step1()
    core.hold(stream_parts[0][1])
    up_order = do_order(1)
    do_stream_back(0)
    key_fold.step0()
    down_order = do_order(2)
    for index in range(1, batches):
        do_stream_back(index)
    results = [
        (
            middle[index]
            + (part.astype(jnp.float32) + other.astype(jnp.float32))
        ).astype(low)
        for index, (part, other) in enumerate(result_parts)
    ]
    wide_shards = wide_fold.end()
    key_shards = key_fold.end()
    query_sum, key_sum = [
        jnp.sum(jnp.stack(items), axis=0)[0] for items in (query_gain_grad, key_gain_grad)
    ]
    wide_sums = [
        jnp.sum(jnp.stack(items), axis=0)[0] for items in (attn_gain_grad, mlp_gain_grad)
    ]
    gain_sum = axis_sum(
        axis_sum(jnp.concatenate(wide_sums + [query_sum, key_sum]), "replica"), "fsdp"
    )
    head_sum = axis_sum(gain_sum[2 * width :], "tensor")

    def own_slice(value, axis):
        size = value.shape[axis] // shards
        return lax.dynamic_slice_in_dim(value, shard * size, size, axis)[None]

    gate_count = head_piece.shape[1]
    gate_grad = in_order([wide_shards], LANES, 2 * per_kv)
    gate_grad = gate_grad.reshape(gate_grad.shape[0], groups, LANES)[:, :, :gate_count]
    return (
        jnp.stack(results),
        jnp.stack(input_grad),
        own_slice(gain_sum[:width], 0),
        own_slice(head_sum.reshape(2, LANES), 1),
        in_order([wide_shards], own, 1)[None],
        in_order([key_shards], LANES, 0)[None],
        in_order([key_shards], LANES, 1)[None],
        gate_grad.reshape(1, gate_grad.shape[0], groups * gate_count),
        in_order([wide_shards], own, 0, turned=True)[None],
        own_slice(gain_sum[width : 2 * width], 0),
        gate_order[None],
        up_order[None],
        down_order[None],
    )


def solution(mesh):
    placed = (
        P(None, ("replica", "fsdp"), None),
        P(None, ("replica", "fsdp"), None),
        P(None, "replica", None),
        P(None, "replica", None),
        P(),
        P(),
        P(None, "fsdp", "tensor"),
        P(None, "fsdp", "tensor"),
        P(None, "fsdp", "tensor"),
        P(None, "fsdp", "tensor"),
        P(None, "tensor", "fsdp"),
        P(),
        P(None, "fsdp", "tensor"),
        P(None, "fsdp", "tensor"),
        P(None, "tensor", "fsdp"),
    )
    return jax.shard_map(
        local,
        mesh=mesh,
        in_specs=placed,
        out_specs=(
            P(None, ("replica", "fsdp"), None),
            P(None, ("replica", "fsdp"), None),
            P(None, "fsdp"),
            P(None, None, "fsdp"),
            P(None, "fsdp", "tensor"),
            P(None, "fsdp", "tensor"),
            P(None, "fsdp", "tensor"),
            P(None, "fsdp", "tensor"),
            P(None, "tensor", "fsdp"),
            P(None, "fsdp"),
            P(None, "fsdp", "tensor"),
            P(None, "fsdp", "tensor"),
            P(None, "tensor", "fsdp"),
        ),
        check_vma=False,
    )
```
